128 devices in a mesh: front: 16 (over z_hi, y, core), row: 4 (over x), col: 2 (over z_lo).
Axes of the slice: x: 4, y: 4, z: 4 (z_hi: 2, z_lo: 2; z = z_hi * 2 + z_lo), core: 2. Of those that a mesh axis runs over, the one named last changes fastest.
Arguments:
- own_rows: float32 [16, 1536, 4096], P('front', 'row', 'col'), may hold values from -1.5 to 1.5
- child_rows: float32 [32768, 4096], P(('front', 'row'), 'col'), may hold values from -3 to 3
- child_dest: int32 [32768, 1], P(('front', 'row')), may hold values from 0 to 15; in each aligned block of 512 rows (0 to 511, 512 to 1023, ...) at most 64 rows name the same one
- child_stair: int32 [32768], P(('front', 'row')), may hold values from 0 to 7
Outputs:
- r_factor: float32 [16, 1024, 4096], P('front', 'row', 'col')
The draws below stay inside these ranges and needn't reach their ends.
Inputs may be any that keep to these rules, and one draw needn't show every extreme that they name: `child_dest`: among the 512 rows of one device at most 64 name one parent, and in every draw some device has exactly 64 rows for some parent.
All inputs are finite; a program needn't handle non-finite values.
Results may differ from the reference program's by a relative error of at most 0.0003.
Values sent between devices are 32-bit elements; how exact they have to be, the bound alone decides.
No kernel may reach another device: no remote copies, remote signals or barrier semaphores. Data moves between devices by JAX's collectives and lax.ppermute only.
A program may use at most 128 MiB of HBM per device.

```python
import math
import jax
import jax.numpy as jnp
import numpy as np
from jax import lax

NC = 4096
PANEL_COLUMNS = 512
PANEL_COUNT = 2
SRC_DEV = 512
STAIR_BLK = 128
CAP = 64
OWN_ALL = 1536
CHILD_ROWS = 32768
N_FRONT = 16
N_ROW = 4


def place_ends(drawn, stream_key, least, high):
    longest = drawn.shape.index(max(drawn.shape))
    spots = []
    for shift in (0, 1):
        where = [jax.random.randint(jax.random.fold_in(stream_key, axis), (), 0, length) for axis, length in enumerate(drawn.shape)]
        where[longest] = (where[longest] + shift) % drawn.shape[longest]
        spots.append(tuple(where))
    return drawn.at[spots[0]].set(least).at[spots[1]].set(high)


def block_scale(key, dims, split, low, top_value):
    def one(dim, blocks):
        heights = jax.random.uniform(jax.random.fold_in(jax.random.fold_in(key, 6), dim), (blocks,), jnp.float32, low / len(split), top_value / len(split))
        return jnp.repeat(jnp.exp(heights), dims[dim] // blocks).reshape((-1,) + (1,) * (len(dims) - dim - 1))

    level = one(*split[0])
    for cut in split[1:]:
        level = level * one(*cut)
    return level


def deal_out(stream_key, own, number, rows, count, top, limit, lean):
    ranking = jax.random.permutation(stream_key, count)
    packed, ordinary = portions_of(count, rows * top, limit, lean, True), portions_of(count, rows * top, limit, lean, False)
    places = jnp.arange(count)

    def named(tallies, offset_by):
        used = int((tallies > 0).sum())
        fixed = max(1, used // 4)
        passed = fixed + (places - fixed + offset_by * (used - fixed)) % max(1, count - fixed)
        return jnp.zeros((count,), jnp.int32).at[ranking[jnp.where(places < fixed, places, passed)]].set(jnp.asarray(tallies, jnp.int32))

    tallies = jnp.where(number % 4 == 0, named(packed, number // 4), named(ordinary, number - number // 4 - 1))
    mixed = jax.random.permutation(jax.random.fold_in(own, 3), count)
    giver, receiver = mixed[0:count // 2 * 2:2], mixed[1:count // 2 * 2:2]
    margin = jnp.minimum(tallies[giver] - 1, limit - tallies[receiver]) // 2
    margin = jnp.where((giver == ranking[0]) | (receiver == ranking[0]) | (tallies[receiver] == 0), 0, jnp.maximum(margin, 0))
    passed = jax.random.randint(jax.random.fold_in(own, 4), (count // 2,), 0, 1 << 20) % (margin + 1)
    tallies = tallies.at[giver].add(-passed).at[receiver].add(passed)
    labels = jnp.searchsorted(jnp.cumsum(tallies), jnp.arange(rows * top), side="right").astype(jnp.int32)
    grid = labels.reshape(top, rows).T
    grid = grid[jax.random.permutation(jax.random.fold_in(own, 1), rows)]
    offset_by = jax.random.randint(jax.random.fold_in(own, 2), (rows, 1), 0, top)
    return jnp.take_along_axis(grid, (jnp.arange(top)[None, :] + offset_by) % top, axis=1)


def portions_of(number_of, total, reach, slope, full):
    weights = [(1 << 20) // math.isqrt(grade ** slope) + 1 for grade in range(1, number_of + 1)]
    largest = reach if full else min(reach, max(-(-total // number_of), total * weights[0] // sum(weights)))
    least = 1 if total - largest >= number_of - 1 else 0
    counts, rest = [largest] + [least] * (number_of - 1), total - largest - least * (number_of - 1)
    while rest > 0:
        free = [i for i in range(1, number_of) if counts[i] < largest] or [i for i in range(1, number_of) if counts[i] < reach]
        whole, remaining = sum([weights[i] for i in free]), rest
        for i in free:
            extra = min(reach - counts[i], max(1, remaining * weights[i] // whole), rest)
            counts[i] = counts[i] + extra
            rest = rest - extra
    return np.array(counts)


def bell_draw(own_key, extent, width, most, pieces=(), kind=jnp.bfloat16):
    result = jax.random.normal(own_key, extent, jnp.float32) * width
    if len(pieces) > 0:
        result = block_scale(own_key, extent, pieces, -0.22, 0.18) * result
    return jnp.clip(result, min=-most, max=most).astype(kind)


def setup_inputs(seed: int = 0) -> dict:
    keys = jax.random.split(jax.random.key(seed), 5)
    own_rows = bell_draw(keys[0], (N_FRONT, OWN_ALL, NC), 0.25, 1.5, ((0, 16), (1, 4), (2, 2)), jnp.float32)
    child_rows = bell_draw(keys[1], (CHILD_ROWS, NC), 0.5, 3.0, ((0, 64), (1, 2)), jnp.float32)
    child_dest_keys = jax.random.split(jax.random.fold_in(keys[2], 1), CHILD_ROWS // SRC_DEV)
    child_dest_turns = jax.random.permutation(jax.random.fold_in(keys[2], 3), CHILD_ROWS // SRC_DEV)
    child_dest = jax.vmap(lambda own, number: deal_out(jax.random.fold_in(keys[2], 2), own, number, SRC_DEV, N_FRONT, 1, CAP, 1))(child_dest_keys, child_dest_turns).reshape((CHILD_ROWS, 1))
    child_stair = place_ends(jax.random.randint(keys[3], (CHILD_ROWS,), 0, 8), jax.random.fold_in(keys[3], 1), 0, 7).astype(jnp.int32)
    return {"own_rows": own_rows, "child_rows": child_rows, "child_dest": child_dest, "child_stair": child_stair}


def reference(own_rows, child_rows, child_dest, child_stair):
    columns = jnp.arange(NC, dtype=jnp.int32)
    kept_mask = columns[None, :] >= (child_stair * STAIR_BLK)[:, None]
    masked_rows = jnp.where(kept_mask, child_rows, jnp.zeros_like(child_rows))
    targets = child_dest[:, 0]
    bound_rows = N_FRONT * N_ROW * CAP
    eliminated_panel = PANEL_COUNT * PANEL_COLUMNS

    def one_parent(parent):
        hits = targets == parent
        position = jnp.nonzero(hits, size=bound_rows, fill_value=0)[0].astype(jnp.int32)
        is_valid = jnp.arange(bound_rows, dtype=jnp.int32) < jnp.sum(hits.astype(jnp.int32))
        picked_rows = jnp.where(is_valid[:, None], masked_rows[position], jnp.zeros((bound_rows, NC), masked_rows.dtype))
        stacked_rows = jnp.concatenate([own_rows[parent], picked_rows], 0)
        gramian_block = jnp.dot(stacked_rows[:, :eliminated_panel].T, stacked_rows, precision=lax.Precision.HIGHEST, preferred_element_type=masked_rows.dtype)
        lower_cholesky_factor = jnp.linalg.cholesky(gramian_block[:, :eliminated_panel])
        return jax.scipy.linalg.solve_triangular(lower_cholesky_factor, gramian_block, lower=True)
    return lax.map(one_parent, jnp.arange(N_FRONT, dtype=jnp.int32))
```

```python
import jax
import jax.numpy as jnp
from jax import lax
from jax.experimental import pallas as pl
from jax.experimental.pallas import tpu as pltpu
from jax.sharding import PartitionSpec as P

ELIMINATED = 1024
STAIR_BLK = 128
BLK = 128
STEPS = ELIMINATED // BLK
LINES = 8


def lower_inverse(diag_block):
    lane = lax.broadcasted_iota(jnp.int32, (LINES, BLK), 1)
    sublane = lax.broadcasted_iota(jnp.int32, (LINES, BLK), 0)
    count = BLK // LINES
    strips = [diag_block[LINES * i : LINES * (i + 1), :] for i in range(count)]
    for b in range(count):
        first = LINES * b
        within = (lane >= first) & (lane < first + LINES)
        strip = strips[b]
        column = [
            jnp.broadcast_to(strip[:, first + t : first + t + 1], (LINES, BLK))
            for t in range(LINES)
        ]
        entry = [
            [jnp.broadcast_to(column[t][i : i + 1, :], (LINES, BLK)) for t in range(i + 1)]
            for i in range(LINES)
        ]
        scale = []
        for t in range(LINES):
            scale.append(lax.rsqrt(entry[t][t]))
            for i in range(t + 1, LINES):
                entry[i][t] = entry[i][t] * scale[t]
            for u in range(t + 1, LINES):
                for i in range(u, LINES):
                    entry[i][u] = entry[i][u] - entry[i][t] * entry[u][t]
        solved = []
        augmented = jnp.where(within, jnp.where(lane == sublane + first, 1.0, 0.0), strip)
        for t in range(LINES):
            line = jnp.broadcast_to(augmented[t : t + 1, :], (LINES, BLK))
            for s in range(t):
                line = line - entry[t][s] * solved[s]
            solved.append(line * scale[t])
        merged = solved[0]
        for t in range(1, LINES):
            merged = jnp.where(sublane == t, solved[t], merged)
        strips[b] = merged
        for i in range(b + 1, count):
            below = strips[i]
            rest = jnp.where(within, 0.0, below)
            factors = []
            for t in range(LINES):
                value = jnp.broadcast_to(below[:, first + t : first + t + 1], (LINES, BLK))
                for s in range(t):
                    value = value - entry[t][s] * factors[s]
                value = value * scale[t]
                factors.append(value)
                rest = rest - value * solved[t]
            strips[i] = rest
    row = lax.broadcasted_iota(jnp.int32, (BLK, BLK), 0)
    col = lax.broadcasted_iota(jnp.int32, (BLK, BLK), 1)
    return jnp.where(row >= col, jnp.concatenate(strips, axis=0), 0.0)


def exact_dot(a, b, dims):
    return lax.dot_general(
        a, b, (dims, ((), ())), precision=lax.Precision.HIGHEST, preferred_element_type=jnp.float32
    )


def factor_kernel(gram_ref, work_ref, diag_ref):
    work_ref[...] = gram_ref[...]
    row = lax.broadcasted_iota(jnp.int32, (BLK, BLK), 0)
    col = lax.broadcasted_iota(jnp.int32, (BLK, BLK), 1)

    def step(k, _):
        here = pl.ds(pl.multiple_of(k * BLK, BLK), BLK)
        block = work_ref[here, here]
        inverse = lower_inverse(block)
        diag_ref[here, :] = jnp.where(row <= col, exact_dot(inverse, block, ((1,), (0,))), 0.0)
        work_ref[here, :] = exact_dot(inverse, work_ref[here, :], ((1,), (0,)))
        work_ref[here, here] = inverse

        def update(i, _):
            there = pl.ds(pl.multiple_of(i * BLK, BLK), BLK)
            work_ref[there, here] = jnp.zeros((BLK, BLK), jnp.float32)
            work_ref[there, :] -= exact_dot(work_ref[here, there], work_ref[here, :], ((0,), (0,)))
            return 0

        lax.fori_loop(k + 1, STEPS, update, 0)
        return 0

    lax.fori_loop(0, STEPS, step, 0)


def factor(gram):
    return pl.pallas_call(
        factor_kernel,
        out_shape=(
            jax.ShapeDtypeStruct((ELIMINATED, ELIMINATED), jnp.float32),
            jax.ShapeDtypeStruct((ELIMINATED, BLK), jnp.float32),
        ),
        in_specs=[pl.BlockSpec(memory_space=pltpu.VMEM)],
        out_specs=(pl.BlockSpec(memory_space=pltpu.VMEM), pl.BlockSpec(memory_space=pltpu.VMEM)),
        compiler_params=pltpu.CompilerParams(vmem_limit_bytes=48 * 1024 * 1024),
        cost_estimate=pl.CostEstimate(flops=10**10, bytes_accessed=9 * 2**20, transcendentals=1024),
    )(gram)


def cross(a, b):
    return lax.dot_general(
        a,
        b,
        (((0,), (0,)), ((), ())),
        precision=lax.Precision.HIGH,
        preferred_element_type=jnp.float32,
    )


def body(own_rows, child_rows, child_dest, child_stair):
    n_front = lax.axis_size("front")
    row_count = lax.axis_size("row")
    source_rows, half_cols = child_rows.shape
    capacity = max(2, 2 * source_rows // n_front)
    col_index = lax.axis_index("col")
    row_index = lax.axis_index("row")
    quarter = ELIMINATED // row_count
    global_cols = col_index * half_cols + lax.broadcasted_iota(
        jnp.int32, (source_rows, half_cols), 1
    )
    masked_rows = jnp.where(global_cols >= (child_stair * STAIR_BLK)[:, None], child_rows, 0.0)
    targets = child_dest[:, 0]
    order = jnp.arange(source_rows, dtype=jnp.int32)
    earlier = (targets[:, None] == targets[None, :]) & (order[None, :] < order[:, None])
    slot = jnp.sum(earlier.astype(jnp.int32), axis=1)
    position = targets * capacity + slot
    send = jnp.zeros((n_front * capacity, half_cols), jnp.float32).at[position].set(masked_rows)

    own = own_rows[0]
    own_a, own_b = own[:, :ELIMINATED], own[:, ELIMINATED:]
    passed = lax.ppermute(own_a, "col", [(0, 1)])
    own_panel = jnp.where(col_index == 0, own_a, passed)

    doubled = jnp.broadcast_to(
        send[:, :ELIMINATED].reshape(n_front, 1, capacity, ELIMINATED),
        (n_front, 2, capacity, ELIMINATED),
    ).reshape(2 * n_front * capacity, ELIMINATED)
    arrived = lax.all_to_all(doubled, ("front", "col"), split_axis=0, concat_axis=0, tiled=True)
    arrived = arrived.reshape(n_front, 2, capacity, ELIMINATED)
    child_panel = arrived[:, 0].reshape(n_front * capacity, ELIMINATED)
    child_a = arrived[:, 1].reshape(n_front * capacity, ELIMINATED)
    child_b = lax.all_to_all(send[:, ELIMINATED:], "front", split_axis=0, concat_axis=0, tiled=True)

    gram = lax.psum(cross(own_panel, own_panel) + cross(child_panel, child_panel), "row")
    work, diag = factor(gram)
    block_row = lax.broadcasted_iota(jnp.int32, (ELIMINATED, ELIMINATED), 0) // BLK
    block_col = lax.broadcasted_iota(jnp.int32, (ELIMINATED, ELIMINATED), 1) // BLK
    inverse = jnp.where(block_row >= block_col, work, 0.0)
    leading = jnp.where(
        block_row < block_col, work, jnp.where(block_row == block_col, jnp.tile(diag, (1, STEPS)), 0.0)
    )
    leading = lax.dynamic_slice_in_dim(leading, row_index * quarter, quarter, 0)

    def finish(own_part, child_part):
        sums = lax.psum_scatter(
            cross(own_part, own_panel) + cross(child_part, child_panel),
            "row",
            scatter_dimension=0,
            tiled=True,
        )
        rows = exact_dot(inverse, sums, ((1,), (1,)))
        return lax.all_to_all(rows, "row", split_axis=0, concat_axis=1, tiled=True)

    first = jnp.where(col_index == 0, leading, finish(own_a, child_a))
    second = finish(own_b, child_b)
    return jnp.concatenate([first, second], 1)[None]


def solution(mesh):
    placed = (
        P("front", "row", "col"),
        P(("front", "row"), "col"),
        P(("front", "row"), None),
        P(("front", "row")),
    )
    return jax.shard_map(
        body, mesh=mesh, in_specs=placed, out_specs=P("front", "row", "col"), check_vma=False
    )
```

```python
import jax
import jax.numpy as jnp
from jax import lax
from jax.experimental import pallas as pl
from jax.experimental.pallas import tpu as pltpu
from jax.sharding import PartitionSpec as P

ELIMINATED = 1024
STAIR_BLK = 128
BLK = 128
STEPS = ELIMINATED // BLK
LINES = 8
VMEM_BYTES = 60 * 2**20
LIGHT = pl.CostEstimate(flops=1, bytes_accessed=1, transcendentals=0)


def lower_inverse(diag_block):
    lane = lax.broadcasted_iota(jnp.int32, (LINES, BLK), 1)
    sublane = lax.broadcasted_iota(jnp.int32, (LINES, BLK), 0)
    count = BLK // LINES
    strips = [diag_block[LINES * i : LINES * (i + 1), :] for i in range(count)]
    for b in range(count):
        first = LINES * b
        within = (lane >= first) & (lane < first + LINES)
        strip = strips[b]
        column = [
            jnp.broadcast_to(strip[:, first + t : first + t + 1], (LINES, BLK))
            for t in range(LINES)
        ]
        entry = [
            [jnp.broadcast_to(column[t][i : i + 1, :], (LINES, BLK)) for t in range(i + 1)]
            for i in range(LINES)
        ]
        scale = []
        for t in range(LINES):
            scale.append(lax.rsqrt(entry[t][t]))
            for i in range(t + 1, LINES):
                entry[i][t] = entry[i][t] * scale[t]
            for u in range(t + 1, LINES):
                for i in range(u, LINES):
                    entry[i][u] = entry[i][u] - entry[i][t] * entry[u][t]
        solved = []
        augmented = jnp.where(within, jnp.where(lane == sublane + first, 1.0, 0.0), strip)
        for t in range(LINES):
            line = jnp.broadcast_to(augmented[t : t + 1, :], (LINES, BLK))
            for s in range(t):
                line = line - entry[t][s] * solved[s]
            solved.append(line * scale[t])
        merged = solved[0]
        for t in range(1, LINES):
            merged = jnp.where(sublane == t, solved[t], merged)
        strips[b] = merged
        for i in range(b + 1, count):
            below = strips[i]
            rest = jnp.where(within, 0.0, below)
            factors = []
            for t in range(LINES):
                value = jnp.broadcast_to(below[:, first + t : first + t + 1], (LINES, BLK))
                for s in range(t):
                    value = value - entry[t][s] * factors[s]
                value = value * scale[t]
                factors.append(value)
                rest = rest - value * solved[t]
            strips[i] = rest
    row = lax.broadcasted_iota(jnp.int32, (BLK, BLK), 0)
    col = lax.broadcasted_iota(jnp.int32, (BLK, BLK), 1)
    return jnp.where(row >= col, jnp.concatenate(strips, axis=0), 0.0)


def exact_dot(a, b, dims):
    return lax.dot_general(
        a, b, (dims, ((), ())), precision=lax.Precision.HIGHEST, preferred_element_type=jnp.float32
    )


PAIRS = ((0, 3), (1, 2))
WIDE = 256
PACKED = ELIMINATED + WIDE


def offsets():
    found = []
    for pair, (long, short) in enumerate(PAIRS):
        found.append((long, pair, 0))
        found.append((short, pair, ELIMINATED - WIDE * long))
    return found


def halves(x):
    high = x.astype(jnp.bfloat16)
    return high, (x - high.astype(jnp.float32)).astype(jnp.bfloat16)


def place_kernel(first_ref, dest_ref, stair_ref, rows_ref, out_ref, select_ref):
    fronts, copies, capacity, width = out_ref.shape
    slots, sources = select_ref.shape
    chunk = pl.program_id(0)

    @pl.when(chunk == 0)
    def _():
        dest = dest_ref[...]
        named = lax.broadcasted_iota(jnp.int32, (fronts, sources), 0) == dest
        source = lax.broadcasted_iota(jnp.int32, (sources, sources), 0)
        later = lax.broadcasted_iota(jnp.int32, (sources, sources), 1)
        before = jnp.dot(
            named.astype(jnp.float32).astype(jnp.bfloat16),
            (source < later).astype(jnp.float32).astype(jnp.bfloat16),
            preferred_element_type=jnp.float32,
        )
        slot = jnp.sum(jnp.where(named, before, 0.0), axis=0, keepdims=True).astype(jnp.int32)
        position = dest * capacity + slot
        line = lax.broadcasted_iota(jnp.int32, (slots, sources), 0)
        select_ref[...] = (line == position).astype(jnp.float32).astype(jnp.bfloat16)

    cols = (
        first_ref[0, 0] + chunk * width + lax.broadcasted_iota(jnp.int32, (sources, width), 1)
    )
    high, low = halves(jnp.where(cols >= stair_ref[...] * STAIR_BLK, rows_ref[...], 0.0))
    select = select_ref[...]
    placed = jnp.dot(select, high, preferred_element_type=jnp.float32) + jnp.dot(
        select, low, preferred_element_type=jnp.float32
    )
    placed = placed.reshape(fronts, capacity, width)
    for copy in range(copies):
        out_ref[:, copy] = placed


def place(first_col, dest, stair, rows, start, copies, n_front, capacity):
    sources = rows.shape[0]
    skipped = start // WIDE
    return pl.pallas_call(
        place_kernel,
        grid=(ELIMINATED // WIDE,),
        out_shape=jax.ShapeDtypeStruct((n_front, copies, capacity, ELIMINATED), jnp.float32),
        in_specs=[
            pl.BlockSpec(memory_space=pltpu.SMEM),
            pl.BlockSpec((1, sources), lambda j: (0, 0)),
            pl.BlockSpec((sources, 1), lambda j: (0, 0)),
            pl.BlockSpec((sources, WIDE), lambda j: (0, skipped + j)),
        ],
        out_specs=pl.BlockSpec((n_front, copies, capacity, WIDE), lambda j: (0, 0, 0, j)),
        scratch_shapes=[pltpu.VMEM((n_front * capacity, sources), jnp.bfloat16)],
        compiler_params=pltpu.CompilerParams(vmem_limit_bytes=VMEM_BYTES),
        cost_estimate=LIGHT,
    )((first_col + start).reshape(1, 1), dest, stair, rows)


def gram_kernel(turn_ref, own_ref, child_ref, *rest):
    outs, (high_ref, low_ref, packed_ref) = rest[:-3], rest[-3:]
    own_count = own_ref.shape[0]
    child = child_ref[:, 0].reshape(-1, ELIMINATED)
    high_ref[:own_count], low_ref[:own_count] = halves(own_ref[...])
    high_ref[own_count:], low_ref[own_count:] = halves(child)
    dims = (((0,), (0,)), ((), ()))
    for block, pair, offset in offsets():
        start = WIDE * block
        left_high, left_low = high_ref[:, start : start + WIDE], low_ref[:, start : start + WIDE]
        right_high, right_low = high_ref[:, start:], low_ref[:, start:]
        total = lax.dot_general(left_high, right_high, dims, preferred_element_type=jnp.float32)
        total += lax.dot_general(left_high, right_low, dims, preferred_element_type=jnp.float32)
        total += lax.dot_general(left_low, right_high, dims, preferred_element_type=jnp.float32)
        for half in range(2):
            packed_ref[2 * pair + half, :, offset : offset + ELIMINATED - start] = total[
                BLK * half : BLK * (half + 1)
            ]
    count = len(outs)
    for s in range(count):
        outs[s][...] = packed_ref[lax.rem(turn_ref[0, 0] + s, count)]


def packed_gram(turn, own_panel, arrived):
    fronts, _, capacity, _ = arrived.shape
    rows = own_panel.shape[0] + fronts * capacity
    vmem = pl.BlockSpec(memory_space=pltpu.VMEM)
    return pl.pallas_call(
        gram_kernel,
        grid=(1,),
        out_shape=[jax.ShapeDtypeStruct((BLK, PACKED), jnp.float32)] * 4
        + [jax.ShapeDtypeStruct((rows, ELIMINATED), jnp.bfloat16)] * 2,
        in_specs=[
            pl.BlockSpec(memory_space=pltpu.SMEM),
            vmem,
            pl.BlockSpec((fronts, 1, capacity, ELIMINATED), lambda j: (0, 0, 0, 0)),
        ],
        out_specs=[vmem] * 6,
        scratch_shapes=[pltpu.VMEM((4, BLK, PACKED), jnp.float32)],
        compiler_params=pltpu.CompilerParams(vmem_limit_bytes=VMEM_BYTES),
        cost_estimate=LIGHT,
    )(turn, own_panel, arrived)


def cross_kernel(high_ref, low_ref, own_ref, child_ref, out_ref):
    child = child_ref[:, 0].reshape(-1, WIDE)
    high, low = halves(jnp.concatenate([own_ref[...], child], axis=0))
    dims = (((0,), (0,)), ((), ()))
    total = lax.dot_general(high, high_ref[...], dims, preferred_element_type=jnp.float32)
    total += lax.dot_general(high, low_ref[...], dims, preferred_element_type=jnp.float32)
    total += lax.dot_general(low, high_ref[...], dims, preferred_element_type=jnp.float32)
    out_ref[...] = total


def cross(high, low, own, start, child, part):
    fronts, _, capacity, _ = child.shape
    skipped = start // WIDE
    vmem = pl.BlockSpec(memory_space=pltpu.VMEM)
    return pl.pallas_call(
        cross_kernel,
        grid=(ELIMINATED // WIDE,),
        out_shape=jax.ShapeDtypeStruct((ELIMINATED, ELIMINATED), jnp.float32),
        in_specs=[
            vmem,
            vmem,
            pl.BlockSpec((own.shape[0], WIDE), lambda j: (0, skipped + j)),
            pl.BlockSpec((fronts, 1, capacity, WIDE), lambda j: (0, part, 0, j)),
        ],
        out_specs=pl.BlockSpec((WIDE, ELIMINATED), lambda j: (j, 0)),
        compiler_params=pltpu.CompilerParams(vmem_limit_bytes=VMEM_BYTES),
        cost_estimate=LIGHT,
    )(high, low, own, child)


def factor_kernel(turn_ref, *rest):
    pieces, (work_ref, leading_ref, diag_ref, packed_ref) = rest[:-4], rest[-4:]
    count = len(pieces)
    for s in range(count):
        packed_ref[lax.rem(turn_ref[0, 0] + count - s, count)] = pieces[s][...]
    work_ref[...] = jnp.zeros_like(work_ref)
    for block, pair, offset in offsets():
        start = WIDE * block
        for half in range(2):
            work_ref[start + BLK * half : start + BLK * (half + 1), start:] = packed_ref[
                2 * pair + half, :, offset : offset + ELIMINATED - start
            ]
    row = lax.broadcasted_iota(jnp.int32, (BLK, BLK), 0)
    col = lax.broadcasted_iota(jnp.int32, (BLK, BLK), 1)

    def step(k, _):
        here = pl.ds(pl.multiple_of(k * BLK, BLK), BLK)
        block = work_ref[here, here]
        inverse = lower_inverse(block)
        diag_ref[here, :] = jnp.where(row <= col, exact_dot(inverse, block, ((1,), (0,))), 0.0)
        work_ref[here, :] = exact_dot(inverse, work_ref[here, :], ((1,), (0,)))
        work_ref[here, here] = inverse

        def update(i, _):
            there = pl.ds(pl.multiple_of(i * BLK, BLK), BLK)
            work_ref[there, here] = jnp.zeros((BLK, BLK), jnp.float32)
            work_ref[there, :] -= exact_dot(work_ref[here, there], work_ref[here, :], ((0,), (0,)))
            return 0

        lax.fori_loop(k + 1, STEPS, update, 0)
        return 0

    lax.fori_loop(0, STEPS, step, 0)
    taken = leading_ref.shape[0] // BLK
    place_of = lax.broadcasted_iota(jnp.int32, (BLK, ELIMINATED), 1) // BLK
    for b in range(taken):
        block = turn_ref[0, 0] * taken + b
        here = pl.ds(pl.multiple_of(block * BLK, BLK), BLK)
        diag = jnp.concatenate([diag_ref[here, :]] * STEPS, axis=1)
        leading_ref[BLK * b : BLK * (b + 1), :] = jnp.where(
            place_of > block, work_ref[here, :], jnp.where(place_of == block, diag, 0.0)
        )
    for k in range(STEPS - 1):
        work_ref[BLK * k : BLK * (k + 1), BLK * (k + 1) :] = jnp.zeros(
            (BLK, ELIMINATED - BLK * (k + 1)), jnp.float32
        )


def factor(turn, pieces):
    vmem = pl.BlockSpec(memory_space=pltpu.VMEM)
    return pl.pallas_call(
        factor_kernel,
        out_shape=(
            jax.ShapeDtypeStruct((ELIMINATED, ELIMINATED), jnp.float32),
            jax.ShapeDtypeStruct((ELIMINATED // len(pieces), ELIMINATED), jnp.float32),
        ),
        in_specs=[pl.BlockSpec(memory_space=pltpu.SMEM)] + [vmem] * len(pieces),
        out_specs=(vmem, vmem),
        scratch_shapes=[
            pltpu.VMEM((ELIMINATED, BLK), jnp.float32),
            pltpu.VMEM((len(pieces), BLK, PACKED), jnp.float32),
        ],
        compiler_params=pltpu.CompilerParams(vmem_limit_bytes=VMEM_BYTES),
        cost_estimate=LIGHT,
    )(turn, *pieces)


def join_kernel(col_ref, leading_ref, first_ref, second_ref, out_ref):
    parts, _, width = first_ref.shape
    for j in range(parts):
        cols = slice(width * j, width * (j + 1))
        out_ref[0, :, cols] = jnp.where(col_ref[0, 0] == 0, leading_ref[:, cols], first_ref[j])
        out_ref[0, :, ELIMINATED + width * j : ELIMINATED + width * (j + 1)] = second_ref[j]


def join(col, leading, first, second):
    vmem = pl.BlockSpec(memory_space=pltpu.VMEM)
    rows = leading.shape[0]
    return pl.pallas_call(
        join_kernel,
        out_shape=jax.ShapeDtypeStruct((1, rows, 2 * ELIMINATED), jnp.float32),
        in_specs=[pl.BlockSpec(memory_space=pltpu.SMEM)] + [vmem] * 3,
        out_specs=vmem,
        compiler_params=pltpu.CompilerParams(vmem_limit_bytes=VMEM_BYTES),
    )(col, leading, first, second)


def shifted(x, shift, count):
    return lax.ppermute(x, "row", [(i, (i + shift) % count) for i in range(count)])


def body(own_rows, child_rows, child_dest, child_stair):
    n_front = lax.axis_size("front")
    row_count = lax.axis_size("row")
    source_rows, half_cols = child_rows.shape
    capacity = max(2, 2 * source_rows // n_front)
    col_index = lax.axis_index("col")
    row_index = lax.axis_index("row")
    quarter = ELIMINATED // row_count
    own = own_rows[0]
    own_a = own[:, :ELIMINATED]
    passed = lax.ppermute(own_a, "col", [(0, 1)])

    first_col = col_index * half_cols
    dest, stair = child_dest.reshape(1, source_rows), child_stair.reshape(source_rows, 1)
    doubled = place(first_col, dest, stair, child_rows, 0, 2, n_front, capacity)
    single = place(first_col, dest, stair, child_rows, ELIMINATED, 1, n_front, capacity)
    doubled, single, passed = lax.optimization_barrier((doubled, single, passed))
    arrived = lax.all_to_all(
        doubled.reshape(2 * n_front * capacity, ELIMINATED),
        ("front", "col"),
        split_axis=0,
        concat_axis=0,
        tiled=True,
    ).reshape(n_front, 2, capacity, ELIMINATED)
    child_b = lax.all_to_all(
        single.reshape(n_front * capacity, ELIMINATED), "front", split_axis=0, concat_axis=0, tiled=True
    ).reshape(n_front, 1, capacity, ELIMINATED)
    own_panel = jnp.where(col_index == 0, own_a, passed)

    turn = row_index.reshape(1, 1)
    *shares, high, low = packed_gram(turn, own_panel, arrived)
    products_a = cross(high, low, own, 0, arrived, 1)
    shares, products_a = lax.optimization_barrier((shares, products_a))
    sent = [shifted(shares[shift], shift, row_count) for shift in range(1, row_count)]
    piece = shares[0]
    for other in sent:
        piece = piece + other
    pieces = [piece] + [shifted(piece, shift, row_count) for shift in range(1, row_count)]

    def summed(products):
        return lax.psum_scatter(products, "row", scatter_dimension=0, tiled=True)

    def solved(sums):
        rows = lax.dot_general(
            inverse,
            sums,
            (((1,), (1,)), ((), ())),
            precision=lax.Precision.HIGH,
            preferred_element_type=jnp.float32,
        )
        return lax.all_to_all(
            rows.reshape(row_count, quarter, quarter), "row", split_axis=0, concat_axis=0, tiled=True
        )

    sums_a = summed(products_a)
    products_b = cross(high, low, own, ELIMINATED, child_b, 0)
    pieces, products_b = lax.optimization_barrier((pieces, products_b))
    sums_b = summed(products_b)
    inverse, leading = factor(turn, pieces)
    return join(col_index.reshape(1, 1), leading, solved(sums_a), solved(sums_b))


def solution(mesh):
    placed = (
        P("front", "row", "col"),
        P(("front", "row"), "col"),
        P(("front", "row"), None),
        P(("front", "row")),
    )
    return jax.shard_map(
        body, mesh=mesh, in_specs=placed, out_specs=P("front", "row", "col"), check_vma=False
    )
```

```python
import jax
import jax.numpy as jnp
from jax import lax
from jax.experimental import pallas as pl
from jax.experimental.pallas import tpu as pltpu
from jax.sharding import PartitionSpec as P

ELIMINATED = 1024
STAIR_BLK = 128
BLK = 128
STEPS = ELIMINATED // BLK
LINES = 8
VMEM_BYTES = 60 * 2**20
LIGHT = pl.CostEstimate(flops=1, bytes_accessed=1, transcendentals=0)


def lower_inverse(diag_block, beside):
    lane = lax.broadcasted_iota(jnp.int32, (LINES, BLK), 1)
    sublane = lax.broadcasted_iota(jnp.int32, (LINES, BLK), 0)
    count = BLK // LINES
    strips = [diag_block[LINES * i : LINES * (i + 1), :] for i in range(count)]
    for b in range(count):
        first = LINES * b
        within = (lane >= first) & (lane < first + LINES)
        strip = strips[b]
        column = [
            jnp.broadcast_to(strip[:, first + t : first + t + 1], (LINES, BLK))
            for t in range(LINES)
        ]
        entry = [
            [jnp.broadcast_to(column[t][i : i + 1, :], (LINES, BLK)) for t in range(i + 1)]
            for i in range(LINES)
        ]
        scale = []
        for t in range(LINES):
            scale.append(lax.rsqrt(entry[t][t]))
            for i in range(t + 1, LINES):
                entry[i][t] = entry[i][t] * scale[t]
            for u in range(t + 1, LINES):
                for i in range(u, LINES):
                    entry[i][u] = entry[i][u] - entry[i][t] * entry[u][t]
        solved = []
        augmented = jnp.where(within, jnp.where(lane == sublane + first, 1.0, 0.0), strip)
        for t in range(LINES):
            line = jnp.broadcast_to(augmented[t : t + 1, :], (LINES, BLK))
            for s in range(t):
                line = line - entry[t][s] * solved[s]
            solved.append(line * scale[t])
        merged = solved[0]
        for t in range(1, LINES):
            merged = jnp.where(sublane == t, solved[t], merged)
        strips[b] = merged
        beside(b, count)
        for i in range(b + 1, count):
            below = strips[i]
            rest = jnp.where(within, 0.0, below)
            factors = []
            for t in range(LINES):
                value = jnp.broadcast_to(below[:, first + t : first + t + 1], (LINES, BLK))
                for s in range(t):
                    value = value - entry[t][s] * factors[s]
                value = value * scale[t]
                factors.append(value)
                rest = rest - value * solved[t]
            strips[i] = rest
    row = lax.broadcasted_iota(jnp.int32, (BLK, BLK), 0)
    col = lax.broadcasted_iota(jnp.int32, (BLK, BLK), 1)
    return jnp.where(row >= col, jnp.concatenate(strips, axis=0), 0.0)


PAIRS = ((0, 3), (1, 2))
WIDE = 256
PACKED = ELIMINATED + WIDE


def offsets():
    found = []
    for pair, (long, short) in enumerate(PAIRS):
        found.append((long, pair, 0))
        found.append((short, pair, ELIMINATED - WIDE * long))
    return found


def halves(x):
    high = x.astype(jnp.bfloat16)
    return high, (x - high.astype(jnp.float32)).astype(jnp.bfloat16)


def place_kernel(first_ref, dest_ref, stair_ref, rows_ref, out_ref, select_ref):
    fronts, copies, capacity, width = out_ref.shape
    slots, sources = select_ref.shape
    chunk = pl.program_id(0)

    @pl.when(chunk == 0)
    def _():
        dest = dest_ref[...]
        named = lax.broadcasted_iota(jnp.int32, (fronts, sources), 0) == dest
        source = lax.broadcasted_iota(jnp.int32, (sources, sources), 0)
        later = lax.broadcasted_iota(jnp.int32, (sources, sources), 1)
        before = jnp.dot(
            named.astype(jnp.float32).astype(jnp.bfloat16),
            (source < later).astype(jnp.float32).astype(jnp.bfloat16),
            preferred_element_type=jnp.float32,
        )
        slot = jnp.sum(jnp.where(named, before, 0.0), axis=0, keepdims=True).astype(jnp.int32)
        position = dest * capacity + slot
        line = lax.broadcasted_iota(jnp.int32, (slots, sources), 0)
        select_ref[...] = (line == position).astype(jnp.float32).astype(jnp.bfloat16)

    cols = (
        first_ref[0, 0] + chunk * width + lax.broadcasted_iota(jnp.int32, (sources, width), 1)
    )
    high, low = halves(jnp.where(cols >= stair_ref[...] * STAIR_BLK, rows_ref[...], 0.0))
    select = select_ref[...]
    placed = jnp.dot(select, high, preferred_element_type=jnp.float32) + jnp.dot(
        select, low, preferred_element_type=jnp.float32
    )
    placed = placed.reshape(fronts, capacity, width)
    for copy in range(copies):
        out_ref[:, copy] = placed


def place(first_col, dest, stair, rows, start, copies, n_front, capacity):
    sources = rows.shape[0]
    skipped = start // WIDE
    return pl.pallas_call(
        place_kernel,
        grid=(ELIMINATED // WIDE,),
        out_shape=jax.ShapeDtypeStruct((n_front, copies, capacity, ELIMINATED), jnp.float32),
        in_specs=[
            pl.BlockSpec(memory_space=pltpu.SMEM),
            pl.BlockSpec((1, sources), lambda j: (0, 0)),
            pl.BlockSpec((sources, 1), lambda j: (0, 0)),
            pl.BlockSpec((sources, WIDE), lambda j: (0, skipped + j)),
        ],
        out_specs=pl.BlockSpec((n_front, copies, capacity, WIDE), lambda j: (0, 0, 0, j)),
        scratch_shapes=[pltpu.VMEM((n_front * capacity, sources), jnp.bfloat16)],
        compiler_params=pltpu.CompilerParams(vmem_limit_bytes=VMEM_BYTES),
        cost_estimate=LIGHT,
    )((first_col + start).reshape(1, 1), dest, stair, rows)


def gram_kernel(turn_ref, own_ref, child_ref, *outs):
    high_ref, low_ref, packed_ref = outs[5:]
    own_count = own_ref.shape[0]
    child = child_ref[:, 0].reshape(-1, ELIMINATED)
    high_ref[:own_count], low_ref[:own_count] = halves(own_ref[...])
    high_ref[own_count:], low_ref[own_count:] = halves(child)
    dims = (((0,), (0,)), ((), ()))
    for block, pair, offset in offsets():
        start = WIDE * block
        left_high, left_low = high_ref[:, start : start + WIDE], low_ref[:, start : start + WIDE]
        right_high, right_low = high_ref[:, start:], low_ref[:, start:]
        total = lax.dot_general(left_high, right_high, dims, preferred_element_type=jnp.float32)
        total += lax.dot_general(left_high, right_low, dims, preferred_element_type=jnp.float32)
        total += lax.dot_general(left_low, right_high, dims, preferred_element_type=jnp.float32)
        for half in range(2):
            packed_ref[2 * pair + half, :, offset : offset + ELIMINATED - start] = total[
                BLK * half : BLK * (half + 1)
            ]
    mine_ref, right_ref, left_ref, right_rest_ref, left_rest_ref, *_ = outs
    turn = turn_ref[0, 0]
    here, right, over, left = [lax.rem(turn + s, 4) for s in range(4)]
    middle = BLK // 2
    mine_ref[...] = packed_ref[here]
    right_ref[:middle], right_ref[middle:] = packed_ref[over, :middle], packed_ref[right, middle:]
    left_ref[:middle], left_ref[middle:] = packed_ref[over, middle:], packed_ref[left, :middle]
    right_rest_ref[...] = packed_ref[right, :middle]
    left_rest_ref[...] = packed_ref[left, middle:]


def packed_gram(turn, own_panel, arrived):
    fronts, _, capacity, _ = arrived.shape
    rows = own_panel.shape[0] + fronts * capacity
    vmem = pl.BlockSpec(memory_space=pltpu.VMEM)
    return pl.pallas_call(
        gram_kernel,
        grid=(1,),
        out_shape=[jax.ShapeDtypeStruct((BLK, PACKED), jnp.float32)] * 3
        + [jax.ShapeDtypeStruct((BLK // 2, PACKED), jnp.float32)] * 2
        + [jax.ShapeDtypeStruct((rows, ELIMINATED), jnp.bfloat16)] * 2,
        in_specs=[
            pl.BlockSpec(memory_space=pltpu.SMEM),
            vmem,
            pl.BlockSpec((fronts, 1, capacity, ELIMINATED), lambda j: (0, 0, 0, 0)),
        ],
        out_specs=[vmem] * 7,
        scratch_shapes=[pltpu.VMEM((4, BLK, PACKED), jnp.float32)],
        compiler_params=pltpu.CompilerParams(vmem_limit_bytes=VMEM_BYTES),
        cost_estimate=LIGHT,
    )(turn, own_panel, arrived)


def cross_kernel(high_ref, low_ref, own_ref, child_ref, out_ref):
    child = child_ref[:, 0].reshape(-1, WIDE)
    high, low = halves(jnp.concatenate([own_ref[...], child], axis=0))
    dims = (((0,), (0,)), ((), ()))
    total = lax.dot_general(high, high_ref[...], dims, preferred_element_type=jnp.float32)
    total += lax.dot_general(high, low_ref[...], dims, preferred_element_type=jnp.float32)
    total += lax.dot_general(low, high_ref[...], dims, preferred_element_type=jnp.float32)
    out_ref[...] = total


def cross(high, low, own, start, child, part):
    fronts, _, capacity, _ = child.shape
    skipped = start // WIDE
    vmem = pl.BlockSpec(memory_space=pltpu.VMEM)
    return pl.pallas_call(
        cross_kernel,
        grid=(ELIMINATED // WIDE,),
        out_shape=jax.ShapeDtypeStruct((ELIMINATED, ELIMINATED), jnp.float32),
        in_specs=[
            vmem,
            vmem,
            pl.BlockSpec((own.shape[0], WIDE), lambda j: (0, skipped + j)),
            pl.BlockSpec((fronts, 1, capacity, WIDE), lambda j: (0, part, 0, j)),
        ],
        out_specs=pl.BlockSpec((WIDE, ELIMINATED), lambda j: (j, 0)),
        compiler_params=pltpu.CompilerParams(vmem_limit_bytes=VMEM_BYTES),
        cost_estimate=LIGHT,
    )(high, low, own, child)


def sharp_dot(a, b, dims):
    (high, low), (other_high, other_low) = a, b
    dims = (dims, ((), ()))
    total = lax.dot_general(high, other_high, dims, preferred_element_type=jnp.float32)
    total += lax.dot_general(high, other_low, dims, preferred_element_type=jnp.float32)
    return total + lax.dot_general(low, other_high, dims, preferred_element_type=jnp.float32)


PLAIN = ((1,), (0,))


def factor_kernel(
    turn_ref, piece_ref, before_ref, after_ref, across_ref, across_rest_ref,
    high_ref, low_ref, leading_ref, work_ref, diag_ref, packed_ref, panel_high_ref, panel_low_ref,
):
    turn = turn_ref[0, 0]
    middle = BLK // 2
    packed_ref[turn] = piece_ref[...]
    packed_ref[lax.rem(turn + 1, 4)] = after_ref[...]
    packed_ref[lax.rem(turn + 3, 4)] = before_ref[...]
    packed_ref[lax.rem(turn + 2, 4), :middle] = across_ref[...]
    packed_ref[lax.rem(turn + 2, 4), middle:] = across_rest_ref[...]
    work_ref[...] = jnp.zeros_like(work_ref)
    panel_high_ref[...] = jnp.zeros_like(panel_high_ref)
    panel_low_ref[...] = jnp.zeros_like(panel_low_ref)
    for block, pair, offset in offsets():
        start = WIDE * block
        for half in range(2):
            work_ref[start + BLK * half : start + BLK * (half + 1), start:] = packed_ref[
                2 * pair + half, :, offset : offset + ELIMINATED - start
            ]
    row = lax.broadcasted_iota(jnp.int32, (BLK, BLK), 0)
    col = lax.broadcasted_iota(jnp.int32, (BLK, BLK), 1)
    place_of = lax.broadcasted_iota(jnp.int32, (BLK, ELIMINATED), 1) // BLK
    chunk_of = lax.broadcasted_iota(jnp.int32, (BLK, WIDE), 1) // BLK
    deferred = [(i, c) for i in range(2, STEPS) for c in range(ELIMINATED // WIDE)]

    def step(k, _):
        here = pl.ds(pl.multiple_of(k * BLK, BLK), BLK)
        block = work_ref[here, here]
        turned = {}

        def update(i, c):
            below = i > k
            rows, cols = slice(BLK * i, BLK * (i + 1)), slice(WIDE * c, WIDE * (c + 1))
            if i not in turned:
                kept = jnp.where(below, 1.0, 0.0)
                turned[i] = [
                    (ref[:, rows].astype(jnp.float32) * kept).T.astype(jnp.bfloat16)
                    for ref in (panel_high_ref, panel_low_ref)
                ]
            panel = (panel_high_ref[:, cols], panel_low_ref[:, cols])
            cleared = jnp.where(below, k - 1 - c * (WIDE // BLK), -1)
            old = jnp.where(chunk_of == cleared, 0.0, work_ref[rows, cols])
            work_ref[rows, cols] = old - sharp_dot(turned[i], panel, PLAIN)

        def beside(b, count):
            for i, c in deferred[len(deferred) * b // count : len(deferred) * (b + 1) // count]:
                update(i, c)

        inverse = lower_inverse(block, beside)
        rows = sharp_dot(halves(inverse), halves(work_ref[here, :]), PLAIN)
        work_ref[here, :] = rows
        diag_ref[here, :] = jnp.where(row <= col, work_ref[here, here], 0.0)
        work_ref[here, here] = inverse
        panel_high_ref[...], panel_low_ref[...] = halves(work_ref[here, :])

        @pl.when(k < STEPS - 1)
        def _():
            there = pl.ds(pl.multiple_of((k + 1) * BLK, BLK), BLK)
            left = [ref[:, there].astype(jnp.float32).T.astype(jnp.bfloat16) for ref in (panel_high_ref, panel_low_ref)]
            old = jnp.where(place_of == k, 0.0, work_ref[there, :])
            work_ref[there, :] = old - sharp_dot(left, (panel_high_ref[...], panel_low_ref[...]), PLAIN)

        return 0

    lax.fori_loop(0, STEPS, step, 0)
    taken = leading_ref.shape[0] // BLK
    for b in range(taken):
        block = turn * taken + b
        here = pl.ds(pl.multiple_of(block * BLK, BLK), BLK)
        diag = jnp.concatenate([diag_ref[here, :]] * STEPS, axis=1)
        leading_ref[BLK * b : BLK * (b + 1), :] = jnp.where(
            place_of > block, work_ref[here, :], jnp.where(place_of == block, diag, 0.0)
        )
    for k in range(STEPS):
        rows = slice(BLK * k, BLK * (k + 1))
        high_ref[rows, :], low_ref[rows, :] = halves(jnp.where(place_of <= k, work_ref[rows, :], 0.0))


def factor(turn, piece, before, after, across, across_rest):
    vmem = pl.BlockSpec(memory_space=pltpu.VMEM)
    return pl.pallas_call(
        factor_kernel,
        out_shape=(
            jax.ShapeDtypeStruct((ELIMINATED, ELIMINATED), jnp.bfloat16),
            jax.ShapeDtypeStruct((ELIMINATED, ELIMINATED), jnp.bfloat16),
            jax.ShapeDtypeStruct((ELIMINATED // 4, ELIMINATED), jnp.float32),
        ),
        in_specs=[pl.BlockSpec(memory_space=pltpu.SMEM)] + [vmem] * 5,
        out_specs=(vmem, vmem, vmem),
        scratch_shapes=[
            pltpu.VMEM((ELIMINATED, ELIMINATED), jnp.float32),
            pltpu.VMEM((ELIMINATED, BLK), jnp.float32),
            pltpu.VMEM((4, BLK, PACKED), jnp.float32),
            pltpu.VMEM((BLK, ELIMINATED), jnp.bfloat16),
            pltpu.VMEM((BLK, ELIMINATED), jnp.bfloat16),
        ],
        compiler_params=pltpu.CompilerParams(vmem_limit_bytes=VMEM_BYTES),
        cost_estimate=LIGHT,
    )(turn, piece, before, after, across, across_rest)


def solve_kernel(high_ref, low_ref, first_ref, second_ref, out_ref):
    parts, quarter, _ = out_ref.shape
    for j, sums_ref in enumerate((first_ref, second_ref)):
        sums = halves(sums_ref[...])
        for i in range(parts):
            rows, depth = slice(quarter * i, quarter * (i + 1)), quarter * (i + 1)
            out_ref[i, :, quarter * j : quarter * (j + 1)] = sharp_dot(
                (high_ref[rows, :depth], low_ref[rows, :depth]),
                tuple(x[:, :depth] for x in sums),
                ((1,), (1,)),
            )


def solve(high, low, first, second):
    vmem = pl.BlockSpec(memory_space=pltpu.VMEM)
    quarter = first.shape[0]
    return pl.pallas_call(
        solve_kernel,
        out_shape=jax.ShapeDtypeStruct((ELIMINATED // quarter, quarter, 2 * quarter), jnp.float32),
        in_specs=[vmem] * 4,
        out_specs=vmem,
        compiler_params=pltpu.CompilerParams(vmem_limit_bytes=VMEM_BYTES),
        cost_estimate=LIGHT,
    )(high, low, first, second)


def join_kernel(col_ref, leading_ref, rows_ref, out_ref):
    parts, _, both = rows_ref.shape
    width = both // 2
    for j in range(parts):
        cols = slice(width * j, width * (j + 1))
        out_ref[0, :, cols] = jnp.where(
            col_ref[0, 0] == 0, leading_ref[:, cols], rows_ref[j, :, :width]
        )
        out_ref[0, :, ELIMINATED + width * j : ELIMINATED + width * (j + 1)] = rows_ref[j, :, width:]


def join(col, leading, rows):
    vmem = pl.BlockSpec(memory_space=pltpu.VMEM)
    return pl.pallas_call(
        join_kernel,
        out_shape=jax.ShapeDtypeStruct((1, leading.shape[0], 2 * ELIMINATED), jnp.float32),
        in_specs=[pl.BlockSpec(memory_space=pltpu.SMEM)] + [vmem] * 2,
        out_specs=vmem,
        compiler_params=pltpu.CompilerParams(vmem_limit_bytes=VMEM_BYTES),
        cost_estimate=LIGHT,
    )(col, leading, rows)


def shifted(x, shift, count):
    return lax.ppermute(x, "row", [(i, (i + shift) % count) for i in range(count)])


def body(own_rows, child_rows, child_dest, child_stair):
    n_front = lax.axis_size("front")
    row_count = lax.axis_size("row")
    source_rows, half_cols = child_rows.shape
    capacity = max(2, 2 * source_rows // n_front)
    col_index = lax.axis_index("col")
    row_index = lax.axis_index("row")
    quarter = ELIMINATED // row_count
    own = own_rows[0]
    own_a = own[:, :ELIMINATED]
    passed = lax.ppermute(own_a, "col", [(0, 1)])

    first_col = col_index * half_cols
    dest, stair = child_dest.reshape(1, source_rows), child_stair.reshape(source_rows, 1)
    doubled = place(first_col, dest, stair, child_rows, 0, 2, n_front, capacity)
    single = place(first_col, dest, stair, child_rows, ELIMINATED, 1, n_front, capacity)
    doubled, single, passed = lax.optimization_barrier((doubled, single, passed))
    arrived = lax.all_to_all(
        doubled.reshape(2 * n_front * capacity, ELIMINATED),
        ("front", "col"),
        split_axis=0,
        concat_axis=0,
        tiled=True,
    ).reshape(n_front, 2, capacity, ELIMINATED)
    child_b = lax.all_to_all(
        single.reshape(n_front * capacity, ELIMINATED), "front", split_axis=0, concat_axis=0, tiled=True
    ).reshape(n_front, 1, capacity, ELIMINATED)
    own_panel = jnp.where(col_index == 0, own_a, passed)

    turn = row_index.reshape(1, 1)
    mine, right, left, right_rest, left_rest, high, low = packed_gram(turn, own_panel, arrived)
    products_a = cross(high, low, own, 0, arrived, 1)
    mine, right, left, products_a = lax.optimization_barrier((mine, right, left, products_a))
    middle = BLK // 2
    from_left, from_right = shifted(right, 1, row_count), shifted(left, -1, row_count)
    rest_left = shifted(right_rest + from_left[:middle], 1, row_count)
    rest_right = shifted(left_rest + from_right[:middle], -1, row_count)
    piece = mine + jnp.concatenate(
        [rest_left + from_right[middle:], from_left[middle:] + rest_right], axis=0
    )
    before, after = shifted(piece, 1, row_count), shifted(piece, -1, row_count)
    across, across_rest = shifted(before[:middle], 1, row_count), shifted(after[middle:], -1, row_count)
    pieces = (piece, before, after, across, across_rest)

    def summed(products):
        return lax.psum_scatter(products, "row", scatter_dimension=0, tiled=True)

    products_b = cross(high, low, own, ELIMINATED, child_b, 0)
    pieces, products_b = lax.optimization_barrier((pieces, products_b))
    inverse_high, inverse_low, leading = factor(turn, *pieces)
    rows = solve(inverse_high, inverse_low, summed(products_a), summed(products_b))
    rows = lax.all_to_all(rows, "row", split_axis=0, concat_axis=0, tiled=True)
    return join(col_index.reshape(1, 1), leading, rows)


def solution(mesh):
    placed = (
        P("front", "row", "col"),
        P(("front", "row"), "col"),
        P(("front", "row"), None),
        P(("front", "row")),
    )
    return jax.shard_map(
        body, mesh=mesh, in_specs=placed, out_specs=P("front", "row", "col"), check_vma=False
    )
```

```python
import jax
import jax.numpy as jnp
from jax import lax
from jax.experimental import pallas as pl
from jax.experimental.pallas import tpu as pltpu
from jax.sharding import PartitionSpec as P

ELIMINATED = 1024
STAIR_BLK = 128
BLK = 128
STEPS = ELIMINATED // BLK
LINES = 8
VMEM_BYTES = 60 * 2**20
LIGHT = pl.CostEstimate(flops=1, bytes_accessed=1, transcendentals=0)


def lower_inverse(diag_block, beside):
    lane = lax.broadcasted_iota(jnp.int32, (LINES, BLK), 1)
    sublane = lax.broadcasted_iota(jnp.int32, (LINES, BLK), 0)
    count = BLK // LINES
    strips = [diag_block[LINES * i : LINES * (i + 1), :] for i in range(count)]
    for b in range(count):
        first = LINES * b
        within = (lane >= first) & (lane < first + LINES)
        strip = strips[b]
        column = [
            jnp.broadcast_to(strip[:, first + t : first + t + 1], (LINES, BLK))
            for t in range(LINES)
        ]
        entry = [
            [jnp.broadcast_to(column[t][i : i + 1, :], (LINES, BLK)) for t in range(i + 1)]
            for i in range(LINES)
        ]
        scale = []
        for t in range(LINES):
            scale.append(lax.rsqrt(entry[t][t]))
            for i in range(t + 1, LINES):
                entry[i][t] = entry[i][t] * scale[t]
            for u in range(t + 1, LINES):
                for i in range(u, LINES):
                    entry[i][u] = entry[i][u] - entry[i][t] * entry[u][t]
        solved = []
        augmented = jnp.where(within, jnp.where(lane == sublane + first, 1.0, 0.0), strip)
        for t in range(LINES):
            line = jnp.broadcast_to(augmented[t : t + 1, :], (LINES, BLK))
            for s in range(t):
                line = line - entry[t][s] * solved[s]
            solved.append(line * scale[t])
        merged = solved[0]
        for t in range(1, LINES):
            merged = jnp.where(sublane == t, solved[t], merged)
        strips[b] = merged
        beside(b, count)
        for i in range(b + 1, count):
            below = strips[i]
            rest = jnp.where(within, 0.0, below)
            factors = []
            for t in range(LINES):
                value = jnp.broadcast_to(below[:, first + t : first + t + 1], (LINES, BLK))
                for s in range(t):
                    value = value - entry[t][s] * factors[s]
                value = value * scale[t]
                factors.append(value)
                rest = rest - value * solved[t]
            strips[i] = rest
    row = lax.broadcasted_iota(jnp.int32, (BLK, BLK), 0)
    col = lax.broadcasted_iota(jnp.int32, (BLK, BLK), 1)
    return jnp.where(row >= col, jnp.concatenate(strips, axis=0), 0.0)


PAIRS = ((0, 3), (1, 2))
WIDE = 256
PACKED = ELIMINATED + WIDE


def offsets():
    found = []
    for pair, (long, short) in enumerate(PAIRS):
        found.append((long, pair, 0))
        found.append((short, pair, ELIMINATED - WIDE * long))
    return found


def halves(x):
    high = x.astype(jnp.bfloat16)
    return high, (x - high.astype(jnp.float32)).astype(jnp.bfloat16)


def place_kernel(first_ref, dest_ref, stair_ref, rows_ref, out_ref, select_ref):
    fronts, copies, capacity, width = out_ref.shape
    slots, sources = select_ref.shape
    chunk = pl.program_id(0)

    @pl.when(chunk == 0)
    def _():
        dest = dest_ref[...]
        named = lax.broadcasted_iota(jnp.int32, (fronts, sources), 0) == dest
        source = lax.broadcasted_iota(jnp.int32, (sources, sources), 0)
        later = lax.broadcasted_iota(jnp.int32, (sources, sources), 1)
        before = jnp.dot(
            named.astype(jnp.float32).astype(jnp.bfloat16),
            (source < later).astype(jnp.float32).astype(jnp.bfloat16),
            preferred_element_type=jnp.float32,
        )
        slot = jnp.sum(jnp.where(named, before, 0.0), axis=0, keepdims=True).astype(jnp.int32)
        position = dest * capacity + slot
        line = lax.broadcasted_iota(jnp.int32, (slots, sources), 0)
        select_ref[...] = (line == position).astype(jnp.float32).astype(jnp.bfloat16)

    cols = (
        first_ref[0, 0] + chunk * width + lax.broadcasted_iota(jnp.int32, (sources, width), 1)
    )
    high, low = halves(jnp.where(cols >= stair_ref[...] * STAIR_BLK, rows_ref[...], 0.0))
    select = select_ref[...]
    placed = jnp.dot(select, high, preferred_element_type=jnp.float32) + jnp.dot(
        select, low, preferred_element_type=jnp.float32
    )
    placed = placed.reshape(fronts, capacity, width)
    for copy in range(copies):
        out_ref[:, copy] = placed


def place(first_col, dest, stair, rows, start, copies, n_front, capacity):
    sources = rows.shape[0]
    skipped = start // WIDE
    return pl.pallas_call(
        place_kernel,
        grid=(ELIMINATED // WIDE,),
        out_shape=jax.ShapeDtypeStruct((n_front, copies, capacity, ELIMINATED), jnp.float32),
        in_specs=[
            pl.BlockSpec(memory_space=pltpu.SMEM),
            pl.BlockSpec((1, sources), lambda j: (0, 0)),
            pl.BlockSpec((sources, 1), lambda j: (0, 0)),
            pl.BlockSpec((sources, WIDE), lambda j: (0, skipped + j)),
        ],
        out_specs=pl.BlockSpec((n_front, copies, capacity, WIDE), lambda j: (0, 0, 0, j)),
        scratch_shapes=[pltpu.VMEM((n_front * capacity, sources), jnp.bfloat16)],
        compiler_params=pltpu.CompilerParams(vmem_limit_bytes=VMEM_BYTES),
        cost_estimate=LIGHT,
    )((first_col + start).reshape(1, 1), dest, stair, rows)


def stacked_halves(out_ref, *parts):
    count = out_ref.shape[0] // 2
    first = 0
    for x in parts:
        rows = x.shape[0]
        high, low = halves(x)
        out_ref[first : first + rows] = low
        out_ref[count + first : count + first + rows] = high
        first += rows


def turned_dot(turned, other):
    count = other.shape[0] // 2
    return jnp.dot(turned, other, preferred_element_type=jnp.float32) + jnp.dot(
        turned[:, :count], other[count:], preferred_element_type=jnp.float32
    )


def gram_kernel(turn_ref, own_ref, child_ref, *outs):
    turned_ref, both_ref, packed_ref = outs[5:]
    count = both_ref.shape[0] // 2
    stacked_halves(both_ref, own_ref[...], child_ref[:, 0].reshape(-1, ELIMINATED))
    for start in range(0, ELIMINATED, WIDE):
        cols = slice(start, start + WIDE)
        turned_ref[cols, :count] = both_ref[count:, cols].T
        turned_ref[cols, count:] = both_ref[:count, cols].T
    for block, pair, offset in offsets():
        start = WIDE * block
        total = turned_dot(turned_ref[start : start + WIDE, :], both_ref[:, start:])
        for half in range(2):
            packed_ref[2 * pair + half, :, offset : offset + ELIMINATED - start] = total[
                BLK * half : BLK * (half + 1)
            ]
    mine_ref, right_ref, left_ref, right_rest_ref, left_rest_ref, *_ = outs
    turn = turn_ref[0, 0]
    here, right, over, left = [lax.rem(turn + s, 4) for s in range(4)]
    middle = BLK // 2
    mine_ref[...] = packed_ref[here]
    right_ref[:middle], right_ref[middle:] = packed_ref[over, :middle], packed_ref[right, middle:]
    left_ref[:middle], left_ref[middle:] = packed_ref[over, middle:], packed_ref[left, :middle]
    right_rest_ref[...] = packed_ref[right, :middle]
    left_rest_ref[...] = packed_ref[left, middle:]


def packed_gram(turn, own_panel, arrived):
    fronts, _, capacity, _ = arrived.shape
    rows = own_panel.shape[0] + fronts * capacity
    vmem = pl.BlockSpec(memory_space=pltpu.VMEM)
    return pl.pallas_call(
        gram_kernel,
        grid=(1,),
        out_shape=[jax.ShapeDtypeStruct((BLK, PACKED), jnp.float32)] * 3
        + [jax.ShapeDtypeStruct((BLK // 2, PACKED), jnp.float32)] * 2
        + [jax.ShapeDtypeStruct((ELIMINATED, 2 * rows), jnp.bfloat16)],
        in_specs=[
            pl.BlockSpec(memory_space=pltpu.SMEM),
            vmem,
            pl.BlockSpec((fronts, 1, capacity, ELIMINATED), lambda j: (0, 0, 0, 0)),
        ],
        out_specs=[vmem] * 6,
        scratch_shapes=[pltpu.VMEM((2 * rows, ELIMINATED), jnp.bfloat16), pltpu.VMEM((4, BLK, PACKED), jnp.float32)],
        compiler_params=pltpu.CompilerParams(vmem_limit_bytes=VMEM_BYTES),
        cost_estimate=LIGHT,
    )(turn, own_panel, arrived)


def cross_kernel(turned_ref, own_ref, child_ref, out_ref, both_ref):
    stacked_halves(both_ref, own_ref[...], child_ref[:, 0].reshape(-1, WIDE))
    out_ref[0] = turned_dot(turned_ref[...], both_ref[...])


def cross(turned, own, start, child, part):
    fronts, _, capacity, _ = child.shape
    skipped = start // WIDE
    return pl.pallas_call(
        cross_kernel,
        grid=(ELIMINATED // WIDE,),
        out_shape=jax.ShapeDtypeStruct((ELIMINATED // WIDE, ELIMINATED, WIDE), jnp.float32),
        in_specs=[
            pl.BlockSpec(memory_space=pltpu.VMEM),
            pl.BlockSpec((own.shape[0], WIDE), lambda j: (0, skipped + j)),
            pl.BlockSpec((fronts, 1, capacity, WIDE), lambda j: (0, part, 0, j)),
        ],
        out_specs=pl.BlockSpec((1, ELIMINATED, WIDE), lambda j: (j, 0, 0)),
        scratch_shapes=[pltpu.VMEM((turned.shape[1], WIDE), jnp.bfloat16)],
        compiler_params=pltpu.CompilerParams(vmem_limit_bytes=VMEM_BYTES),
        cost_estimate=LIGHT,
    )(turned, own, child)


def sharp_dot(a, b, dims):
    (high, low), (other_high, other_low) = a, b
    dims = (dims, ((), ()))
    total = lax.dot_general(high, other_high, dims, preferred_element_type=jnp.float32)
    total += lax.dot_general(high, other_low, dims, preferred_element_type=jnp.float32)
    return total + lax.dot_general(low, other_high, dims, preferred_element_type=jnp.float32)


PLAIN = ((1,), (0,))


def factor_kernel(
    turn_ref, piece_ref, before_ref, after_ref, across_ref, across_rest_ref,
    high_ref, low_ref, leading_ref, work_ref, diag_ref, packed_ref, panel_high_ref, panel_low_ref,
):
    turn = turn_ref[0, 0]
    middle = BLK // 2
    packed_ref[turn] = piece_ref[...]
    packed_ref[lax.rem(turn + 1, 4)] = after_ref[...]
    packed_ref[lax.rem(turn + 3, 4)] = before_ref[...]
    packed_ref[lax.rem(turn + 2, 4), :middle] = across_ref[...]
    packed_ref[lax.rem(turn + 2, 4), middle:] = across_rest_ref[...]
    work_ref[...] = jnp.zeros_like(work_ref)
    panel_high_ref[...] = jnp.zeros_like(panel_high_ref)
    panel_low_ref[...] = jnp.zeros_like(panel_low_ref)
    for block, pair, offset in offsets():
        start = WIDE * block
        for half in range(2):
            work_ref[start + BLK * half : start + BLK * (half + 1), start:] = packed_ref[
                2 * pair + half, :, offset : offset + ELIMINATED - start
            ]
    row = lax.broadcasted_iota(jnp.int32, (BLK, BLK), 0)
    col = lax.broadcasted_iota(jnp.int32, (BLK, BLK), 1)
    place_of = lax.broadcasted_iota(jnp.int32, (BLK, ELIMINATED), 1) // BLK
    chunk_of = lax.broadcasted_iota(jnp.int32, (BLK, WIDE), 1) // BLK
    deferred = [(i, c) for i in range(2, STEPS) for c in range(ELIMINATED // WIDE)]

    def step(k, _):
        here = pl.ds(pl.multiple_of(k * BLK, BLK), BLK)
        block = work_ref[here, here]
        turned = {}

        def update(i, c):
            below = i > k
            rows, cols = slice(BLK * i, BLK * (i + 1)), slice(WIDE * c, WIDE * (c + 1))
            if i not in turned:
                kept = jnp.where(below, 1.0, 0.0)
                turned[i] = [
                    (ref[:, rows].astype(jnp.float32) * kept).T.astype(jnp.bfloat16)
                    for ref in (panel_high_ref, panel_low_ref)
                ]
            panel = (panel_high_ref[:, cols], panel_low_ref[:, cols])
            cleared = jnp.where(below, k - 1 - c * (WIDE // BLK), -1)
            old = jnp.where(chunk_of == cleared, 0.0, work_ref[rows, cols])
            work_ref[rows, cols] = old - sharp_dot(turned[i], panel, PLAIN)

        def beside(b, count):
            for i, c in deferred[len(deferred) * b // count : len(deferred) * (b + 1) // count]:
                update(i, c)

        inverse = lower_inverse(block, beside)
        rows = sharp_dot(halves(inverse), halves(work_ref[here, :]), PLAIN)
        work_ref[here, :] = rows
        diag_ref[here, :] = jnp.where(row <= col, work_ref[here, here], 0.0)
        work_ref[here, here] = inverse
        panel_high_ref[...], panel_low_ref[...] = halves(work_ref[here, :])

        @pl.when(k < STEPS - 1)
        def _():
            there = pl.ds(pl.multiple_of((k + 1) * BLK, BLK), BLK)
            left = [ref[:, there].astype(jnp.float32).T.astype(jnp.bfloat16) for ref in (panel_high_ref, panel_low_ref)]
            old = jnp.where(place_of == k, 0.0, work_ref[there, :])
            work_ref[there, :] = old - sharp_dot(left, (panel_high_ref[...], panel_low_ref[...]), PLAIN)

        return 0

    lax.fori_loop(0, STEPS, step, 0)
    taken = leading_ref.shape[0] // BLK
    for b in range(taken):
        block = turn * taken + b
        here = pl.ds(pl.multiple_of(block * BLK, BLK), BLK)
        diag = jnp.concatenate([diag_ref[here, :]] * STEPS, axis=1)
        leading_ref[BLK * b : BLK * (b + 1), :] = jnp.where(
            place_of > block, work_ref[here, :], jnp.where(place_of == block, diag, 0.0)
        )
    for k in range(STEPS):
        rows = slice(BLK * k, BLK * (k + 1))
        high_ref[rows, :], low_ref[rows, :] = halves(jnp.where(place_of <= k, work_ref[rows, :], 0.0))


def factor(turn, piece, before, after, across, across_rest):
    vmem = pl.BlockSpec(memory_space=pltpu.VMEM)
    return pl.pallas_call(
        factor_kernel,
        out_shape=(
            jax.ShapeDtypeStruct((ELIMINATED, ELIMINATED), jnp.bfloat16),
            jax.ShapeDtypeStruct((ELIMINATED, ELIMINATED), jnp.bfloat16),
            jax.ShapeDtypeStruct((ELIMINATED // 4, ELIMINATED), jnp.float32),
        ),
        in_specs=[pl.BlockSpec(memory_space=pltpu.SMEM)] + [vmem] * 5,
        out_specs=(vmem, vmem, vmem),
        scratch_shapes=[
            pltpu.VMEM((ELIMINATED, ELIMINATED), jnp.float32),
            pltpu.VMEM((ELIMINATED, BLK), jnp.float32),
            pltpu.VMEM((4, BLK, PACKED), jnp.float32),
            pltpu.VMEM((BLK, ELIMINATED), jnp.bfloat16),
            pltpu.VMEM((BLK, ELIMINATED), jnp.bfloat16),
        ],
        compiler_params=pltpu.CompilerParams(vmem_limit_bytes=VMEM_BYTES),
        cost_estimate=LIGHT,
    )(turn, piece, before, after, across, across_rest)


def solve_kernel(high_ref, low_ref, first_ref, second_ref, out_ref):
    parts, quarter, _ = out_ref.shape
    for j, sums_ref in enumerate((first_ref, second_ref)):
        sums = halves(sums_ref[0])
        for i in range(parts):
            rows, depth = slice(quarter * i, quarter * (i + 1)), quarter * (i + 1)
            out_ref[i, :, quarter * j : quarter * (j + 1)] = sharp_dot(
                (high_ref[rows, :depth], low_ref[rows, :depth]),
                tuple(x[:depth] for x in sums),
                PLAIN,
            )


def solve(high, low, first, second):
    vmem = pl.BlockSpec(memory_space=pltpu.VMEM)
    quarter = first.shape[2]
    return pl.pallas_call(
        solve_kernel,
        out_shape=jax.ShapeDtypeStruct((ELIMINATED // quarter, quarter, 2 * quarter), jnp.float32),
        in_specs=[vmem] * 4,
        out_specs=vmem,
        compiler_params=pltpu.CompilerParams(vmem_limit_bytes=VMEM_BYTES),
        cost_estimate=LIGHT,
    )(high, low, first, second)


def join_kernel(col_ref, leading_ref, rows_ref, out_ref):
    parts, _, both = rows_ref.shape
    width = both // 2
    for j in range(parts):
        cols = slice(width * j, width * (j + 1))
        out_ref[0, :, cols] = jnp.where(
            col_ref[0, 0] == 0, leading_ref[:, cols], rows_ref[j, :, :width]
        )
        out_ref[0, :, ELIMINATED + width * j : ELIMINATED + width * (j + 1)] = rows_ref[j, :, width:]


def join(col, leading, rows):
    vmem = pl.BlockSpec(memory_space=pltpu.VMEM)
    return pl.pallas_call(
        join_kernel,
        out_shape=jax.ShapeDtypeStruct((1, leading.shape[0], 2 * ELIMINATED), jnp.float32),
        in_specs=[pl.BlockSpec(memory_space=pltpu.SMEM)] + [vmem] * 2,
        out_specs=vmem,
        compiler_params=pltpu.CompilerParams(vmem_limit_bytes=VMEM_BYTES),
        cost_estimate=LIGHT,
    )(col, leading, rows)


def shifted(x, shift, count):
    return lax.ppermute(x, "row", [(i, (i + shift) % count) for i in range(count)])


def body(own_rows, child_rows, child_dest, child_stair):
    n_front = lax.axis_size("front")
    row_count = lax.axis_size("row")
    source_rows, half_cols = child_rows.shape
    capacity = max(2, 2 * source_rows // n_front)
    col_index = lax.axis_index("col")
    row_index = lax.axis_index("row")
    quarter = ELIMINATED // row_count
    own = own_rows[0]
    own_a = own[:, :ELIMINATED]
    split = own_a.shape[0] // 2
    passed = lax.ppermute(own_a[:split], "col", [(0, 1)])
    passed_rest = lax.ppermute(own_a[split:], "col", [(0, 1)])

    first_col = col_index * half_cols
    dest, stair = child_dest.reshape(1, source_rows), child_stair.reshape(source_rows, 1)
    doubled = place(first_col, dest, stair, child_rows, 0, 2, n_front, capacity)
    single = place(first_col, dest, stair, child_rows, ELIMINATED, 1, n_front, capacity)
    doubled, single, passed = lax.optimization_barrier((doubled, single, passed))
    arrived = lax.all_to_all(
        doubled.reshape(2 * n_front * capacity, ELIMINATED),
        ("front", "col"),
        split_axis=0,
        concat_axis=0,
        tiled=True,
    ).reshape(n_front, 2, capacity, ELIMINATED)
    child_b = lax.all_to_all(
        single.reshape(n_front * capacity, ELIMINATED), "front", split_axis=0, concat_axis=0, tiled=True
    ).reshape(n_front, 1, capacity, ELIMINATED)
    own_panel = jnp.where(col_index == 0, own_a, jnp.concatenate([passed, passed_rest], axis=0))

    turn = row_index.reshape(1, 1)
    mine, right, left, right_rest, left_rest, turned = packed_gram(turn, own_panel, arrived)
    products_a = cross(turned, own, 0, arrived, 1)
    mine, right, left, products_a = lax.optimization_barrier((mine, right, left, products_a))
    middle = BLK // 2
    from_left, from_right = shifted(right, 1, row_count), shifted(left, -1, row_count)
    rest_left = shifted(right_rest + from_left[:middle], 1, row_count)
    rest_right = shifted(left_rest + from_right[:middle], -1, row_count)
    piece = mine + jnp.concatenate(
        [rest_left + from_right[middle:], from_left[middle:] + rest_right], axis=0
    )
    before, after = shifted(piece, 1, row_count), shifted(piece, -1, row_count)
    across, across_rest = shifted(before[:middle], 1, row_count), shifted(after[middle:], -1, row_count)
    pieces = (piece, before, after, across, across_rest)

    def summed(products):
        return lax.psum_scatter(products, "row", scatter_dimension=0, tiled=True)

    products_b = cross(turned, own, ELIMINATED, child_b, 0)
    pieces, products_b = lax.optimization_barrier((pieces, products_b))
    inverse_high, inverse_low, leading = factor(turn, *pieces)
    rows = solve(inverse_high, inverse_low, summed(products_a), summed(products_b))
    rows = lax.all_to_all(rows, "row", split_axis=0, concat_axis=0, tiled=True)
    return join(col_index.reshape(1, 1), leading, rows)


def solution(mesh):
    placed = (
        P("front", "row", "col"),
        P(("front", "row"), "col"),
        P(("front", "row"), None),
        P(("front", "row")),
    )
    return jax.shard_map(
        body, mesh=mesh, in_specs=placed, out_specs=P("front", "row", "col"), check_vma=False
    )
```

```python
import jax
import jax.numpy as jnp
from jax import lax
from jax.experimental import pallas as pl
from jax.experimental.pallas import tpu as pltpu
from jax.sharding import PartitionSpec as P

ELIMINATED = 1024
STAIR_BLK = 128
BLK = 128
STEPS = ELIMINATED // BLK
LINES = 8
VMEM_BYTES = 60 * 2**20
LIGHT = pl.CostEstimate(flops=1, bytes_accessed=1, transcendentals=0)


def lower_inverse(diag_block, beside):
    lane = lax.broadcasted_iota(jnp.int32, (LINES, BLK), 1)
    sublane = lax.broadcasted_iota(jnp.int32, (LINES, BLK), 0)
    count = BLK // LINES
    strips = [diag_block[LINES * i : LINES * (i + 1), :] for i in range(count)]
    for b in range(count):
        first = LINES * b
        within = (lane >= first) & (lane < first + LINES)
        strip = strips[b]
        column = [
            jnp.broadcast_to(strip[:, first + t : first + t + 1], (LINES, BLK))
            for t in range(LINES)
        ]
        entry = [
            [jnp.broadcast_to(column[t][i : i + 1, :], (LINES, BLK)) for t in range(i + 1)]
            for i in range(LINES)
        ]
        scale = []
        for t in range(LINES):
            scale.append(lax.rsqrt(entry[t][t]))
            for i in range(t + 1, LINES):
                entry[i][t] = entry[i][t] * scale[t]
            for u in range(t + 1, LINES):
                for i in range(u, LINES):
                    entry[i][u] = entry[i][u] - entry[i][t] * entry[u][t]
        solved = []
        augmented = jnp.where(within, jnp.where(lane == sublane + first, 1.0, 0.0), strip)
        for t in range(LINES):
            line = jnp.broadcast_to(augmented[t : t + 1, :], (LINES, BLK))
            for s in range(t):
                line = line - entry[t][s] * solved[s]
            solved.append(line * scale[t])
        merged = solved[0]
        for t in range(1, LINES):
            merged = jnp.where(sublane == t, solved[t], merged)
        strips[b] = merged
        beside(b, count)
        for i in range(b + 1, count):
            below = strips[i]
            rest = jnp.where(within, 0.0, below)
            factors = []
            for t in range(LINES):
                value = jnp.broadcast_to(below[:, first + t : first + t + 1], (LINES, BLK))
                for s in range(t):
                    value = value - entry[t][s] * factors[s]
                value = value * scale[t]
                factors.append(value)
                rest = rest - value * solved[t]
            strips[i] = rest
    row = lax.broadcasted_iota(jnp.int32, (BLK, BLK), 0)
    col = lax.broadcasted_iota(jnp.int32, (BLK, BLK), 1)
    return jnp.where(row >= col, jnp.concatenate(strips, axis=0), 0.0)


PAIRS = ((0, 3), (1, 2))
WIDE = 256
PACKED = ELIMINATED + WIDE


def offsets():
    found = []
    for pair, (long, short) in enumerate(PAIRS):
        found.append((long, pair, 0))
        found.append((short, pair, ELIMINATED - WIDE * long))
    return found


def halves(x):
    high = x.astype(jnp.bfloat16)
    return high, (x - high.astype(jnp.float32)).astype(jnp.bfloat16)


def place_kernel(first_ref, dest_ref, stair_ref, rows_ref, out_ref, select_ref):
    fronts, copies, capacity, width = out_ref.shape
    slots, sources = select_ref.shape
    chunk = pl.program_id(0)

    @pl.when(chunk == 0)
    def _():
        dest = dest_ref[...]
        named = lax.broadcasted_iota(jnp.int32, (fronts, sources), 0) == dest
        source = lax.broadcasted_iota(jnp.int32, (sources, sources), 0)
        later = lax.broadcasted_iota(jnp.int32, (sources, sources), 1)
        before = jnp.dot(
            named.astype(jnp.float32).astype(jnp.bfloat16),
            (source < later).astype(jnp.float32).astype(jnp.bfloat16),
            preferred_element_type=jnp.float32,
        )
        slot = jnp.sum(jnp.where(named, before, 0.0), axis=0, keepdims=True).astype(jnp.int32)
        position = dest * capacity + slot
        line = lax.broadcasted_iota(jnp.int32, (slots, sources), 0)
        select_ref[...] = (line == position).astype(jnp.float32).astype(jnp.bfloat16)

    cols = (
        first_ref[0, 0] + chunk * width + lax.broadcasted_iota(jnp.int32, (sources, width), 1)
    )
    high, low = halves(jnp.where(cols >= stair_ref[...] * STAIR_BLK, rows_ref[...], 0.0))
    select = select_ref[...]
    placed = jnp.dot(select, high, preferred_element_type=jnp.float32) + jnp.dot(
        select, low, preferred_element_type=jnp.float32
    )
    placed = placed.reshape(fronts, capacity, width)
    for copy in range(copies):
        out_ref[:, copy] = placed


def place(first_col, dest, stair, rows, start, copies, n_front, capacity):
    sources = rows.shape[0]
    skipped = start // WIDE
    return pl.pallas_call(
        place_kernel,
        grid=(ELIMINATED // WIDE,),
        out_shape=jax.ShapeDtypeStruct((n_front, copies, capacity, ELIMINATED), jnp.float32),
        in_specs=[
            pl.BlockSpec(memory_space=pltpu.SMEM),
            pl.BlockSpec((1, sources), lambda j: (0, 0)),
            pl.BlockSpec((sources, 1), lambda j: (0, 0)),
            pl.BlockSpec((sources, WIDE), lambda j: (0, skipped + j)),
        ],
        out_specs=pl.BlockSpec((n_front, copies, capacity, WIDE), lambda j: (0, 0, 0, j)),
        scratch_shapes=[pltpu.VMEM((n_front * capacity, sources), jnp.bfloat16)],
        compiler_params=pltpu.CompilerParams(vmem_limit_bytes=VMEM_BYTES),
        cost_estimate=LIGHT,
    )((first_col + start).reshape(1, 1), dest, stair, rows)


def stacked_halves(out_ref, *parts):
    count = out_ref.shape[0] // 2
    first = 0
    for x in parts:
        rows = x.shape[0]
        high, low = halves(x)
        out_ref[first : first + rows] = low
        out_ref[count + first : count + first + rows] = high
        first += rows


def turned_dot(turned, other):
    count = other.shape[0] // 2
    return jnp.dot(turned, other, preferred_element_type=jnp.float32) + jnp.dot(
        turned[:, :count], other[count:], preferred_element_type=jnp.float32
    )


def gram_kernel(turn_ref, own_ref, child_ref, *outs):
    turned_ref, both_ref, packed_ref = outs[5:]
    count = both_ref.shape[0] // 2
    stacked_halves(both_ref, own_ref[...], child_ref[:, 0].reshape(-1, ELIMINATED))
    for start in range(0, ELIMINATED, WIDE):
        cols = slice(start, start + WIDE)
        turned_ref[cols, :count] = both_ref[count:, cols].T
        turned_ref[cols, count:] = both_ref[:count, cols].T
    for block, pair, offset in offsets():
        start = WIDE * block
        total = turned_dot(turned_ref[start : start + WIDE, :], both_ref[:, start:])
        for half in range(2):
            packed_ref[2 * pair + half, :, offset : offset + ELIMINATED - start] = total[
                BLK * half : BLK * (half + 1)
            ]
    mine_ref, right_ref, left_ref, right_rest_ref, left_rest_ref, *_ = outs
    turn = turn_ref[0, 0]
    here, right, over, left = [lax.rem(turn + s, 4) for s in range(4)]
    middle = BLK // 2
    mine_ref[...] = packed_ref[here]
    right_ref[:middle], right_ref[middle:] = packed_ref[over, :middle], packed_ref[right, middle:]
    left_ref[:middle], left_ref[middle:] = packed_ref[over, middle:], packed_ref[left, :middle]
    right_rest_ref[...] = packed_ref[right, :middle]
    left_rest_ref[...] = packed_ref[left, middle:]


def packed_gram(turn, own_panel, arrived):
    fronts, _, capacity, _ = arrived.shape
    rows = own_panel.shape[0] + fronts * capacity
    vmem = pl.BlockSpec(memory_space=pltpu.VMEM)
    return pl.pallas_call(
        gram_kernel,
        grid=(1,),
        out_shape=[jax.ShapeDtypeStruct((BLK, PACKED), jnp.float32)] * 3
        + [jax.ShapeDtypeStruct((BLK // 2, PACKED), jnp.float32)] * 2
        + [jax.ShapeDtypeStruct((ELIMINATED, 2 * rows), jnp.bfloat16)],
        in_specs=[
            pl.BlockSpec(memory_space=pltpu.SMEM),
            vmem,
            pl.BlockSpec((fronts, 1, capacity, ELIMINATED), lambda j: (0, 0, 0, 0)),
        ],
        out_specs=[vmem] * 6,
        scratch_shapes=[pltpu.VMEM((2 * rows, ELIMINATED), jnp.bfloat16), pltpu.VMEM((4, BLK, PACKED), jnp.float32)],
        compiler_params=pltpu.CompilerParams(vmem_limit_bytes=VMEM_BYTES),
        cost_estimate=LIGHT,
    )(turn, own_panel, arrived)


def cross_kernel(turned_ref, own_ref, child_ref, out_ref, both_ref):
    stacked_halves(both_ref, own_ref[...], child_ref[:, 0].reshape(-1, WIDE))
    out_ref[0] = turned_dot(turned_ref[...], both_ref[...])


def cross(turned, own, start, child, part):
    fronts, _, capacity, _ = child.shape
    skipped = start // WIDE
    return pl.pallas_call(
        cross_kernel,
        grid=(ELIMINATED // WIDE,),
        out_shape=jax.ShapeDtypeStruct((ELIMINATED // WIDE, ELIMINATED, WIDE), jnp.float32),
        in_specs=[
            pl.BlockSpec(memory_space=pltpu.VMEM),
            pl.BlockSpec((own.shape[0], WIDE), lambda j: (0, skipped + j)),
            pl.BlockSpec((fronts, 1, capacity, WIDE), lambda j: (0, part, 0, j)),
        ],
        out_specs=pl.BlockSpec((1, ELIMINATED, WIDE), lambda j: (j, 0, 0)),
        scratch_shapes=[pltpu.VMEM((turned.shape[1], WIDE), jnp.bfloat16)],
        compiler_params=pltpu.CompilerParams(vmem_limit_bytes=VMEM_BYTES),
        cost_estimate=LIGHT,
    )(turned, own, child)


def shared_kernel(_, turned_ref, own_ref, child_ref, out_ref, both_ref):
    stacked_halves(both_ref, own_ref[...], child_ref[:, 0].reshape(-1, WIDE))
    total = turned_dot(turned_ref[...], both_ref[...])
    for half in range(2):
        out_ref[half] = total[:, BLK * half : BLK * (half + 1)]


def shared_cross(col, turned, own, child):
    fronts, _, capacity, _ = child.shape
    steps = own.shape[1] // WIDE
    return pl.pallas_call(
        shared_kernel,
        grid_spec=pltpu.PrefetchScalarGridSpec(
            num_scalar_prefetch=1,
            grid=(steps,),
            in_specs=[
                pl.BlockSpec(memory_space=pltpu.VMEM),
                pl.BlockSpec((own.shape[0], WIDE), lambda j, c: (0, j)),
                pl.BlockSpec((fronts, 1, capacity, WIDE), lambda j, c: (0, 1, 0, c[0] * steps + j)),
            ],
            out_specs=pl.BlockSpec((2, ELIMINATED, BLK), lambda j, c: (j, 0, 0)),
            scratch_shapes=[pltpu.VMEM((turned.shape[1], WIDE), jnp.bfloat16)],
        ),
        out_shape=jax.ShapeDtypeStruct((own.shape[1] // BLK, ELIMINATED, BLK), jnp.float32),
        compiler_params=pltpu.CompilerParams(vmem_limit_bytes=VMEM_BYTES),
        cost_estimate=LIGHT,
    )(col, turned, own, child)


def sharp_dot(a, b, dims):
    (high, low), (other_high, other_low) = a, b
    dims = (dims, ((), ()))
    total = lax.dot_general(high, other_high, dims, preferred_element_type=jnp.float32)
    total += lax.dot_general(high, other_low, dims, preferred_element_type=jnp.float32)
    return total + lax.dot_general(low, other_high, dims, preferred_element_type=jnp.float32)


PLAIN = ((1,), (0,))


def factor_kernel(
    turn_ref, piece_ref, before_ref, after_ref, across_ref, across_rest_ref,
    high_ref, low_ref, leading_ref, work_ref, diag_ref, packed_ref, panel_high_ref, panel_low_ref,
):
    turn = turn_ref[0, 0]
    middle = BLK // 2
    packed_ref[turn] = piece_ref[...]
    packed_ref[lax.rem(turn + 1, 4)] = after_ref[...]
    packed_ref[lax.rem(turn + 3, 4)] = before_ref[...]
    packed_ref[lax.rem(turn + 2, 4), :middle] = across_ref[...]
    packed_ref[lax.rem(turn + 2, 4), middle:] = across_rest_ref[...]
    work_ref[...] = jnp.zeros_like(work_ref)
    panel_high_ref[...] = jnp.zeros_like(panel_high_ref)
    panel_low_ref[...] = jnp.zeros_like(panel_low_ref)
    for block, pair, offset in offsets():
        start = WIDE * block
        for half in range(2):
            work_ref[start + BLK * half : start + BLK * (half + 1), start:] = packed_ref[
                2 * pair + half, :, offset : offset + ELIMINATED - start
            ]
    row = lax.broadcasted_iota(jnp.int32, (BLK, BLK), 0)
    col = lax.broadcasted_iota(jnp.int32, (BLK, BLK), 1)
    place_of = lax.broadcasted_iota(jnp.int32, (BLK, ELIMINATED), 1) // BLK
    chunk_of = lax.broadcasted_iota(jnp.int32, (BLK, WIDE), 1) // BLK
    deferred = [(i, c) for i in range(2, STEPS) for c in range(ELIMINATED // WIDE)]

    def step(k, _):
        here = pl.ds(pl.multiple_of(k * BLK, BLK), BLK)
        block = work_ref[here, here]
        turned = {}

        def update(i, c):
            below = i > k
            rows, cols = slice(BLK * i, BLK * (i + 1)), slice(WIDE * c, WIDE * (c + 1))
            if i not in turned:
                kept = jnp.where(below, 1.0, 0.0)
                turned[i] = [
                    (ref[:, rows].astype(jnp.float32) * kept).T.astype(jnp.bfloat16)
                    for ref in (panel_high_ref, panel_low_ref)
                ]
            panel = (panel_high_ref[:, cols], panel_low_ref[:, cols])
            cleared = jnp.where(below, k - 1 - c * (WIDE // BLK), -1)
            old = jnp.where(chunk_of == cleared, 0.0, work_ref[rows, cols])
            work_ref[rows, cols] = old - sharp_dot(turned[i], panel, PLAIN)

        def beside(b, count):
            for i, c in deferred[len(deferred) * b // count : len(deferred) * (b + 1) // count]:
                update(i, c)

        inverse = lower_inverse(block, beside)
        rows = sharp_dot(halves(inverse), halves(work_ref[here, :]), PLAIN)
        work_ref[here, :] = rows
        diag_ref[here, :] = jnp.where(row <= col, work_ref[here, here], 0.0)
        work_ref[here, here] = inverse
        panel_high_ref[...], panel_low_ref[...] = halves(work_ref[here, :])

        @pl.when(k < STEPS - 1)
        def _():
            there = pl.ds(pl.multiple_of((k + 1) * BLK, BLK), BLK)
            left = [ref[:, there].astype(jnp.float32).T.astype(jnp.bfloat16) for ref in (panel_high_ref, panel_low_ref)]
            old = jnp.where(place_of == k, 0.0, work_ref[there, :])
            work_ref[there, :] = old - sharp_dot(left, (panel_high_ref[...], panel_low_ref[...]), PLAIN)

        return 0

    lax.fori_loop(0, STEPS, step, 0)
    taken = leading_ref.shape[0] // BLK
    for b in range(taken):
        block = turn * taken + b
        here = pl.ds(pl.multiple_of(block * BLK, BLK), BLK)
        diag = jnp.concatenate([diag_ref[here, :]] * STEPS, axis=1)
        leading_ref[BLK * b : BLK * (b + 1), :] = jnp.where(
            place_of > block, work_ref[here, :], jnp.where(place_of == block, diag, 0.0)
        )
    for k in range(STEPS):
        rows = slice(BLK * k, BLK * (k + 1))
        high_ref[rows, :], low_ref[rows, :] = halves(jnp.where(place_of <= k, work_ref[rows, :], 0.0))


def factor(turn, piece, before, after, across, across_rest):
    vmem = pl.BlockSpec(memory_space=pltpu.VMEM)
    return pl.pallas_call(
        factor_kernel,
        out_shape=(
            jax.ShapeDtypeStruct((ELIMINATED, ELIMINATED), jnp.bfloat16),
            jax.ShapeDtypeStruct((ELIMINATED, ELIMINATED), jnp.bfloat16),
            jax.ShapeDtypeStruct((ELIMINATED // 4, ELIMINATED), jnp.float32),
        ),
        in_specs=[pl.BlockSpec(memory_space=pltpu.SMEM)] + [vmem] * 5,
        out_specs=(vmem, vmem, vmem),
        scratch_shapes=[
            pltpu.VMEM((ELIMINATED, ELIMINATED), jnp.float32),
            pltpu.VMEM((ELIMINATED, BLK), jnp.float32),
            pltpu.VMEM((4, BLK, PACKED), jnp.float32),
            pltpu.VMEM((BLK, ELIMINATED), jnp.bfloat16),
            pltpu.VMEM((BLK, ELIMINATED), jnp.bfloat16),
        ],
        compiler_params=pltpu.CompilerParams(vmem_limit_bytes=VMEM_BYTES),
        cost_estimate=LIGHT,
    )(turn, piece, before, after, across, across_rest)


def solve_kernel(high_ref, low_ref, sums_ref, out_ref):
    parts, quarter, _ = out_ref.shape
    sums = halves(sums_ref[0])
    for i in range(parts):
        rows, depth = slice(quarter * i, quarter * (i + 1)), quarter * (i + 1)
        out_ref[i] = sharp_dot(
            (high_ref[rows, :depth], low_ref[rows, :depth]), tuple(x[:depth] for x in sums), PLAIN
        )


def solve(high, low, sums):
    vmem = pl.BlockSpec(memory_space=pltpu.VMEM)
    return pl.pallas_call(
        solve_kernel,
        out_shape=jax.ShapeDtypeStruct((4, ELIMINATED // 4, sums.shape[2]), jnp.float32),
        in_specs=[vmem] * 3,
        out_specs=vmem,
        compiler_params=pltpu.CompilerParams(vmem_limit_bytes=VMEM_BYTES),
        cost_estimate=LIGHT,
    )(high, low, sums)


def join_kernel(col_ref, leading_ref, first_ref, second_ref, out_ref):
    parts, _, width = second_ref.shape
    for half in range(2):
        for j in range(parts):
            cols = slice(ELIMINATED // 2 * half + BLK * j, ELIMINATED // 2 * half + BLK * (j + 1))
            out_ref[0, :, cols] = jnp.where(
                col_ref[0, 0] == 0, leading_ref[:, cols], first_ref[j, :, BLK * half : BLK * (half + 1)]
            )
    for j in range(parts):
        out_ref[0, :, ELIMINATED + width * j : ELIMINATED + width * (j + 1)] = second_ref[j]


def join(col, leading, first, second):
    vmem = pl.BlockSpec(memory_space=pltpu.VMEM)
    return pl.pallas_call(
        join_kernel,
        out_shape=jax.ShapeDtypeStruct((1, leading.shape[0], 2 * ELIMINATED), jnp.float32),
        in_specs=[pl.BlockSpec(memory_space=pltpu.SMEM)] + [vmem] * 3,
        out_specs=vmem,
        compiler_params=pltpu.CompilerParams(vmem_limit_bytes=VMEM_BYTES),
        cost_estimate=LIGHT,
    )(col, leading, first, second)


def shifted(x, shift, count):
    return lax.ppermute(x, "row", [(i, (i + shift) % count) for i in range(count)])


def body(own_rows, child_rows, child_dest, child_stair):
    n_front = lax.axis_size("front")
    row_count = lax.axis_size("row")
    source_rows, half_cols = child_rows.shape
    capacity = max(2, 2 * source_rows // n_front)
    col_index = lax.axis_index("col")
    row_index = lax.axis_index("row")
    quarter = ELIMINATED // row_count
    own = own_rows[0]
    own_a = own[:, :ELIMINATED]
    split = own_a.shape[0] // 4
    passed = lax.ppermute(own_a[:split], "col", [(0, 1), (1, 0)])
    passed_rest = lax.ppermute(own_a[split:], "col", [(0, 1), (1, 0)])

    first_col = col_index * half_cols
    dest, stair = child_dest.reshape(1, source_rows), child_stair.reshape(source_rows, 1)
    doubled = place(first_col, dest, stair, child_rows, 0, 2, n_front, capacity)
    single = place(first_col, dest, stair, child_rows, ELIMINATED, 1, n_front, capacity)
    doubled, passed = lax.optimization_barrier((doubled, passed))
    arrived = lax.all_to_all(
        doubled.reshape(2 * n_front * capacity, ELIMINATED),
        ("front", "col"),
        split_axis=0,
        concat_axis=0,
        tiled=True,
    ).reshape(n_front, 2, capacity, ELIMINATED)
    passed = jnp.concatenate([passed, passed_rest], axis=0)
    own_panel = jnp.where(col_index == 0, own_a, passed)
    own_shared = jnp.where(
        col_index == 0, passed[:, : ELIMINATED // 2], own_a[:, ELIMINATED // 2 :]
    )

    own_panel, single = lax.optimization_barrier((own_panel, single))
    child_b = lax.all_to_all(
        single.reshape(n_front * capacity, ELIMINATED), "front", split_axis=0, concat_axis=0, tiled=True
    ).reshape(n_front, 1, capacity, ELIMINATED)
    turn = row_index.reshape(1, 1)
    mine, right, left, right_rest, left_rest, turned = packed_gram(turn, own_panel, arrived)
    products_a = shared_cross(col_index.reshape(1), turned, own_shared, arrived)
    mine, right, left, products_a = lax.optimization_barrier((mine, right, left, products_a))
    middle = BLK // 2
    from_left, from_right = shifted(right, 1, row_count), shifted(left, -1, row_count)
    rest_left = shifted(right_rest + from_left[:middle], 1, row_count)
    rest_right = shifted(left_rest + from_right[:middle], -1, row_count)
    piece = mine + jnp.concatenate(
        [rest_left + from_right[middle:], from_left[middle:] + rest_right], axis=0
    )
    before, after = shifted(piece, 1, row_count), shifted(piece, -1, row_count)
    across, across_rest = shifted(before[:middle], 1, row_count), shifted(after[middle:], -1, row_count)
    pieces = (piece, before, after, across, across_rest)

    def summed(products):
        return lax.psum_scatter(products, "row", scatter_dimension=0, tiled=True)

    products_b = cross(turned, own, ELIMINATED, child_b, 0)
    pieces, products_b = lax.optimization_barrier((pieces, products_b))
    inverse_high, inverse_low, leading = factor(turn, *pieces)
    first = solve(inverse_high, inverse_low, summed(products_a))
    handed = lax.ppermute(first, "col", [(0, 1)])
    second = solve(inverse_high, inverse_low, summed(products_b))
    handed, later = lax.optimization_barrier((handed, second))
    second = lax.all_to_all(later, "row", split_axis=0, concat_axis=0, tiled=True)
    first = jnp.concatenate([handed, first], axis=2)
    first = lax.all_to_all(first, "row", split_axis=0, concat_axis=0, tiled=True)
    return join(col_index.reshape(1, 1), leading, first, second)


def solution(mesh):
    placed = (
        P("front", "row", "col"),
        P(("front", "row"), "col"),
        P(("front", "row"), None),
        P(("front", "row")),
    )
    return jax.shard_map(
        body, mesh=mesh, in_specs=placed, out_specs=P("front", "row", "col"), check_vma=False
    )
```

```python
import jax
import jax.numpy as jnp
from jax import lax
from jax.experimental import pallas as pl
from jax.experimental.pallas import tpu as pltpu
from jax.sharding import PartitionSpec as P

ELIMINATED = 1024
STAIR_BLK = 128
BLK = 128
STEPS = ELIMINATED // BLK
LINES = 8
VMEM_BYTES = 60 * 2**20
LIGHT = pl.CostEstimate(flops=1, bytes_accessed=1, transcendentals=0)


def lower_inverse(diag_block, beside):
    lane = lax.broadcasted_iota(jnp.int32, (LINES, BLK), 1)
    sublane = lax.broadcasted_iota(jnp.int32, (LINES, BLK), 0)
    count = BLK // LINES
    strips = [diag_block[LINES * i : LINES * (i + 1), :] for i in range(count)]
    for b in range(count):
        first = LINES * b
        within = (lane >= first) & (lane < first + LINES)
        strip = strips[b]
        column = [
            jnp.broadcast_to(strip[:, first + t : first + t + 1], (LINES, BLK))
            for t in range(LINES)
        ]
        entry = [
            [jnp.broadcast_to(column[t][i : i + 1, :], (LINES, BLK)) for t in range(i + 1)]
            for i in range(LINES)
        ]
        scale = []
        for t in range(LINES):
            scale.append(lax.rsqrt(entry[t][t]))
            for i in range(t + 1, LINES):
                entry[i][t] = entry[i][t] * scale[t]
            for u in range(t + 1, LINES):
                for i in range(u, LINES):
                    entry[i][u] = entry[i][u] - entry[i][t] * entry[u][t]
        solved = []
        augmented = jnp.where(within, jnp.where(lane == sublane + first, 1.0, 0.0), strip)
        for t in range(LINES):
            line = jnp.broadcast_to(augmented[t : t + 1, :], (LINES, BLK))
            for s in range(t):
                line = line - entry[t][s] * solved[s]
            solved.append(line * scale[t])
        merged = solved[0]
        for t in range(1, LINES):
            merged = jnp.where(sublane == t, solved[t], merged)
        strips[b] = merged
        beside(b, count)
        for i in range(b + 1, count):
            below = strips[i]
            rest = jnp.where(within, 0.0, below)
            factors = []
            for t in range(LINES):
                value = jnp.broadcast_to(below[:, first + t : first + t + 1], (LINES, BLK))
                for s in range(t):
                    value = value - entry[t][s] * factors[s]
                value = value * scale[t]
                factors.append(value)
                rest = rest - value * solved[t]
            strips[i] = rest
    row = lax.broadcasted_iota(jnp.int32, (BLK, BLK), 0)
    col = lax.broadcasted_iota(jnp.int32, (BLK, BLK), 1)
    return jnp.where(row >= col, jnp.concatenate(strips, axis=0), 0.0)


PAIRS = ((0, 3), (1, 2))
WIDE = 256
PACKED = ELIMINATED + WIDE


def offsets():
    found = []
    for pair, (long, short) in enumerate(PAIRS):
        found.append((long, pair, 0))
        found.append((short, pair, ELIMINATED - WIDE * long))
    return found


def halves(x):
    high = x.astype(jnp.bfloat16)
    return high, (x - high.astype(jnp.float32)).astype(jnp.bfloat16)


def place_kernel(first_ref, dest_ref, stair_ref, rows_ref, out_ref, select_ref):
    fronts, copies, capacity, width = out_ref.shape
    slots, sources = select_ref.shape
    chunk = pl.program_id(0)

    @pl.when(chunk == 0)
    def _():
        dest = dest_ref[...]
        named = lax.broadcasted_iota(jnp.int32, (fronts, sources), 0) == dest
        source = lax.broadcasted_iota(jnp.int32, (sources, sources), 0)
        later = lax.broadcasted_iota(jnp.int32, (sources, sources), 1)
        before = jnp.dot(
            named.astype(jnp.float32).astype(jnp.bfloat16),
            (source < later).astype(jnp.float32).astype(jnp.bfloat16),
            preferred_element_type=jnp.float32,
        )
        slot = jnp.sum(jnp.where(named, before, 0.0), axis=0, keepdims=True).astype(jnp.int32)
        position = dest * capacity + slot
        line = lax.broadcasted_iota(jnp.int32, (slots, sources), 0)
        select_ref[...] = (line == position).astype(jnp.float32).astype(jnp.bfloat16)

    cols = (
        first_ref[0, 0] + chunk * width + lax.broadcasted_iota(jnp.int32, (sources, width), 1)
    )
    high, low = halves(jnp.where(cols >= stair_ref[...] * STAIR_BLK, rows_ref[...], 0.0))
    select = select_ref[...]
    placed = jnp.dot(select, high, preferred_element_type=jnp.float32) + jnp.dot(
        select, low, preferred_element_type=jnp.float32
    )
    placed = placed.reshape(fronts, capacity, width)
    for copy in range(copies):
        out_ref[:, copy] = placed


def place(first_col, dest, stair, rows, start, copies, n_front, capacity):
    sources = rows.shape[0]
    skipped = start // WIDE
    return pl.pallas_call(
        place_kernel,
        grid=(ELIMINATED // WIDE,),
        out_shape=jax.ShapeDtypeStruct((n_front, copies, capacity, ELIMINATED), jnp.float32),
        in_specs=[
            pl.BlockSpec(memory_space=pltpu.SMEM),
            pl.BlockSpec((1, sources), lambda j: (0, 0)),
            pl.BlockSpec((sources, 1), lambda j: (0, 0)),
            pl.BlockSpec((sources, WIDE), lambda j: (0, skipped + j)),
        ],
        out_specs=pl.BlockSpec((n_front, copies, capacity, WIDE), lambda j: (0, 0, 0, j)),
        scratch_shapes=[pltpu.VMEM((n_front * capacity, sources), jnp.bfloat16)],
        compiler_params=pltpu.CompilerParams(vmem_limit_bytes=VMEM_BYTES),
        cost_estimate=LIGHT,
    )((first_col + start).reshape(1, 1), dest, stair, rows)


def stacked_halves(out_ref, *parts):
    count = out_ref.shape[0] // 2
    first = 0
    for x in parts:
        rows = x.shape[0]
        high, low = halves(x)
        out_ref[first : first + rows] = low
        out_ref[count + first : count + first + rows] = high
        first += rows


def turned_dot(turned, other):
    count = other.shape[0] // 2
    return jnp.dot(turned, other, preferred_element_type=jnp.float32) + jnp.dot(
        turned[:, :count], other[count:], preferred_element_type=jnp.float32
    )


def gram_kernel(turn_ref, own_ref, child_ref, *outs):
    turned_ref, both_ref, packed_ref = outs[5:]
    count = both_ref.shape[0] // 2
    stacked_halves(both_ref, own_ref[...], child_ref[:, 0].reshape(-1, ELIMINATED))
    for start in range(0, ELIMINATED, WIDE):
        cols = slice(start, start + WIDE)
        turned_ref[cols, :count] = both_ref[count:, cols].T
        turned_ref[cols, count:] = both_ref[:count, cols].T
    for block, pair, offset in offsets():
        start = WIDE * block
        total = turned_dot(turned_ref[start : start + WIDE, :], both_ref[:, start:])
        for half in range(2):
            packed_ref[2 * pair + half, :, offset : offset + ELIMINATED - start] = total[
                BLK * half : BLK * (half + 1)
            ]
    mine_ref, right_ref, left_ref, right_rest_ref, left_rest_ref, *_ = outs
    turn = turn_ref[0, 0]
    here, right, over, left = [lax.rem(turn + s, 4) for s in range(4)]
    middle = BLK // 2
    mine_ref[...] = packed_ref[here]
    right_ref[:middle], right_ref[middle:] = packed_ref[over, :middle], packed_ref[right, middle:]
    left_ref[:middle], left_ref[middle:] = packed_ref[over, middle:], packed_ref[left, :middle]
    right_rest_ref[...] = packed_ref[right, :middle]
    left_rest_ref[...] = packed_ref[left, middle:]


def packed_gram(turn, own_panel, arrived):
    fronts, _, capacity, _ = arrived.shape
    rows = own_panel.shape[0] + fronts * capacity
    vmem = pl.BlockSpec(memory_space=pltpu.VMEM)
    return pl.pallas_call(
        gram_kernel,
        grid=(1,),
        out_shape=[jax.ShapeDtypeStruct((BLK, PACKED), jnp.float32)] * 3
        + [jax.ShapeDtypeStruct((BLK // 2, PACKED), jnp.float32)] * 2
        + [jax.ShapeDtypeStruct((ELIMINATED, 2 * rows), jnp.bfloat16)],
        in_specs=[
            pl.BlockSpec(memory_space=pltpu.SMEM),
            vmem,
            pl.BlockSpec((fronts, 1, capacity, ELIMINATED), lambda j: (0, 0, 0, 0)),
        ],
        out_specs=[vmem] * 6,
        scratch_shapes=[pltpu.VMEM((2 * rows, ELIMINATED), jnp.bfloat16), pltpu.VMEM((4, BLK, PACKED), jnp.float32)],
        compiler_params=pltpu.CompilerParams(vmem_limit_bytes=VMEM_BYTES),
        cost_estimate=LIGHT,
    )(turn, own_panel, arrived)


def cross_kernel(turned_ref, own_ref, child_ref, out_ref, both_ref):
    stacked_halves(both_ref, own_ref[...], child_ref[:, 0].reshape(-1, WIDE))
    out_ref[0] = turned_dot(turned_ref[...], both_ref[...])


def cross(turned, own, start, child, part):
    fronts, _, capacity, _ = child.shape
    skipped = start // WIDE
    return pl.pallas_call(
        cross_kernel,
        grid=(ELIMINATED // WIDE,),
        out_shape=jax.ShapeDtypeStruct((ELIMINATED // WIDE, ELIMINATED, WIDE), jnp.float32),
        in_specs=[
            pl.BlockSpec(memory_space=pltpu.VMEM),
            pl.BlockSpec((own.shape[0], WIDE), lambda j: (0, skipped + j)),
            pl.BlockSpec((fronts, 1, capacity, WIDE), lambda j: (0, part, 0, j)),
        ],
        out_specs=pl.BlockSpec((1, ELIMINATED, WIDE), lambda j: (j, 0, 0)),
        scratch_shapes=[pltpu.VMEM((turned.shape[1], WIDE), jnp.bfloat16)],
        compiler_params=pltpu.CompilerParams(vmem_limit_bytes=VMEM_BYTES),
        cost_estimate=LIGHT,
    )(turned, own, child)


def shared_kernel(_, turned_ref, own_ref, child_ref, out_ref, both_ref):
    stacked_halves(both_ref, own_ref[...], child_ref[:, 0].reshape(-1, WIDE))
    total = turned_dot(turned_ref[...], both_ref[...])
    for half in range(2):
        out_ref[half] = total[:, BLK * half : BLK * (half + 1)]


def shared_cross(col, turned, own, child):
    fronts, _, capacity, _ = child.shape
    steps = own.shape[1] // WIDE
    return pl.pallas_call(
        shared_kernel,
        grid_spec=pltpu.PrefetchScalarGridSpec(
            num_scalar_prefetch=1,
            grid=(steps,),
            in_specs=[
                pl.BlockSpec(memory_space=pltpu.VMEM),
                pl.BlockSpec((own.shape[0], WIDE), lambda j, c: (0, j)),
                pl.BlockSpec((fronts, 1, capacity, WIDE), lambda j, c: (0, 1, 0, c[0] * steps + j)),
            ],
            out_specs=pl.BlockSpec((2, ELIMINATED, BLK), lambda j, c: (j, 0, 0)),
            scratch_shapes=[pltpu.VMEM((turned.shape[1], WIDE), jnp.bfloat16)],
        ),
        out_shape=jax.ShapeDtypeStruct((own.shape[1] // BLK, ELIMINATED, BLK), jnp.float32),
        compiler_params=pltpu.CompilerParams(vmem_limit_bytes=VMEM_BYTES),
        cost_estimate=LIGHT,
    )(col, turned, own, child)


def sharp_dot(a, b, dims):
    (high, low), (other_high, other_low) = a, b
    dims = (dims, ((), ()))
    total = lax.dot_general(high, other_high, dims, preferred_element_type=jnp.float32)
    total += lax.dot_general(high, other_low, dims, preferred_element_type=jnp.float32)
    return total + lax.dot_general(low, other_high, dims, preferred_element_type=jnp.float32)


PLAIN = ((1,), (0,))


def factor_kernel(
    turn_ref, piece_ref, before_ref, after_ref, across_ref, across_rest_ref, sums_ref,
    high_ref, low_ref, leading_ref, solved_ref,
    work_ref, diag_ref, packed_ref, panel_high_ref, panel_low_ref, found_ref,
):
    turn = turn_ref[0, 0]
    middle = BLK // 2
    packed_ref[turn] = piece_ref[...]
    packed_ref[lax.rem(turn + 1, 4)] = after_ref[...]
    packed_ref[lax.rem(turn + 3, 4)] = before_ref[...]
    packed_ref[lax.rem(turn + 2, 4), :middle] = across_ref[...]
    packed_ref[lax.rem(turn + 2, 4), middle:] = across_rest_ref[...]
    work_ref[...] = jnp.zeros_like(work_ref)
    panel_high_ref[...] = jnp.zeros_like(panel_high_ref)
    panel_low_ref[...] = jnp.zeros_like(panel_low_ref)
    for block, pair, offset in offsets():
        start = WIDE * block
        for half in range(2):
            work_ref[start + BLK * half : start + BLK * (half + 1), start:] = packed_ref[
                2 * pair + half, :, offset : offset + ELIMINATED - start
            ]
    row = lax.broadcasted_iota(jnp.int32, (BLK, BLK), 0)
    col = lax.broadcasted_iota(jnp.int32, (BLK, BLK), 1)
    place_of = lax.broadcasted_iota(jnp.int32, (BLK, ELIMINATED), 1) // BLK
    chunk_of = lax.broadcasted_iota(jnp.int32, (BLK, WIDE), 1) // BLK
    deferred = [(i, c) for i in range(2, STEPS) for c in range(ELIMINATED // WIDE)]

    sums = halves(sums_ref[0])

    def solve_rows(k):
        rows = pl.ds(pl.multiple_of(k * BLK, BLK), BLK)
        found_ref[rows, :] = sharp_dot((high_ref[rows, :], low_ref[rows, :]), sums, PLAIN)

    def step(k, _):
        here = pl.ds(pl.multiple_of(k * BLK, BLK), BLK)
        block = work_ref[here, here]
        turned = {}

        def update(i, c):
            below = i > k
            rows, cols = slice(BLK * i, BLK * (i + 1)), slice(WIDE * c, WIDE * (c + 1))
            if i not in turned:
                kept = jnp.where(below, 1.0, 0.0)
                turned[i] = [
                    (ref[:, rows].astype(jnp.float32) * kept).T.astype(jnp.bfloat16)
                    for ref in (panel_high_ref, panel_low_ref)
                ]
            panel = (panel_high_ref[:, cols], panel_low_ref[:, cols])
            cleared = jnp.where(below, k - 1 - c * (WIDE // BLK), -1)
            old = jnp.where(chunk_of == cleared, 0.0, work_ref[rows, cols])
            work_ref[rows, cols] = old - sharp_dot(turned[i], panel, PLAIN)

        def beside(b, count):
            for i, c in deferred[len(deferred) * b // count : len(deferred) * (b + 1) // count]:
                update(i, c)

        solve_rows(jnp.maximum(k - 1, 0))
        inverse = lower_inverse(block, beside)
        rows = sharp_dot(halves(inverse), halves(work_ref[here, :]), PLAIN)
        work_ref[here, :] = rows
        diag_ref[here, :] = jnp.where(row <= col, work_ref[here, here], 0.0)
        work_ref[here, here] = inverse
        rows = work_ref[here, :]
        panel_high_ref[...], panel_low_ref[...] = halves(rows)
        high_ref[here, :], low_ref[here, :] = halves(jnp.where(place_of <= k, rows, 0.0))

        @pl.when(k < STEPS - 1)
        def _():
            there = pl.ds(pl.multiple_of((k + 1) * BLK, BLK), BLK)
            left = [ref[:, there].astype(jnp.float32).T.astype(jnp.bfloat16) for ref in (panel_high_ref, panel_low_ref)]
            old = jnp.where(place_of == k, 0.0, work_ref[there, :])
            work_ref[there, :] = old - sharp_dot(left, (panel_high_ref[...], panel_low_ref[...]), PLAIN)

        return 0

    lax.fori_loop(0, STEPS, step, 0)
    taken = leading_ref.shape[0] // BLK
    for b in range(taken):
        block = turn * taken + b
        here = pl.ds(pl.multiple_of(block * BLK, BLK), BLK)
        diag = jnp.concatenate([diag_ref[here, :]] * STEPS, axis=1)
        leading_ref[BLK * b : BLK * (b + 1), :] = jnp.where(
            place_of > block, work_ref[here, :], jnp.where(place_of == block, diag, 0.0)
        )
    solve_rows(STEPS - 1)
    parts, copies, quarter, _ = solved_ref.shape
    for i in range(parts):
        for copy in range(copies):
            solved_ref[i, copy] = found_ref[quarter * i : quarter * (i + 1), :]


def factor(turn, piece, before, after, across, across_rest, sums):
    vmem = pl.BlockSpec(memory_space=pltpu.VMEM)
    return pl.pallas_call(
        factor_kernel,
        out_shape=(
            jax.ShapeDtypeStruct((ELIMINATED, ELIMINATED), jnp.bfloat16),
            jax.ShapeDtypeStruct((ELIMINATED, ELIMINATED), jnp.bfloat16),
            jax.ShapeDtypeStruct((ELIMINATED // 4, ELIMINATED), jnp.float32),
            jax.ShapeDtypeStruct((4, 2, ELIMINATED // 4, BLK), jnp.float32),
        ),
        in_specs=[pl.BlockSpec(memory_space=pltpu.SMEM)] + [vmem] * 6,
        out_specs=(vmem, vmem, vmem, vmem),
        scratch_shapes=[
            pltpu.VMEM((ELIMINATED, ELIMINATED), jnp.float32),
            pltpu.VMEM((ELIMINATED, BLK), jnp.float32),
            pltpu.VMEM((4, BLK, PACKED), jnp.float32),
            pltpu.VMEM((BLK, ELIMINATED), jnp.bfloat16),
            pltpu.VMEM((BLK, ELIMINATED), jnp.bfloat16),
            pltpu.VMEM((ELIMINATED, BLK), jnp.float32),
        ],
        compiler_params=pltpu.CompilerParams(vmem_limit_bytes=VMEM_BYTES),
        cost_estimate=LIGHT,
    )(turn, piece, before, after, across, across_rest, sums)


def solve_kernel(high_ref, low_ref, sums_ref, out_ref):
    parts, quarter, _ = out_ref.shape
    sums = halves(sums_ref[0])
    for i in range(parts):
        rows, depth = slice(quarter * i, quarter * (i + 1)), quarter * (i + 1)
        out_ref[i] = sharp_dot(
            (high_ref[rows, :depth], low_ref[rows, :depth]), tuple(x[:depth] for x in sums), PLAIN
        )


def solve(high, low, sums):
    vmem = pl.BlockSpec(memory_space=pltpu.VMEM)
    return pl.pallas_call(
        solve_kernel,
        out_shape=jax.ShapeDtypeStruct((4, ELIMINATED // 4, sums.shape[2]), jnp.float32),
        in_specs=[vmem] * 3,
        out_specs=vmem,
        compiler_params=pltpu.CompilerParams(vmem_limit_bytes=VMEM_BYTES),
        cost_estimate=LIGHT,
    )(high, low, sums)


def join_kernel(col_ref, leading_ref, first_ref, second_ref, out_ref):
    parts, _, width = second_ref.shape
    for j in range(parts):
        for half in range(2):
            start = ELIMINATED // 2 * half + BLK * j
            cols = slice(start, start + BLK)
            out_ref[0, :, cols] = jnp.where(
                col_ref[0, 0] == 0, leading_ref[:, cols], first_ref[j, half]
            )
    for j in range(parts):
        out_ref[0, :, ELIMINATED + width * j : ELIMINATED + width * (j + 1)] = second_ref[j]


def join(col, leading, first, second):
    vmem = pl.BlockSpec(memory_space=pltpu.VMEM)
    return pl.pallas_call(
        join_kernel,
        out_shape=jax.ShapeDtypeStruct((1, leading.shape[0], 2 * ELIMINATED), jnp.float32),
        in_specs=[pl.BlockSpec(memory_space=pltpu.SMEM)] + [vmem] * 3,
        out_specs=vmem,
        compiler_params=pltpu.CompilerParams(vmem_limit_bytes=VMEM_BYTES),
        cost_estimate=LIGHT,
    )(col, leading, first, second)


def shifted(x, shift, count):
    return lax.ppermute(x, "row", [(i, (i + shift) % count) for i in range(count)])


def body(own_rows, child_rows, child_dest, child_stair):
    n_front = lax.axis_size("front")
    row_count = lax.axis_size("row")
    source_rows, half_cols = child_rows.shape
    capacity = max(2, 2 * source_rows // n_front)
    col_index = lax.axis_index("col")
    row_index = lax.axis_index("row")
    quarter = ELIMINATED // row_count
    own = own_rows[0]
    own_a = own[:, :ELIMINATED]
    split = own_a.shape[0] // 4
    passed = lax.ppermute(own_a[:split], "col", [(0, 1), (1, 0)])
    passed_rest = lax.ppermute(own_a[split:], "col", [(0, 1), (1, 0)])

    first_col = col_index * half_cols
    dest, stair = child_dest.reshape(1, source_rows), child_stair.reshape(source_rows, 1)
    doubled = place(first_col, dest, stair, child_rows, 0, 2, n_front, capacity)
    single = place(first_col, dest, stair, child_rows, ELIMINATED, 1, n_front, capacity)
    doubled, passed = lax.optimization_barrier((doubled, passed))
    arrived = lax.all_to_all(
        doubled.reshape(2 * n_front * capacity, ELIMINATED),
        ("front", "col"),
        split_axis=0,
        concat_axis=0,
        tiled=True,
    ).reshape(n_front, 2, capacity, ELIMINATED)
    passed = jnp.concatenate([passed, passed_rest], axis=0)
    own_panel = jnp.where(col_index == 0, own_a, passed)
    own_shared = jnp.where(
        col_index == 0, passed[:, : ELIMINATED // 2], own_a[:, ELIMINATED // 2 :]
    )

    own_panel, single = lax.optimization_barrier((own_panel, single))
    child_b = lax.all_to_all(
        single.reshape(n_front * capacity, ELIMINATED), "front", split_axis=0, concat_axis=0, tiled=True
    ).reshape(n_front, 1, capacity, ELIMINATED)
    turn = row_index.reshape(1, 1)
    mine, right, left, right_rest, left_rest, turned = packed_gram(turn, own_panel, arrived)
    products_a = shared_cross(col_index.reshape(1), turned, own_shared, arrived)
    middle = BLK // 2
    from_left, from_right = shifted(right, 1, row_count), shifted(left, -1, row_count)
    rest_left = shifted(right_rest + from_left[:middle], 1, row_count)
    rest_right = shifted(left_rest + from_right[:middle], -1, row_count)
    piece = mine + jnp.concatenate(
        [rest_left + from_right[middle:], from_left[middle:] + rest_right], axis=0
    )
    piece, child_b = lax.optimization_barrier((piece, child_b))
    before, after = shifted(piece, 1, row_count), shifted(piece, -1, row_count)
    across, across_rest = shifted(before[:middle], 1, row_count), shifted(after[middle:], -1, row_count)
    pieces = (piece, before, after, across, across_rest)

    def summed(products):
        return lax.psum_scatter(products, "row", scatter_dimension=0, tiled=True)

    products_b = cross(turned, own, ELIMINATED, child_b, 0)
    pieces, products_b = lax.optimization_barrier((pieces, products_b))
    inverse_high, inverse_low, leading, first = factor(turn, *pieces, summed(products_a))
    first = lax.all_to_all(
        first.reshape(2 * row_count, quarter, BLK), ("row", "col"), split_axis=0, concat_axis=0, tiled=True
    ).reshape(row_count, 2, quarter, BLK)
    second = solve(inverse_high, inverse_low, summed(products_b))
    second = lax.all_to_all(second, "row", split_axis=0, concat_axis=0, tiled=True)
    return join(col_index.reshape(1, 1), leading, first, second)


def solution(mesh):
    placed = (
        P("front", "row", "col"),
        P(("front", "row"), "col"),
        P(("front", "row"), None),
        P(("front", "row")),
    )
    return jax.shard_map(
        body, mesh=mesh, in_specs=placed, out_specs=P("front", "row", "col"), check_vma=False
    )
```

```python
import jax
import jax.numpy as jnp
from jax import lax
from jax.experimental import pallas as pl
from jax.experimental.pallas import tpu as pltpu
from jax.sharding import PartitionSpec as P

ELIMINATED = 1024
STAIR_BLK = 128
BLK = 128
STEPS = ELIMINATED // BLK
LINES = 8
VMEM_BYTES = 60 * 2**20
LIGHT = pl.CostEstimate(flops=1, bytes_accessed=1, transcendentals=0)


def lower_inverse(diag_block, beside):
    lane = lax.broadcasted_iota(jnp.int32, (LINES, BLK), 1)
    sublane = lax.broadcasted_iota(jnp.int32, (LINES, BLK), 0)
    count = BLK // LINES
    strips = [diag_block[LINES * i : LINES * (i + 1), :] for i in range(count)]
    for b in range(count):
        first = LINES * b
        within = (lane >= first) & (lane < first + LINES)
        strip = strips[b]
        column = [
            jnp.broadcast_to(strip[:, first + t : first + t + 1], (LINES, BLK))
            for t in range(LINES)
        ]
        entry = [
            [jnp.broadcast_to(column[t][i : i + 1, :], (LINES, BLK)) for t in range(i + 1)]
            for i in range(LINES)
        ]
        scale = []
        for t in range(LINES):
            scale.append(lax.rsqrt(entry[t][t]))
            for i in range(t + 1, LINES):
                entry[i][t] = entry[i][t] * scale[t]
            for u in range(t + 1, LINES):
                for i in range(u, LINES):
                    entry[i][u] = entry[i][u] - entry[i][t] * entry[u][t]
        solved = []
        augmented = jnp.where(within, jnp.where(lane == sublane + first, 1.0, 0.0), strip)
        for t in range(LINES):
            line = jnp.broadcast_to(augmented[t : t + 1, :], (LINES, BLK))
            for s in range(t):
                line = line - entry[t][s] * solved[s]
            solved.append(line * scale[t])
        merged = solved[0]
        for t in range(1, LINES):
            merged = jnp.where(sublane == t, solved[t], merged)
        strips[b] = merged
        beside(b, count)
        for i in range(b + 1, count):
            below = strips[i]
            rest = jnp.where(within, 0.0, below)
            factors = []
            for t in range(LINES):
                value = jnp.broadcast_to(below[:, first + t : first + t + 1], (LINES, BLK))
                for s in range(t):
                    value = value - entry[t][s] * factors[s]
                value = value * scale[t]
                factors.append(value)
                rest = rest - value * solved[t]
            strips[i] = rest
    row = lax.broadcasted_iota(jnp.int32, (BLK, BLK), 0)
    col = lax.broadcasted_iota(jnp.int32, (BLK, BLK), 1)
    return jnp.where(row >= col, jnp.concatenate(strips, axis=0), 0.0)


PAIRS = ((0, 3), (1, 2))
WIDE = 256
PACKED = ELIMINATED + WIDE


def offsets():
    found = []
    for pair, (long, short) in enumerate(PAIRS):
        found.append((long, pair, 0))
        found.append((short, pair, ELIMINATED - WIDE * long))
    return found


def halves(x):
    high = x.astype(jnp.bfloat16)
    return high, (x - high.astype(jnp.float32)).astype(jnp.bfloat16)


def place_kernel(first_ref, dest_ref, stair_ref, rows_ref, out_ref, select_ref):
    fronts, copies, capacity, width = out_ref.shape
    slots, sources = select_ref.shape
    chunk = pl.program_id(0)

    @pl.when(chunk == 0)
    def _():
        dest = dest_ref[...]
        named = lax.broadcasted_iota(jnp.int32, (fronts, sources), 0) == dest
        source = lax.broadcasted_iota(jnp.int32, (sources, sources), 0)
        later = lax.broadcasted_iota(jnp.int32, (sources, sources), 1)
        before = jnp.dot(
            named.astype(jnp.float32).astype(jnp.bfloat16),
            (source < later).astype(jnp.float32).astype(jnp.bfloat16),
            preferred_element_type=jnp.float32,
        )
        slot = jnp.sum(jnp.where(named, before, 0.0), axis=0, keepdims=True).astype(jnp.int32)
        position = dest * capacity + slot
        line = lax.broadcasted_iota(jnp.int32, (slots, sources), 0)
        select_ref[...] = (line == position).astype(jnp.float32).astype(jnp.bfloat16)

    cols = (
        first_ref[0, 0] + chunk * width + lax.broadcasted_iota(jnp.int32, (sources, width), 1)
    )
    high, low = halves(jnp.where(cols >= stair_ref[...] * STAIR_BLK, rows_ref[...], 0.0))
    select = select_ref[...]
    placed = jnp.dot(select, high, preferred_element_type=jnp.float32) + jnp.dot(
        select, low, preferred_element_type=jnp.float32
    )
    placed = placed.reshape(fronts, capacity, width)
    for copy in range(copies):
        out_ref[:, copy] = placed


def place(first_col, dest, stair, rows, start, copies, n_front, capacity):
    sources = rows.shape[0]
    skipped = start // WIDE
    return pl.pallas_call(
        place_kernel,
        grid=(ELIMINATED // WIDE,),
        out_shape=jax.ShapeDtypeStruct((n_front, copies, capacity, ELIMINATED), jnp.float32),
        in_specs=[
            pl.BlockSpec(memory_space=pltpu.SMEM),
            pl.BlockSpec((1, sources), lambda j: (0, 0)),
            pl.BlockSpec((sources, 1), lambda j: (0, 0)),
            pl.BlockSpec((sources, WIDE), lambda j: (0, skipped + j)),
        ],
        out_specs=pl.BlockSpec((n_front, copies, capacity, WIDE), lambda j: (0, 0, 0, j)),
        scratch_shapes=[pltpu.VMEM((n_front * capacity, sources), jnp.bfloat16)],
        compiler_params=pltpu.CompilerParams(vmem_limit_bytes=VMEM_BYTES),
        cost_estimate=LIGHT,
    )((first_col + start).reshape(1, 1), dest, stair, rows)


def stacked_halves(out_ref, *parts):
    count = out_ref.shape[0] // 2
    first = 0
    for x in parts:
        rows = x.shape[0]
        high, low = halves(x)
        out_ref[first : first + rows] = low
        out_ref[count + first : count + first + rows] = high
        first += rows


def turned_dot(turned, other):
    count = other.shape[0] // 2
    return jnp.dot(turned, other, preferred_element_type=jnp.float32) + jnp.dot(
        turned[:, :count], other[count:], preferred_element_type=jnp.float32
    )


def gram_kernel(turn_ref, own_ref, child_ref, *outs):
    turned_ref, both_ref, packed_ref = outs[5:]
    count = both_ref.shape[0] // 2
    stacked_halves(both_ref, own_ref[...], child_ref[:, 0].reshape(-1, ELIMINATED))
    for start in range(0, ELIMINATED, WIDE):
        cols = slice(start, start + WIDE)
        turned_ref[cols, :count] = both_ref[count:, cols].T
        turned_ref[cols, count:] = both_ref[:count, cols].T
    for block, pair, offset in offsets():
        start = WIDE * block
        total = turned_dot(turned_ref[start : start + WIDE, :], both_ref[:, start:])
        for half in range(2):
            packed_ref[2 * pair + half, :, offset : offset + ELIMINATED - start] = total[
                BLK * half : BLK * (half + 1)
            ]
    mine_ref, right_ref, left_ref, right_rest_ref, left_rest_ref, *_ = outs
    turn = turn_ref[0, 0]
    here, right, over, left = [lax.rem(turn + s, 4) for s in range(4)]
    middle = BLK // 2
    mine_ref[...] = packed_ref[here]
    right_ref[:middle], right_ref[middle:] = packed_ref[over, :middle], packed_ref[right, middle:]
    left_ref[:middle], left_ref[middle:] = packed_ref[over, middle:], packed_ref[left, :middle]
    right_rest_ref[...] = packed_ref[right, :middle]
    left_rest_ref[...] = packed_ref[left, middle:]


def packed_gram(turn, own_panel, arrived):
    fronts, _, capacity, _ = arrived.shape
    rows = own_panel.shape[0] + fronts * capacity
    vmem = pl.BlockSpec(memory_space=pltpu.VMEM)
    return pl.pallas_call(
        gram_kernel,
        grid=(1,),
        out_shape=[jax.ShapeDtypeStruct((BLK, PACKED), jnp.float32)] * 3
        + [jax.ShapeDtypeStruct((BLK // 2, PACKED), jnp.float32)] * 2
        + [jax.ShapeDtypeStruct((ELIMINATED, 2 * rows), jnp.bfloat16)],
        in_specs=[
            pl.BlockSpec(memory_space=pltpu.SMEM),
            vmem,
            pl.BlockSpec((fronts, 1, capacity, ELIMINATED), lambda j: (0, 0, 0, 0)),
        ],
        out_specs=[vmem] * 6,
        scratch_shapes=[pltpu.VMEM((2 * rows, ELIMINATED), jnp.bfloat16), pltpu.VMEM((4, BLK, PACKED), jnp.float32)],
        compiler_params=pltpu.CompilerParams(vmem_limit_bytes=VMEM_BYTES),
        cost_estimate=LIGHT,
    )(turn, own_panel, arrived)


def cross_kernel(turned_ref, own_ref, child_ref, out_ref, both_ref):
    stacked_halves(both_ref, own_ref[...], child_ref[:, 0].reshape(-1, WIDE))
    out_ref[0] = turned_dot(turned_ref[...], both_ref[...])


def cross(turned, own, start, child, part):
    fronts, _, capacity, _ = child.shape
    skipped = start // WIDE
    return pl.pallas_call(
        cross_kernel,
        grid=(ELIMINATED // WIDE,),
        out_shape=jax.ShapeDtypeStruct((ELIMINATED // WIDE, ELIMINATED, WIDE), jnp.float32),
        in_specs=[
            pl.BlockSpec(memory_space=pltpu.VMEM),
            pl.BlockSpec((own.shape[0], WIDE), lambda j: (0, skipped + j)),
            pl.BlockSpec((fronts, 1, capacity, WIDE), lambda j: (0, part, 0, j)),
        ],
        out_specs=pl.BlockSpec((1, ELIMINATED, WIDE), lambda j: (j, 0, 0)),
        scratch_shapes=[pltpu.VMEM((turned.shape[1], WIDE), jnp.bfloat16)],
        compiler_params=pltpu.CompilerParams(vmem_limit_bytes=VMEM_BYTES),
        cost_estimate=LIGHT,
    )(turned, own, child)


def shared_kernel(_, turned_ref, own_ref, child_ref, out_ref, both_ref):
    stacked_halves(both_ref, own_ref[...], child_ref[:, 0].reshape(-1, WIDE))
    total = turned_dot(turned_ref[...], both_ref[...])
    for half in range(2):
        out_ref[half] = total[:, BLK * half : BLK * (half + 1)]


def shared_cross(col, turned, own, child):
    fronts, _, capacity, _ = child.shape
    steps = own.shape[1] // WIDE
    return pl.pallas_call(
        shared_kernel,
        grid_spec=pltpu.PrefetchScalarGridSpec(
            num_scalar_prefetch=1,
            grid=(steps,),
            in_specs=[
                pl.BlockSpec(memory_space=pltpu.VMEM),
                pl.BlockSpec((own.shape[0], WIDE), lambda j, c: (0, j)),
                pl.BlockSpec((fronts, 1, capacity, WIDE), lambda j, c: (0, 1, 0, c[0] * steps + j)),
            ],
            out_specs=pl.BlockSpec((2, ELIMINATED, BLK), lambda j, c: (j, 0, 0)),
            scratch_shapes=[pltpu.VMEM((turned.shape[1], WIDE), jnp.bfloat16)],
        ),
        out_shape=jax.ShapeDtypeStruct((own.shape[1] // BLK, ELIMINATED, BLK), jnp.float32),
        compiler_params=pltpu.CompilerParams(vmem_limit_bytes=VMEM_BYTES),
        cost_estimate=LIGHT,
    )(col, turned, own, child)


def sharp_dot(a, b, dims):
    (high, low), (other_high, other_low) = a, b
    dims = (dims, ((), ()))
    total = lax.dot_general(high, other_high, dims, preferred_element_type=jnp.float32)
    total += lax.dot_general(high, other_low, dims, preferred_element_type=jnp.float32)
    return total + lax.dot_general(low, other_high, dims, preferred_element_type=jnp.float32)


PLAIN = ((1,), (0,))


def factor_kernel(
    turn_ref, piece_ref, before_ref, after_ref, across_ref, across_rest_ref, sums_ref,
    high_ref, low_ref, leading_ref, solved_ref,
    work_ref, diag_ref, packed_ref, panel_high_ref, panel_low_ref, found_ref,
):
    turn = turn_ref[0, 0]
    middle = BLK // 2
    packed_ref[turn] = piece_ref[...]
    packed_ref[lax.rem(turn + 1, 4)] = after_ref[...]
    packed_ref[lax.rem(turn + 3, 4)] = before_ref[...]
    packed_ref[lax.rem(turn + 2, 4), :middle] = across_ref[...]
    packed_ref[lax.rem(turn + 2, 4), middle:] = across_rest_ref[...]
    work_ref[...] = jnp.zeros_like(work_ref)
    panel_high_ref[...] = jnp.zeros_like(panel_high_ref)
    panel_low_ref[...] = jnp.zeros_like(panel_low_ref)
    for block, pair, offset in offsets():
        start = WIDE * block
        for half in range(2):
            work_ref[start + BLK * half : start + BLK * (half + 1), start:] = packed_ref[
                2 * pair + half, :, offset : offset + ELIMINATED - start
            ]
    row = lax.broadcasted_iota(jnp.int32, (BLK, BLK), 0)
    col = lax.broadcasted_iota(jnp.int32, (BLK, BLK), 1)
    place_of = lax.broadcasted_iota(jnp.int32, (BLK, ELIMINATED), 1) // BLK
    chunk_of = lax.broadcasted_iota(jnp.int32, (BLK, WIDE), 1) // BLK
    deferred = [(i, c) for i in range(2, STEPS) for c in range(ELIMINATED // WIDE)]

    sums = halves(sums_ref[0])

    def solve_rows(k):
        rows = pl.ds(pl.multiple_of(k * BLK, BLK), BLK)
        found_ref[rows, :] = sharp_dot((high_ref[rows, :], low_ref[rows, :]), sums, PLAIN)

    def step(k, _):
        here = pl.ds(pl.multiple_of(k * BLK, BLK), BLK)
        block = work_ref[here, here]
        turned = {}

        def update(i, c):
            below = i > k
            rows, cols = slice(BLK * i, BLK * (i + 1)), slice(WIDE * c, WIDE * (c + 1))
            if i not in turned:
                kept = jnp.where(below, 1.0, 0.0)
                turned[i] = [
                    (ref[:, rows].astype(jnp.float32) * kept).T.astype(jnp.bfloat16)
                    for ref in (panel_high_ref, panel_low_ref)
                ]
            panel = (panel_high_ref[:, cols], panel_low_ref[:, cols])
            cleared = jnp.where(below, k - 1 - c * (WIDE // BLK), -1)
            old = jnp.where(chunk_of == cleared, 0.0, work_ref[rows, cols])
            work_ref[rows, cols] = old - sharp_dot(turned[i], panel, PLAIN)

        def beside(b, count):
            for i, c in deferred[len(deferred) * b // count : len(deferred) * (b + 1) // count]:
                update(i, c)

        solve_rows(jnp.maximum(k - 1, 0))
        inverse = lower_inverse(block, beside)
        rows = sharp_dot(halves(inverse), halves(work_ref[here, :]), PLAIN)
        work_ref[here, :] = rows
        diag_ref[here, :] = jnp.where(row <= col, work_ref[here, here], 0.0)
        work_ref[here, here] = inverse
        rows = work_ref[here, :]
        panel_high_ref[...], panel_low_ref[...] = halves(rows)
        high_ref[here, :], low_ref[here, :] = halves(jnp.where(place_of <= k, rows, 0.0))

        @pl.when(k < STEPS - 1)
        def _():
            there = pl.ds(pl.multiple_of((k + 1) * BLK, BLK), BLK)
            left = [ref[:, there].astype(jnp.float32).T.astype(jnp.bfloat16) for ref in (panel_high_ref, panel_low_ref)]
            old = jnp.where(place_of == k, 0.0, work_ref[there, :])
            work_ref[there, :] = old - sharp_dot(left, (panel_high_ref[...], panel_low_ref[...]), PLAIN)

        return 0

    lax.fori_loop(0, STEPS, step, 0)
    taken = leading_ref.shape[0] // BLK
    for b in range(taken):
        block = turn * taken + b
        here = pl.ds(pl.multiple_of(block * BLK, BLK), BLK)
        diag = jnp.concatenate([diag_ref[here, :]] * STEPS, axis=1)
        leading_ref[BLK * b : BLK * (b + 1), :] = jnp.where(
            place_of > block, work_ref[here, :], jnp.where(place_of == block, diag, 0.0)
        )
    solve_rows(STEPS - 1)
    parts, copies, quarter, _ = solved_ref.shape
    for i in range(parts):
        for copy in range(copies):
            solved_ref[i, copy] = found_ref[quarter * i : quarter * (i + 1), :]


def factor(turn, piece, before, after, across, across_rest, sums):
    vmem = pl.BlockSpec(memory_space=pltpu.VMEM)
    return pl.pallas_call(
        factor_kernel,
        out_shape=(
            jax.ShapeDtypeStruct((ELIMINATED, ELIMINATED), jnp.bfloat16),
            jax.ShapeDtypeStruct((ELIMINATED, ELIMINATED), jnp.bfloat16),
            jax.ShapeDtypeStruct((ELIMINATED // 4, ELIMINATED), jnp.float32),
            jax.ShapeDtypeStruct((4, 2, ELIMINATED // 4, BLK), jnp.float32),
        ),
        in_specs=[pl.BlockSpec(memory_space=pltpu.SMEM)] + [vmem] * 6,
        out_specs=(vmem, vmem, vmem, vmem),
        scratch_shapes=[
            pltpu.VMEM((ELIMINATED, ELIMINATED), jnp.float32),
            pltpu.VMEM((ELIMINATED, BLK), jnp.float32),
            pltpu.VMEM((4, BLK, PACKED), jnp.float32),
            pltpu.VMEM((BLK, ELIMINATED), jnp.bfloat16),
            pltpu.VMEM((BLK, ELIMINATED), jnp.bfloat16),
            pltpu.VMEM((ELIMINATED, BLK), jnp.float32),
        ],
        compiler_params=pltpu.CompilerParams(vmem_limit_bytes=VMEM_BYTES),
        cost_estimate=LIGHT,
    )(turn, piece, before, after, across, across_rest, sums)


def solve_kernel(high_ref, low_ref, sums_ref, out_ref):
    parts, quarter, _ = out_ref.shape
    sums = halves(sums_ref[0])
    for i in range(parts):
        rows, depth = slice(quarter * i, quarter * (i + 1)), quarter * (i + 1)
        out_ref[i] = sharp_dot(
            (high_ref[rows, :depth], low_ref[rows, :depth]), tuple(x[:depth] for x in sums), PLAIN
        )


def solve(high, low, sums):
    vmem = pl.BlockSpec(memory_space=pltpu.VMEM)
    return pl.pallas_call(
        solve_kernel,
        out_shape=jax.ShapeDtypeStruct((4, ELIMINATED // 4, sums.shape[2]), jnp.float32),
        in_specs=[vmem] * 3,
        out_specs=vmem,
        compiler_params=pltpu.CompilerParams(vmem_limit_bytes=VMEM_BYTES),
        cost_estimate=LIGHT,
    )(high, low, sums)


def join_kernel(col_ref, leading_ref, first_ref, second_ref, out_ref):
    parts, _, width = second_ref.shape
    for j in range(parts):
        for half in range(2):
            start = ELIMINATED // 2 * half + BLK * j
            cols = slice(start, start + BLK)
            out_ref[0, :, cols] = jnp.where(
                col_ref[0, 0] == 0, leading_ref[:, cols], first_ref[j, half]
            )
    for j in range(parts):
        out_ref[0, :, ELIMINATED + width * j : ELIMINATED + width * (j + 1)] = second_ref[j]


def join(col, leading, first, second):
    vmem = pl.BlockSpec(memory_space=pltpu.VMEM)
    return pl.pallas_call(
        join_kernel,
        out_shape=jax.ShapeDtypeStruct((1, leading.shape[0], 2 * ELIMINATED), jnp.float32),
        in_specs=[pl.BlockSpec(memory_space=pltpu.SMEM)] + [vmem] * 3,
        out_specs=vmem,
        compiler_params=pltpu.CompilerParams(vmem_limit_bytes=VMEM_BYTES),
        cost_estimate=LIGHT,
    )(col, leading, first, second)


def shifted(x, shift, count):
    return lax.ppermute(x, "row", [(i, (i + shift) % count) for i in range(count)])


def body(own_rows, child_rows, child_dest, child_stair):
    n_front = lax.axis_size("front")
    row_count = lax.axis_size("row")
    source_rows, half_cols = child_rows.shape
    capacity = max(2, 2 * source_rows // n_front)
    col_index = lax.axis_index("col")
    row_index = lax.axis_index("row")
    quarter = ELIMINATED // row_count
    own = own_rows[0]
    own_a = own[:, :ELIMINATED]
    split = own_a.shape[0] // 4
    passed = lax.ppermute(own_a[:split], "col", [(0, 1), (1, 0)])
    passed_rest = lax.ppermute(own_a[split:], "col", [(0, 1), (1, 0)])

    first_col = col_index * half_cols
    dest, stair = child_dest.reshape(1, source_rows), child_stair.reshape(source_rows, 1)
    doubled = place(first_col, dest, stair, child_rows, 0, 2, n_front, capacity)
    single = place(first_col, dest, stair, child_rows, ELIMINATED, 1, n_front, capacity)
    doubled, passed = lax.optimization_barrier((doubled, passed))
    arrived = lax.all_to_all(
        doubled.reshape(2 * n_front * capacity, ELIMINATED),
        ("front", "col"),
        split_axis=0,
        concat_axis=0,
        tiled=True,
    ).reshape(n_front, 2, capacity, ELIMINATED)
    passed = jnp.concatenate([passed, passed_rest], axis=0)
    own_panel = jnp.where(col_index == 0, own_a, passed)
    own_shared = jnp.where(
        col_index == 0, passed[:, : ELIMINATED // 2], own_a[:, ELIMINATED // 2 :]
    )

    own_panel, single = lax.optimization_barrier((own_panel, single))
    child_b = lax.all_to_all(
        single.reshape(n_front * capacity, ELIMINATED), "front", split_axis=0, concat_axis=0, tiled=True
    ).reshape(n_front, 1, capacity, ELIMINATED)
    turn = row_index.reshape(1, 1)
    mine, right, left, right_rest, left_rest, turned = packed_gram(turn, own_panel, arrived)
    middle = BLK // 2
    from_left, from_right = shifted(right, 1, row_count), shifted(left, -1, row_count)
    from_left, from_right, turned_later = lax.optimization_barrier((from_left, from_right, turned))
    products_a = shared_cross(col_index.reshape(1), turned_later, own_shared, arrived)
    rest_left = shifted(right_rest + from_left[:middle], 1, row_count)
    rest_right = shifted(left_rest + from_right[:middle], -1, row_count)
    rest_left, rest_right = lax.optimization_barrier((rest_left, rest_right))
    piece = mine + jnp.concatenate(
        [rest_left + from_right[middle:], from_left[middle:] + rest_right], axis=0
    )
    before, after = shifted(piece, 1, row_count), shifted(piece, -1, row_count)
    before, after, child_b = lax.optimization_barrier((before, after, child_b))
    across, across_rest = shifted(before[:middle], 1, row_count), shifted(after[middle:], -1, row_count)
    pieces = (piece, before, after, across, across_rest)

    def summed(products):
        return lax.psum_scatter(products, "row", scatter_dimension=0, tiled=True)

    products_b = cross(turned, own, ELIMINATED, child_b, 0)
    pieces, products_b = lax.optimization_barrier((pieces, products_b))
    inverse_high, inverse_low, leading, first = factor(turn, *pieces, summed(products_a))
    first = lax.all_to_all(
        first.reshape(2 * row_count, quarter, BLK), ("row", "col"), split_axis=0, concat_axis=0, tiled=True
    ).reshape(row_count, 2, quarter, BLK)
    second = solve(inverse_high, inverse_low, summed(products_b))
    second = lax.all_to_all(second, "row", split_axis=0, concat_axis=0, tiled=True)
    return join(col_index.reshape(1, 1), leading, first, second)


def solution(mesh):
    placed = (
        P("front", "row", "col"),
        P(("front", "row"), "col"),
        P(("front", "row"), None),
        P(("front", "row")),
    )
    return jax.shard_map(
        body, mesh=mesh, in_specs=placed, out_specs=P("front", "row", "col"), check_vma=False
    )
```

```python
import jax
import jax.numpy as jnp
from jax import lax
from jax.experimental import pallas as pl
from jax.experimental.pallas import tpu as pltpu
from jax.sharding import PartitionSpec as P

ELIMINATED = 1024
STAIR_BLK = 128
BLK = 128
STEPS = ELIMINATED // BLK
LINES = 8
VMEM_BYTES = 60 * 2**20
LIGHT = pl.CostEstimate(flops=1, bytes_accessed=1, transcendentals=0)


def lower_inverse(diag_block, beside):
    lane = lax.broadcasted_iota(jnp.int32, (LINES, BLK), 1)
    sublane = lax.broadcasted_iota(jnp.int32, (LINES, BLK), 0)
    count = BLK // LINES
    strips = [diag_block[LINES * i : LINES * (i + 1), :] for i in range(count)]
    for b in range(count):
        first = LINES * b
        within = (lane >= first) & (lane < first + LINES)
        strip = strips[b]
        column = [
            jnp.broadcast_to(strip[:, first + t : first + t + 1], (LINES, BLK))
            for t in range(LINES)
        ]
        entry = [
            [jnp.broadcast_to(column[t][i : i + 1, :], (LINES, BLK)) for t in range(i + 1)]
            for i in range(LINES)
        ]
        unit = [lax.rsqrt(entry[t][t]) for t in range(LINES)]
        for i in range(LINES):
            for t in range(i + 1):
                entry[i][t] = entry[i][t] * unit[i] * unit[t]
        scale = []
        for t in range(0, LINES, 2):
            top, side, last = entry[t][t], entry[t + 1][t], entry[t + 1][t + 1]
            root = lax.rsqrt(top)
            scale.append(root)
            scale.append(top * root * lax.rsqrt(top * last - side * side))
            for i in range(t + 1, LINES):
                entry[i][t] = entry[i][t] * root
            for i in range(t + 2, LINES):
                entry[i][t + 1] = (entry[i][t + 1] - entry[i][t] * entry[t + 1][t]) * scale[t + 1]
            for u in range(t + 2, LINES):
                for i in range(u, LINES):
                    entry[i][u] = (
                        entry[i][u] - entry[i][t] * entry[u][t] - entry[i][t + 1] * entry[u][t + 1]
                    )
        solved = []
        augmented = jnp.where(within, jnp.where(lane == sublane + first, 1.0, 0.0), strip)
        for t in range(LINES):
            line = jnp.broadcast_to(augmented[t : t + 1, :], (LINES, BLK)) * unit[t]
            for s in range(t):
                line = line - entry[t][s] * solved[s]
            solved.append(line * scale[t])
        merged = solved[0]
        for t in range(1, LINES):
            merged = jnp.where(sublane == t, solved[t], merged)
        strips[b] = merged
        beside(b, count)
        for i in range(b + 1, count):
            below = strips[i]
            rest = jnp.where(within, 0.0, below)
            factors = []
            for t in range(LINES):
                value = jnp.broadcast_to(below[:, first + t : first + t + 1], (LINES, BLK)) * unit[t]
                for s in range(t):
                    value = value - entry[t][s] * factors[s]
                value = value * scale[t]
                factors.append(value)
                rest = rest - value * solved[t]
            strips[i] = rest
    row = lax.broadcasted_iota(jnp.int32, (BLK, BLK), 0)
    col = lax.broadcasted_iota(jnp.int32, (BLK, BLK), 1)
    return jnp.where(row >= col, jnp.concatenate(strips, axis=0), 0.0)


PAIRS = ((0, 3), (1, 2))
WIDE = 256
PACKED = ELIMINATED + WIDE


def offsets():
    found = []
    for pair, (long, short) in enumerate(PAIRS):
        found.append((long, pair, 0))
        found.append((short, pair, ELIMINATED - WIDE * long))
    return found


def halves(x):
    high = x.astype(jnp.bfloat16)
    return high, (x - high.astype(jnp.float32)).astype(jnp.bfloat16)


def place_kernel(first_ref, dest_ref, stair_ref, rows_ref, out_ref, select_ref):
    fronts, copies, capacity, width = out_ref.shape
    slots, sources = select_ref.shape
    chunk = pl.program_id(0)

    @pl.when(chunk == 0)
    def _():
        dest = dest_ref[...]
        named = lax.broadcasted_iota(jnp.int32, (fronts, sources), 0) == dest
        source = lax.broadcasted_iota(jnp.int32, (sources, sources), 0)
        later = lax.broadcasted_iota(jnp.int32, (sources, sources), 1)
        before = jnp.dot(
            named.astype(jnp.float32).astype(jnp.bfloat16),
            (source < later).astype(jnp.float32).astype(jnp.bfloat16),
            preferred_element_type=jnp.float32,
        )
        slot = jnp.sum(jnp.where(named, before, 0.0), axis=0, keepdims=True).astype(jnp.int32)
        position = dest * capacity + slot
        line = lax.broadcasted_iota(jnp.int32, (slots, sources), 0)
        select_ref[...] = (line == position).astype(jnp.float32).astype(jnp.bfloat16)

    cols = (
        first_ref[0, 0] + chunk * width + lax.broadcasted_iota(jnp.int32, (sources, width), 1)
    )
    high, low = halves(jnp.where(cols >= stair_ref[...] * STAIR_BLK, rows_ref[...], 0.0))
    select = select_ref[...]
    placed = jnp.dot(select, high, preferred_element_type=jnp.float32) + jnp.dot(
        select, low, preferred_element_type=jnp.float32
    )
    placed = placed.reshape(fronts, capacity, width)
    for copy in range(copies):
        out_ref[:, copy] = placed


def place(first_col, dest, stair, rows, start, copies, n_front, capacity):
    sources = rows.shape[0]
    skipped = start // WIDE
    return pl.pallas_call(
        place_kernel,
        grid=(ELIMINATED // WIDE,),
        out_shape=jax.ShapeDtypeStruct((n_front, copies, capacity, ELIMINATED), jnp.float32),
        in_specs=[
            pl.BlockSpec(memory_space=pltpu.SMEM),
            pl.BlockSpec((1, sources), lambda j: (0, 0)),
            pl.BlockSpec((sources, 1), lambda j: (0, 0)),
            pl.BlockSpec((sources, WIDE), lambda j: (0, skipped + j)),
        ],
        out_specs=pl.BlockSpec((n_front, copies, capacity, WIDE), lambda j: (0, 0, 0, j)),
        scratch_shapes=[pltpu.VMEM((n_front * capacity, sources), jnp.bfloat16)],
        compiler_params=pltpu.CompilerParams(vmem_limit_bytes=VMEM_BYTES),
        cost_estimate=LIGHT,
    )((first_col + start).reshape(1, 1), dest, stair, rows)


def stacked_halves(out_ref, *parts):
    count = out_ref.shape[0] // 2
    first = 0
    for x in parts:
        rows = x.shape[0]
        high, low = halves(x)
        out_ref[first : first + rows] = low
        out_ref[count + first : count + first + rows] = high
        first += rows


def turned_dot(turned, other):
    count = other.shape[0] // 2
    return jnp.dot(turned, other, preferred_element_type=jnp.float32) + jnp.dot(
        turned[:, :count], other[count:], preferred_element_type=jnp.float32
    )


def gram_kernel(turn_ref, own_ref, child_ref, *outs):
    turned_ref, both_ref, packed_ref = outs[5:]
    count = both_ref.shape[0] // 2
    stacked_halves(both_ref, own_ref[...], child_ref[:, 0].reshape(-1, ELIMINATED))
    for start in range(0, ELIMINATED, WIDE):
        cols = slice(start, start + WIDE)
        turned_ref[cols, :count] = both_ref[count:, cols].T
        turned_ref[cols, count:] = both_ref[:count, cols].T
    for block, pair, offset in offsets():
        start = WIDE * block
        total = turned_dot(turned_ref[start : start + WIDE, :], both_ref[:, start:])
        for half in range(2):
            packed_ref[2 * pair + half, :, offset : offset + ELIMINATED - start] = total[
                BLK * half : BLK * (half + 1)
            ]
    mine_ref, right_ref, left_ref, right_rest_ref, left_rest_ref, *_ = outs
    turn = turn_ref[0, 0]
    here, right, over, left = [lax.rem(turn + s, 4) for s in range(4)]
    middle = BLK // 2
    mine_ref[...] = packed_ref[here]
    right_ref[:middle], right_ref[middle:] = packed_ref[over, :middle], packed_ref[right, middle:]
    left_ref[:middle], left_ref[middle:] = packed_ref[over, middle:], packed_ref[left, :middle]
    right_rest_ref[...] = packed_ref[right, :middle]
    left_rest_ref[...] = packed_ref[left, middle:]


def packed_gram(turn, own_panel, arrived):
    fronts, _, capacity, _ = arrived.shape
    rows = own_panel.shape[0] + fronts * capacity
    vmem = pl.BlockSpec(memory_space=pltpu.VMEM)
    return pl.pallas_call(
        gram_kernel,
        grid=(1,),
        out_shape=[jax.ShapeDtypeStruct((BLK, PACKED), jnp.float32)] * 3
        + [jax.ShapeDtypeStruct((BLK // 2, PACKED), jnp.float32)] * 2
        + [jax.ShapeDtypeStruct((ELIMINATED, 2 * rows), jnp.bfloat16)],
        in_specs=[
            pl.BlockSpec(memory_space=pltpu.SMEM),
            vmem,
            pl.BlockSpec((fronts, 1, capacity, ELIMINATED), lambda j: (0, 0, 0, 0)),
        ],
        out_specs=[vmem] * 6,
        scratch_shapes=[pltpu.VMEM((2 * rows, ELIMINATED), jnp.bfloat16), pltpu.VMEM((4, BLK, PACKED), jnp.float32)],
        compiler_params=pltpu.CompilerParams(vmem_limit_bytes=VMEM_BYTES),
        cost_estimate=LIGHT,
    )(turn, own_panel, arrived)


def cross_kernel(turned_ref, own_ref, child_ref, out_ref, both_ref):
    stacked_halves(both_ref, own_ref[...], child_ref[:, 0].reshape(-1, WIDE))
    out_ref[0] = turned_dot(turned_ref[...], both_ref[...])


def cross(turned, own, start, child, part):
    fronts, _, capacity, _ = child.shape
    skipped = start // WIDE
    return pl.pallas_call(
        cross_kernel,
        grid=(ELIMINATED // WIDE,),
        out_shape=jax.ShapeDtypeStruct((ELIMINATED // WIDE, ELIMINATED, WIDE), jnp.float32),
        in_specs=[
            pl.BlockSpec(memory_space=pltpu.VMEM),
            pl.BlockSpec((own.shape[0], WIDE), lambda j: (0, skipped + j)),
            pl.BlockSpec((fronts, 1, capacity, WIDE), lambda j: (0, part, 0, j)),
        ],
        out_specs=pl.BlockSpec((1, ELIMINATED, WIDE), lambda j: (j, 0, 0)),
        scratch_shapes=[pltpu.VMEM((turned.shape[1], WIDE), jnp.bfloat16)],
        compiler_params=pltpu.CompilerParams(vmem_limit_bytes=VMEM_BYTES),
        cost_estimate=LIGHT,
    )(turned, own, child)


def shared_kernel(_, turned_ref, own_ref, child_ref, out_ref, both_ref):
    stacked_halves(both_ref, own_ref[...], child_ref[:, 0].reshape(-1, WIDE))
    total = turned_dot(turned_ref[...], both_ref[...])
    for half in range(2):
        out_ref[half] = total[:, BLK * half : BLK * (half + 1)]


def shared_cross(col, turned, own, child):
    fronts, _, capacity, _ = child.shape
    steps = own.shape[1] // WIDE
    return pl.pallas_call(
        shared_kernel,
        grid_spec=pltpu.PrefetchScalarGridSpec(
            num_scalar_prefetch=1,
            grid=(steps,),
            in_specs=[
                pl.BlockSpec(memory_space=pltpu.VMEM),
                pl.BlockSpec((own.shape[0], WIDE), lambda j, c: (0, j)),
                pl.BlockSpec((fronts, 1, capacity, WIDE), lambda j, c: (0, 1, 0, c[0] * steps + j)),
            ],
            out_specs=pl.BlockSpec((2, ELIMINATED, BLK), lambda j, c: (j, 0, 0)),
            scratch_shapes=[pltpu.VMEM((turned.shape[1], WIDE), jnp.bfloat16)],
        ),
        out_shape=jax.ShapeDtypeStruct((own.shape[1] // BLK, ELIMINATED, BLK), jnp.float32),
        compiler_params=pltpu.CompilerParams(vmem_limit_bytes=VMEM_BYTES),
        cost_estimate=LIGHT,
    )(col, turned, own, child)


def sharp_dot(a, b, dims):
    (high, low), (other_high, other_low) = a, b
    dims = (dims, ((), ()))
    total = lax.dot_general(high, other_high, dims, preferred_element_type=jnp.float32)
    total += lax.dot_general(high, other_low, dims, preferred_element_type=jnp.float32)
    return total + lax.dot_general(low, other_high, dims, preferred_element_type=jnp.float32)


PLAIN = ((1,), (0,))


def factor_kernel(
    turn_ref, piece_ref, before_ref, after_ref, across_ref, across_rest_ref, sums_ref,
    high_ref, low_ref, leading_ref, solved_ref,
    work_ref, diag_ref, packed_ref, panel_high_ref, panel_low_ref, found_ref,
):
    turn = turn_ref[0, 0]
    middle = BLK // 2
    packed_ref[turn] = piece_ref[...]
    packed_ref[lax.rem(turn + 1, 4)] = after_ref[...]
    packed_ref[lax.rem(turn + 3, 4)] = before_ref[...]
    packed_ref[lax.rem(turn + 2, 4), :middle] = across_ref[...]
    packed_ref[lax.rem(turn + 2, 4), middle:] = across_rest_ref[...]
    work_ref[...] = jnp.zeros_like(work_ref)
    panel_high_ref[...] = jnp.zeros_like(panel_high_ref)
    panel_low_ref[...] = jnp.zeros_like(panel_low_ref)
    for block, pair, offset in offsets():
        start = WIDE * block
        for half in range(2):
            work_ref[start + BLK * half : start + BLK * (half + 1), start:] = packed_ref[
                2 * pair + half, :, offset : offset + ELIMINATED - start
            ]
    row = lax.broadcasted_iota(jnp.int32, (BLK, BLK), 0)
    col = lax.broadcasted_iota(jnp.int32, (BLK, BLK), 1)
    place_of = lax.broadcasted_iota(jnp.int32, (BLK, ELIMINATED), 1) // BLK
    chunk_of = lax.broadcasted_iota(jnp.int32, (BLK, WIDE), 1) // BLK
    deferred = [(i, c) for i in range(2, STEPS) for c in range(ELIMINATED // WIDE)]

    sums = halves(sums_ref[0])

    def solve_rows(k):
        rows = pl.ds(pl.multiple_of(k * BLK, BLK), BLK)
        found_ref[rows, :] = sharp_dot((high_ref[rows, :], low_ref[rows, :]), sums, PLAIN)

    def step(k, _):
        here = pl.ds(pl.multiple_of(k * BLK, BLK), BLK)
        block = work_ref[here, here]
        turned = {}

        def update(i, c):
            below = i > k
            rows, cols = slice(BLK * i, BLK * (i + 1)), slice(WIDE * c, WIDE * (c + 1))
            if i not in turned:
                kept = jnp.where(below, 1.0, 0.0)
                turned[i] = [
                    (ref[:, rows].astype(jnp.float32) * kept).T.astype(jnp.bfloat16)
                    for ref in (panel_high_ref, panel_low_ref)
                ]
            panel = (panel_high_ref[:, cols], panel_low_ref[:, cols])
            cleared = jnp.where(below, k - 1 - c * (WIDE // BLK), -1)
            old = jnp.where(chunk_of == cleared, 0.0, work_ref[rows, cols])
            work_ref[rows, cols] = old - sharp_dot(turned[i], panel, PLAIN)

        def beside(b, count):
            for i, c in deferred[len(deferred) * b // count : len(deferred) * (b + 1) // count]:
                update(i, c)

        solve_rows(jnp.maximum(k - 1, 0))
        inverse = lower_inverse(block, beside)
        rows = sharp_dot(halves(inverse), halves(work_ref[here, :]), PLAIN)
        work_ref[here, :] = rows
        diag_ref[here, :] = jnp.where(row <= col, work_ref[here, here], 0.0)
        work_ref[here, here] = inverse
        rows = work_ref[here, :]
        panel_high_ref[...], panel_low_ref[...] = halves(rows)
        high_ref[here, :], low_ref[here, :] = halves(jnp.where(place_of <= k, rows, 0.0))

        @pl.when(k < STEPS - 1)
        def _():
            there = pl.ds(pl.multiple_of((k + 1) * BLK, BLK), BLK)
            left = [ref[:, there].astype(jnp.float32).T.astype(jnp.bfloat16) for ref in (panel_high_ref, panel_low_ref)]
            old = jnp.where(place_of == k, 0.0, work_ref[there, :])
            work_ref[there, :] = old - sharp_dot(left, (panel_high_ref[...], panel_low_ref[...]), PLAIN)

        return 0

    lax.fori_loop(0, STEPS, step, 0)
    taken = leading_ref.shape[0] // BLK
    for b in range(taken):
        block = turn * taken + b
        here = pl.ds(pl.multiple_of(block * BLK, BLK), BLK)
        diag = jnp.concatenate([diag_ref[here, :]] * STEPS, axis=1)
        leading_ref[BLK * b : BLK * (b + 1), :] = jnp.where(
            place_of > block, work_ref[here, :], jnp.where(place_of == block, diag, 0.0)
        )
    solve_rows(STEPS - 1)
    parts, copies, quarter, _ = solved_ref.shape
    for i in range(parts):
        for copy in range(copies):
            solved_ref[i, copy] = found_ref[quarter * i : quarter * (i + 1), :]


def factor(turn, piece, before, after, across, across_rest, sums):
    vmem = pl.BlockSpec(memory_space=pltpu.VMEM)
    return pl.pallas_call(
        factor_kernel,
        out_shape=(
            jax.ShapeDtypeStruct((ELIMINATED, ELIMINATED), jnp.bfloat16),
            jax.ShapeDtypeStruct((ELIMINATED, ELIMINATED), jnp.bfloat16),
            jax.ShapeDtypeStruct((ELIMINATED // 4, ELIMINATED), jnp.float32),
            jax.ShapeDtypeStruct((4, 2, ELIMINATED // 4, BLK), jnp.float32),
        ),
        in_specs=[pl.BlockSpec(memory_space=pltpu.SMEM)] + [vmem] * 6,
        out_specs=(vmem, vmem, vmem, vmem),
        scratch_shapes=[
            pltpu.VMEM((ELIMINATED, ELIMINATED), jnp.float32),
            pltpu.VMEM((ELIMINATED, BLK), jnp.float32),
            pltpu.VMEM((4, BLK, PACKED), jnp.float32),
            pltpu.VMEM((BLK, ELIMINATED), jnp.bfloat16),
            pltpu.VMEM((BLK, ELIMINATED), jnp.bfloat16),
            pltpu.VMEM((ELIMINATED, BLK), jnp.float32),
        ],
        compiler_params=pltpu.CompilerParams(vmem_limit_bytes=VMEM_BYTES),
        cost_estimate=LIGHT,
    )(turn, piece, before, after, across, across_rest, sums)


def solve_kernel(high_ref, low_ref, sums_ref, out_ref):
    parts, quarter, _ = out_ref.shape
    sums = halves(sums_ref[0])
    for i in range(parts):
        rows, depth = slice(quarter * i, quarter * (i + 1)), quarter * (i + 1)
        out_ref[i] = sharp_dot(
            (high_ref[rows, :depth], low_ref[rows, :depth]), tuple(x[:depth] for x in sums), PLAIN
        )


def solve(high, low, sums):
    vmem = pl.BlockSpec(memory_space=pltpu.VMEM)
    return pl.pallas_call(
        solve_kernel,
        out_shape=jax.ShapeDtypeStruct((4, ELIMINATED // 4, sums.shape[2]), jnp.float32),
        in_specs=[vmem] * 3,
        out_specs=vmem,
        compiler_params=pltpu.CompilerParams(vmem_limit_bytes=VMEM_BYTES),
        cost_estimate=LIGHT,
    )(high, low, sums)


def join_kernel(col_ref, leading_ref, first_ref, second_ref, out_ref):
    parts, _, width = second_ref.shape
    for j in range(parts):
        for half in range(2):
            start = ELIMINATED // 2 * half + BLK * j
            cols = slice(start, start + BLK)
            out_ref[0, :, cols] = jnp.where(
                col_ref[0, 0] == 0, leading_ref[:, cols], first_ref[j, half]
            )
    for j in range(parts):
        out_ref[0, :, ELIMINATED + width * j : ELIMINATED + width * (j + 1)] = second_ref[j]


def join(col, leading, first, second):
    vmem = pl.BlockSpec(memory_space=pltpu.VMEM)
    return pl.pallas_call(
        join_kernel,
        out_shape=jax.ShapeDtypeStruct((1, leading.shape[0], 2 * ELIMINATED), jnp.float32),
        in_specs=[pl.BlockSpec(memory_space=pltpu.SMEM)] + [vmem] * 3,
        out_specs=vmem,
        compiler_params=pltpu.CompilerParams(vmem_limit_bytes=VMEM_BYTES),
        cost_estimate=LIGHT,
    )(col, leading, first, second)


def shifted(x, shift, count):
    return lax.ppermute(x, "row", [(i, (i + shift) % count) for i in range(count)])


def body(own_rows, child_rows, child_dest, child_stair):
    n_front = lax.axis_size("front")
    row_count = lax.axis_size("row")
    source_rows, half_cols = child_rows.shape
    capacity = max(2, 2 * source_rows // n_front)
    col_index = lax.axis_index("col")
    row_index = lax.axis_index("row")
    quarter = ELIMINATED // row_count
    own = own_rows[0]
    own_a = own[:, :ELIMINATED]
    split = own_a.shape[0] // 4
    passed = lax.ppermute(own_a[:split], "col", [(0, 1), (1, 0)])
    passed_rest = lax.ppermute(own_a[split:], "col", [(0, 1), (1, 0)])

    first_col = col_index * half_cols
    dest, stair = child_dest.reshape(1, source_rows), child_stair.reshape(source_rows, 1)
    doubled = place(first_col, dest, stair, child_rows, 0, 2, n_front, capacity)
    single = place(first_col, dest, stair, child_rows, ELIMINATED, 1, n_front, capacity)
    doubled, passed = lax.optimization_barrier((doubled, passed))
    arrived = lax.all_to_all(
        doubled.reshape(2 * n_front * capacity, ELIMINATED),
        ("front", "col"),
        split_axis=0,
        concat_axis=0,
        tiled=True,
    ).reshape(n_front, 2, capacity, ELIMINATED)
    passed = jnp.concatenate([passed, passed_rest], axis=0)
    own_panel = jnp.where(col_index == 0, own_a, passed)
    own_shared = jnp.where(
        col_index == 0, passed[:, : ELIMINATED // 2], own_a[:, ELIMINATED // 2 :]
    )

    own_panel, single = lax.optimization_barrier((own_panel, single))
    child_b = lax.all_to_all(
        single.reshape(n_front * capacity, ELIMINATED), "front", split_axis=0, concat_axis=0, tiled=True
    ).reshape(n_front, 1, capacity, ELIMINATED)
    turn = row_index.reshape(1, 1)
    mine, right, left, right_rest, left_rest, turned = packed_gram(turn, own_panel, arrived)
    middle = BLK // 2
    from_left, from_right = shifted(right, 1, row_count), shifted(left, -1, row_count)
    from_left, from_right, turned_later = lax.optimization_barrier((from_left, from_right, turned))
    products_a = shared_cross(col_index.reshape(1), turned_later, own_shared, arrived)
    rest_left = shifted(right_rest + from_left[:middle], 1, row_count)
    rest_right = shifted(left_rest + from_right[:middle], -1, row_count)
    rest_left, rest_right = lax.optimization_barrier((rest_left, rest_right))
    piece = mine + jnp.concatenate(
        [rest_left + from_right[middle:], from_left[middle:] + rest_right], axis=0
    )
    before, after = shifted(piece, 1, row_count), shifted(piece, -1, row_count)
    before, after, child_b = lax.optimization_barrier((before, after, child_b))
    across, across_rest = shifted(before[:middle], 1, row_count), shifted(after[middle:], -1, row_count)
    pieces = (piece, before, after, across, across_rest)

    def summed(products):
        return lax.psum_scatter(products, "row", scatter_dimension=0, tiled=True)

    products_b = cross(turned, own, ELIMINATED, child_b, 0)
    pieces, products_b = lax.optimization_barrier((pieces, products_b))
    inverse_high, inverse_low, leading, first = factor(turn, *pieces, summed(products_a))
    first = lax.all_to_all(
        first.reshape(2 * row_count, quarter, BLK), ("row", "col"), split_axis=0, concat_axis=0, tiled=True
    ).reshape(row_count, 2, quarter, BLK)
    second = solve(inverse_high, inverse_low, summed(products_b))
    second = lax.all_to_all(second, "row", split_axis=0, concat_axis=0, tiled=True)
    return join(col_index.reshape(1, 1), leading, first, second)


def solution(mesh):
    placed = (
        P("front", "row", "col"),
        P(("front", "row"), "col"),
        P(("front", "row"), None),
        P(("front", "row")),
    )
    return jax.shard_map(
        body, mesh=mesh, in_specs=placed, out_specs=P("front", "row", "col"), check_vma=False
    )
```

```python
import jax
import jax.numpy as jnp
from jax import lax
from jax.experimental import pallas as pl
from jax.experimental.pallas import tpu as pltpu
from jax.sharding import PartitionSpec as P

ELIMINATED = 1024
STAIR_BLK = 128
BLK = 128
STEPS = ELIMINATED // BLK
LINES = 8
VMEM_BYTES = 60 * 2**20
LIGHT = pl.CostEstimate(flops=1, bytes_accessed=1, transcendentals=0)


def lower_inverse(diag_block, beside):
    lane = lax.broadcasted_iota(jnp.int32, (LINES, BLK), 1)
    sublane = lax.broadcasted_iota(jnp.int32, (LINES, BLK), 0)
    count = BLK // LINES
    strips = [diag_block[LINES * i : LINES * (i + 1), :] for i in range(count)]
    for b in range(count):
        first = LINES * b
        within = (lane >= first) & (lane < first + LINES)
        strip = strips[b]
        column = [
            jnp.broadcast_to(strip[:, first + t : first + t + 1], (LINES, BLK))
            for t in range(LINES)
        ]
        entry = [
            [jnp.broadcast_to(column[t][i : i + 1, :], (LINES, BLK)) for t in range(i + 1)]
            for i in range(LINES)
        ]
        scale = []
        for t in range(LINES):
            scale.append(lax.rsqrt(entry[t][t]))
            for i in range(t + 1, LINES):
                entry[i][t] = entry[i][t] * scale[t]
            for u in range(t + 1, LINES):
                for i in range(u, LINES):
                    entry[i][u] = entry[i][u] - entry[i][t] * entry[u][t]
        solved = []
        augmented = jnp.where(within, jnp.where(lane == sublane + first, 1.0, 0.0), strip)
        for t in range(LINES):
            line = jnp.broadcast_to(augmented[t : t + 1, :], (LINES, BLK))
            for s in range(t):
                line = line - entry[t][s] * solved[s]
            solved.append(line * scale[t])
        merged = solved[0]
        for t in range(1, LINES):
            merged = jnp.where(sublane == t, solved[t], merged)
        strips[b] = merged
        beside(b, count)
        for i in range(b + 1, count):
            below = strips[i]
            rest = jnp.where(within, 0.0, below)
            factors = []
            for t in range(LINES):
                value = jnp.broadcast_to(below[:, first + t : first + t + 1], (LINES, BLK))
                for s in range(t):
                    value = value - entry[t][s] * factors[s]
                value = value * scale[t]
                factors.append(value)
                rest = rest - value * solved[t]
            strips[i] = rest
    row = lax.broadcasted_iota(jnp.int32, (BLK, BLK), 0)
    col = lax.broadcasted_iota(jnp.int32, (BLK, BLK), 1)
    return jnp.where(row >= col, jnp.concatenate(strips, axis=0), 0.0)


PAIRS = ((0, 3), (1, 2))
WIDE = 256
PACKED = ELIMINATED + WIDE


def offsets():
    found = []
    for pair, (long, short) in enumerate(PAIRS):
        found.append((long, pair, 0))
        found.append((short, pair, ELIMINATED - WIDE * long))
    return found


def halves(x):
    high = x.astype(jnp.bfloat16)
    return high, (x - high.astype(jnp.float32)).astype(jnp.bfloat16)


def place_kernel(first_ref, dest_ref, stair_ref, rows_ref, out_ref, select_ref):
    fronts, copies, capacity, width = out_ref.shape
    slots, sources = select_ref.shape
    chunk = pl.program_id(0)

    @pl.when(chunk == 0)
    def _():
        dest = dest_ref[...]
        named = lax.broadcasted_iota(jnp.int32, (fronts, sources), 0) == dest
        source = lax.broadcasted_iota(jnp.int32, (sources, sources), 0)
        later = lax.broadcasted_iota(jnp.int32, (sources, sources), 1)
        before = jnp.dot(
            named.astype(jnp.float32).astype(jnp.bfloat16),
            (source < later).astype(jnp.float32).astype(jnp.bfloat16),
            preferred_element_type=jnp.float32,
        )
        slot = jnp.sum(jnp.where(named, before, 0.0), axis=0, keepdims=True).astype(jnp.int32)
        position = dest * capacity + slot
        line = lax.broadcasted_iota(jnp.int32, (slots, sources), 0)
        select_ref[...] = (line == position).astype(jnp.float32).astype(jnp.bfloat16)

    cols = (
        first_ref[0, 0] + chunk * width + lax.broadcasted_iota(jnp.int32, (sources, width), 1)
    )
    high, low = halves(jnp.where(cols >= stair_ref[...] * STAIR_BLK, rows_ref[...], 0.0))
    select = select_ref[...]
    placed = jnp.dot(select, high, preferred_element_type=jnp.float32) + jnp.dot(
        select, low, preferred_element_type=jnp.float32
    )
    placed = placed.reshape(fronts, capacity, width)
    for copy in range(copies):
        out_ref[:, copy] = placed


def place(first_col, dest, stair, rows, start, copies, n_front, capacity):
    sources = rows.shape[0]
    skipped = start // WIDE
    return pl.pallas_call(
        place_kernel,
        grid=(ELIMINATED // WIDE,),
        out_shape=jax.ShapeDtypeStruct((n_front, copies, capacity, ELIMINATED), jnp.float32),
        in_specs=[
            pl.BlockSpec(memory_space=pltpu.SMEM),
            pl.BlockSpec((1, sources), lambda j: (0, 0)),
            pl.BlockSpec((sources, 1), lambda j: (0, 0)),
            pl.BlockSpec((sources, WIDE), lambda j: (0, skipped + j)),
        ],
        out_specs=pl.BlockSpec((n_front, copies, capacity, WIDE), lambda j: (0, 0, 0, j)),
        scratch_shapes=[pltpu.VMEM((n_front * capacity, sources), jnp.bfloat16)],
        compiler_params=pltpu.CompilerParams(vmem_limit_bytes=VMEM_BYTES),
        cost_estimate=LIGHT,
    )((first_col + start).reshape(1, 1), dest, stair, rows)


def stacked_halves(out_ref, *parts):
    count = out_ref.shape[0] // 2
    first = 0
    for x in parts:
        rows = x.shape[0]
        high, low = halves(x)
        out_ref[first : first + rows] = low
        out_ref[count + first : count + first + rows] = high
        first += rows


def turned_dot(turned, other):
    count = other.shape[0] // 2
    return jnp.dot(turned, other, preferred_element_type=jnp.float32) + jnp.dot(
        turned[:, :count], other[count:], preferred_element_type=jnp.float32
    )


def gram_kernel(turn_ref, own_ref, child_ref, *outs):
    turned_ref, both_ref, packed_ref = outs[5:]
    count = both_ref.shape[0] // 2
    stacked_halves(both_ref, own_ref[...], child_ref[:, 0].reshape(-1, ELIMINATED))
    for start in range(0, ELIMINATED, WIDE):
        cols = slice(start, start + WIDE)
        turned_ref[cols, :count] = both_ref[count:, cols].T
        turned_ref[cols, count:] = both_ref[:count, cols].T
    for block, pair, offset in offsets():
        start = WIDE * block
        total = turned_dot(turned_ref[start : start + WIDE, :], both_ref[:, start:])
        for half in range(2):
            packed_ref[2 * pair + half, :, offset : offset + ELIMINATED - start] = total[
                BLK * half : BLK * (half + 1)
            ]
    mine_ref, right_ref, left_ref, right_rest_ref, left_rest_ref, *_ = outs
    turn = turn_ref[0, 0]
    here, right, over, left = [lax.rem(turn + s, 4) for s in range(4)]
    middle = BLK // 2
    mine_ref[...] = packed_ref[here]
    right_ref[:middle], right_ref[middle:] = packed_ref[over, :middle], packed_ref[right, middle:]
    left_ref[:middle], left_ref[middle:] = packed_ref[over, middle:], packed_ref[left, :middle]
    right_rest_ref[...] = packed_ref[right, :middle]
    left_rest_ref[...] = packed_ref[left, middle:]


def packed_gram(turn, own_panel, arrived):
    fronts, _, capacity, _ = arrived.shape
    rows = own_panel.shape[0] + fronts * capacity
    vmem = pl.BlockSpec(memory_space=pltpu.VMEM)
    return pl.pallas_call(
        gram_kernel,
        grid=(1,),
        out_shape=[jax.ShapeDtypeStruct((BLK, PACKED), jnp.float32)] * 3
        + [jax.ShapeDtypeStruct((BLK // 2, PACKED), jnp.float32)] * 2
        + [jax.ShapeDtypeStruct((ELIMINATED, 2 * rows), jnp.bfloat16)],
        in_specs=[
            pl.BlockSpec(memory_space=pltpu.SMEM),
            vmem,
            pl.BlockSpec((fronts, 1, capacity, ELIMINATED), lambda j: (0, 0, 0, 0)),
        ],
        out_specs=[vmem] * 6,
        scratch_shapes=[pltpu.VMEM((2 * rows, ELIMINATED), jnp.bfloat16), pltpu.VMEM((4, BLK, PACKED), jnp.float32)],
        compiler_params=pltpu.CompilerParams(vmem_limit_bytes=VMEM_BYTES),
        cost_estimate=LIGHT,
    )(turn, own_panel, arrived)


def cross_kernel(turned_ref, own_ref, child_ref, out_ref, both_ref):
    stacked_halves(both_ref, own_ref[...], child_ref[:, 0].reshape(-1, WIDE))
    out_ref[0] = turned_dot(turned_ref[...], both_ref[...])


def cross(turned, own, start, child, part):
    fronts, _, capacity, _ = child.shape
    skipped = start // WIDE
    return pl.pallas_call(
        cross_kernel,
        grid=(ELIMINATED // WIDE,),
        out_shape=jax.ShapeDtypeStruct((ELIMINATED // WIDE, ELIMINATED, WIDE), jnp.float32),
        in_specs=[
            pl.BlockSpec(memory_space=pltpu.VMEM),
            pl.BlockSpec((own.shape[0], WIDE), lambda j: (0, skipped + j)),
            pl.BlockSpec((fronts, 1, capacity, WIDE), lambda j: (0, part, 0, j)),
        ],
        out_specs=pl.BlockSpec((1, ELIMINATED, WIDE), lambda j: (j, 0, 0)),
        scratch_shapes=[pltpu.VMEM((turned.shape[1], WIDE), jnp.bfloat16)],
        compiler_params=pltpu.CompilerParams(vmem_limit_bytes=VMEM_BYTES),
        cost_estimate=LIGHT,
    )(turned, own, child)


def shared_kernel(_, turned_ref, own_ref, child_ref, out_ref, both_ref):
    stacked_halves(both_ref, own_ref[...], child_ref[:, 0].reshape(-1, WIDE))
    total = turned_dot(turned_ref[...], both_ref[...])
    for half in range(2):
        out_ref[half] = total[:, BLK * half : BLK * (half + 1)]


def shared_cross(col, turned, own, child):
    fronts, _, capacity, _ = child.shape
    steps = own.shape[1] // WIDE
    return pl.pallas_call(
        shared_kernel,
        grid_spec=pltpu.PrefetchScalarGridSpec(
            num_scalar_prefetch=1,
            grid=(steps,),
            in_specs=[
                pl.BlockSpec(memory_space=pltpu.VMEM),
                pl.BlockSpec((own.shape[0], WIDE), lambda j, c: (0, j)),
                pl.BlockSpec((fronts, 1, capacity, WIDE), lambda j, c: (0, 1, 0, c[0] * steps + j)),
            ],
            out_specs=pl.BlockSpec((2, ELIMINATED, BLK), lambda j, c: (j, 0, 0)),
            scratch_shapes=[pltpu.VMEM((turned.shape[1], WIDE), jnp.bfloat16)],
        ),
        out_shape=jax.ShapeDtypeStruct((own.shape[1] // BLK, ELIMINATED, BLK), jnp.float32),
        compiler_params=pltpu.CompilerParams(vmem_limit_bytes=VMEM_BYTES),
        cost_estimate=LIGHT,
    )(col, turned, own, child)


def sharp_dot(a, b, dims):
    (high, low), (other_high, other_low) = a, b
    dims = (dims, ((), ()))
    total = lax.dot_general(high, other_high, dims, preferred_element_type=jnp.float32)
    total += lax.dot_general(high, other_low, dims, preferred_element_type=jnp.float32)
    return total + lax.dot_general(low, other_high, dims, preferred_element_type=jnp.float32)


PLAIN = ((1,), (0,))


def factor_kernel(
    turn_ref, piece_ref, before_ref, after_ref, across_ref, across_rest_ref, sums_ref,
    high_ref, low_ref, leading_ref, solved_ref,
    work_ref, diag_ref, packed_ref, panel_high_ref, panel_low_ref, found_ref,
):
    turn = turn_ref[0, 0]
    middle = BLK // 2
    packed_ref[turn] = piece_ref[...]
    packed_ref[lax.rem(turn + 1, 4)] = after_ref[...]
    packed_ref[lax.rem(turn + 3, 4)] = before_ref[...]
    packed_ref[lax.rem(turn + 2, 4), :middle] = across_ref[...]
    packed_ref[lax.rem(turn + 2, 4), middle:] = across_rest_ref[...]
    work_ref[...] = jnp.zeros_like(work_ref)
    panel_high_ref[...] = jnp.zeros_like(panel_high_ref)
    panel_low_ref[...] = jnp.zeros_like(panel_low_ref)
    for block, pair, offset in offsets():
        start = WIDE * block
        for half in range(2):
            work_ref[start + BLK * half : start + BLK * (half + 1), start:] = packed_ref[
                2 * pair + half, :, offset : offset + ELIMINATED - start
            ]
    row = lax.broadcasted_iota(jnp.int32, (BLK, BLK), 0)
    col = lax.broadcasted_iota(jnp.int32, (BLK, BLK), 1)
    place_of = lax.broadcasted_iota(jnp.int32, (BLK, ELIMINATED), 1) // BLK
    chunk_of = lax.broadcasted_iota(jnp.int32, (BLK, WIDE), 1) // BLK
    deferred = [(i, c) for i in range(2, STEPS) for c in range(ELIMINATED // WIDE)]

    sums = halves(sums_ref[0])

    def solve_rows(k):
        rows = pl.ds(pl.multiple_of(k * BLK, BLK), BLK)
        found_ref[rows, :] = sharp_dot((high_ref[rows, :], low_ref[rows, :]), sums, PLAIN)

    def step(k, _):
        here = pl.ds(pl.multiple_of(k * BLK, BLK), BLK)
        block = work_ref[here, here]
        turned = {}

        def update(i, c):
            below = i > k
            rows, cols = slice(BLK * i, BLK * (i + 1)), slice(WIDE * c, WIDE * (c + 1))
            if i not in turned:
                kept = jnp.where(below, 1.0, 0.0)
                turned[i] = [
                    (ref[:, rows].astype(jnp.float32) * kept).T.astype(jnp.bfloat16)
                    for ref in (panel_high_ref, panel_low_ref)
                ]
            panel = (panel_high_ref[:, cols], panel_low_ref[:, cols])
            cleared = jnp.where(below, k - 1 - c * (WIDE // BLK), -1)
            old = jnp.where(chunk_of == cleared, 0.0, work_ref[rows, cols])
            work_ref[rows, cols] = old - sharp_dot(turned[i], panel, PLAIN)

        def beside(b, count):
            for i, c in deferred[len(deferred) * b // count : len(deferred) * (b + 1) // count]:
                update(i, c)

        solve_rows(jnp.maximum(k - 1, 0))
        inverse = lower_inverse(block, beside)
        rows = sharp_dot(halves(inverse), halves(work_ref[here, :]), PLAIN)
        work_ref[here, :] = rows
        diag_ref[here, :] = jnp.where(row <= col, work_ref[here, here], 0.0)
        work_ref[here, here] = inverse
        rows = work_ref[here, :]
        panel_high_ref[...], panel_low_ref[...] = halves(rows)
        high_ref[here, :], low_ref[here, :] = halves(jnp.where(place_of <= k, rows, 0.0))

        @pl.when(k < STEPS - 1)
        def _():
            there = pl.ds(pl.multiple_of((k + 1) * BLK, BLK), BLK)
            left = [ref[:, there].astype(jnp.float32).T.astype(jnp.bfloat16) for ref in (panel_high_ref, panel_low_ref)]
            old = jnp.where(place_of == k, 0.0, work_ref[there, :])
            work_ref[there, :] = old - sharp_dot(left, (panel_high_ref[...], panel_low_ref[...]), PLAIN)

        return 0

    lax.fori_loop(0, STEPS, step, 0)
    taken = leading_ref.shape[0] // BLK
    for b in range(taken):
        block = turn * taken + b
        here = pl.ds(pl.multiple_of(block * BLK, BLK), BLK)
        diag = jnp.concatenate([diag_ref[here, :]] * STEPS, axis=1)
        leading_ref[BLK * b : BLK * (b + 1), :] = jnp.where(
            place_of > block, work_ref[here, :], jnp.where(place_of == block, diag, 0.0)
        )
    solve_rows(STEPS - 1)
    parts, copies, quarter, _ = solved_ref.shape
    for i in range(parts):
        for copy in range(copies):
            solved_ref[i, copy] = found_ref[quarter * i : quarter * (i + 1), :]


def factor(turn, piece, before, after, across, across_rest, sums):
    vmem = pl.BlockSpec(memory_space=pltpu.VMEM)
    return pl.pallas_call(
        factor_kernel,
        out_shape=(
            jax.ShapeDtypeStruct((ELIMINATED, ELIMINATED), jnp.bfloat16),
            jax.ShapeDtypeStruct((ELIMINATED, ELIMINATED), jnp.bfloat16),
            jax.ShapeDtypeStruct((ELIMINATED // 4, ELIMINATED), jnp.float32),
            jax.ShapeDtypeStruct((4, 2, ELIMINATED // 4, BLK), jnp.float32),
        ),
        in_specs=[pl.BlockSpec(memory_space=pltpu.SMEM)] + [vmem] * 6,
        out_specs=(vmem, vmem, vmem, vmem),
        scratch_shapes=[
            pltpu.VMEM((ELIMINATED, ELIMINATED), jnp.float32),
            pltpu.VMEM((ELIMINATED, BLK), jnp.float32),
            pltpu.VMEM((4, BLK, PACKED), jnp.float32),
            pltpu.VMEM((BLK, ELIMINATED), jnp.bfloat16),
            pltpu.VMEM((BLK, ELIMINATED), jnp.bfloat16),
            pltpu.VMEM((ELIMINATED, BLK), jnp.float32),
        ],
        compiler_params=pltpu.CompilerParams(vmem_limit_bytes=VMEM_BYTES),
        cost_estimate=LIGHT,
    )(turn, piece, before, after, across, across_rest, sums)


def solve_kernel(high_ref, low_ref, sums_ref, out_ref):
    parts, quarter, _ = out_ref.shape
    sums = halves(sums_ref[0])
    for i in range(parts):
        rows, depth = slice(quarter * i, quarter * (i + 1)), quarter * (i + 1)
        out_ref[i] = sharp_dot(
            (high_ref[rows, :depth], low_ref[rows, :depth]), tuple(x[:depth] for x in sums), PLAIN
        )


def solve(high, low, sums):
    vmem = pl.BlockSpec(memory_space=pltpu.VMEM)
    return pl.pallas_call(
        solve_kernel,
        out_shape=jax.ShapeDtypeStruct((4, ELIMINATED // 4, sums.shape[2]), jnp.float32),
        in_specs=[vmem] * 3,
        out_specs=vmem,
        compiler_params=pltpu.CompilerParams(vmem_limit_bytes=VMEM_BYTES),
        cost_estimate=LIGHT,
    )(high, low, sums)


def join_kernel(col_ref, leading_ref, first_ref, second_ref, out_ref):
    parts, _, width = second_ref.shape
    for j in range(parts):
        for half in range(2):
            start = ELIMINATED // 2 * half + BLK * j
            cols = slice(start, start + BLK)
            out_ref[0, :, cols] = jnp.where(
                col_ref[0, 0] == 0, leading_ref[:, cols], first_ref[j, half]
            )
    for j in range(parts):
        out_ref[0, :, ELIMINATED + width * j : ELIMINATED + width * (j + 1)] = second_ref[j]


def join(col, leading, first, second):
    vmem = pl.BlockSpec(memory_space=pltpu.VMEM)
    return pl.pallas_call(
        join_kernel,
        out_shape=jax.ShapeDtypeStruct((1, leading.shape[0], 2 * ELIMINATED), jnp.float32),
        in_specs=[pl.BlockSpec(memory_space=pltpu.SMEM)] + [vmem] * 3,
        out_specs=vmem,
        compiler_params=pltpu.CompilerParams(vmem_limit_bytes=VMEM_BYTES),
        cost_estimate=LIGHT,
    )(col, leading, first, second)


def shifted(x, shift, count):
    return lax.ppermute(x, "row", [(i, (i + shift) % count) for i in range(count)])


def body(own_rows, child_rows, child_dest, child_stair):
    n_front = lax.axis_size("front")
    row_count = lax.axis_size("row")
    source_rows, half_cols = child_rows.shape
    capacity = max(2, 2 * source_rows // n_front)
    col_index = lax.axis_index("col")
    row_index = lax.axis_index("row")
    quarter = ELIMINATED // row_count
    own = own_rows[0]
    own_a = own[:, :ELIMINATED]
    split = own_a.shape[0] // 4
    passed = lax.ppermute(own_a[:split], "col", [(0, 1), (1, 0)])
    passed_rest = lax.ppermute(own_a[split:], "col", [(0, 1), (1, 0)])

    first_col = col_index * half_cols
    dest, stair = child_dest.reshape(1, source_rows), child_stair.reshape(source_rows, 1)
    doubled = place(first_col, dest, stair, child_rows, 0, 2, n_front, capacity)
    single = place(first_col, dest, stair, child_rows, ELIMINATED, 1, n_front, capacity)
    doubled, passed = lax.optimization_barrier((doubled, passed))
    arrived = lax.all_to_all(
        doubled.reshape(2 * n_front * capacity, ELIMINATED),
        ("front", "col"),
        split_axis=0,
        concat_axis=0,
        tiled=True,
    ).reshape(n_front, 2, capacity, ELIMINATED)
    passed = jnp.concatenate([passed, passed_rest], axis=0)
    own_panel = jnp.where(col_index == 0, own_a, passed)
    own_shared = jnp.where(
        col_index == 0, passed[:, : ELIMINATED // 2], own_a[:, ELIMINATED // 2 :]
    )

    own_panel, single = lax.optimization_barrier((own_panel, single))
    child_b = lax.all_to_all(
        single.reshape(n_front * capacity, ELIMINATED), "front", split_axis=0, concat_axis=0, tiled=True
    ).reshape(n_front, 1, capacity, ELIMINATED)
    turn = row_index.reshape(1, 1)
    mine, right, left, right_rest, left_rest, turned = packed_gram(turn, own_panel, arrived)
    middle = BLK // 2
    from_left, from_right = shifted(right, 1, row_count), shifted(left, -1, row_count)
    from_left, from_right, turned_later = lax.optimization_barrier((from_left, from_right, turned))
    products_a = shared_cross(col_index.reshape(1), turned_later, own_shared, arrived)
    rest_left = shifted(right_rest + from_left[:middle], 1, row_count)
    rest_right = shifted(left_rest + from_right[:middle], -1, row_count)
    rest_left, rest_right = lax.optimization_barrier((rest_left, rest_right))
    piece = mine + jnp.concatenate(
        [rest_left + from_right[middle:], from_left[middle:] + rest_right], axis=0
    )
    piece, child_b = lax.optimization_barrier((piece, child_b))
    products_b = cross(turned, own, ELIMINATED, child_b, 0)
    before, after = shifted(piece, 1, row_count), shifted(piece, -1, row_count)
    before, after, products_b = lax.optimization_barrier((before, after, products_b))
    across, across_rest = shifted(before[:middle], 1, row_count), shifted(after[middle:], -1, row_count)
    pieces = (piece, before, after, across, across_rest)

    def summed(products):
        return lax.psum_scatter(products, "row", scatter_dimension=0, tiled=True)

    inverse_high, inverse_low, leading, first = factor(turn, *pieces, summed(products_a))
    first = lax.all_to_all(
        first.reshape(2 * row_count, quarter, BLK), ("row", "col"), split_axis=0, concat_axis=0, tiled=True
    ).reshape(row_count, 2, quarter, BLK)
    second = solve(inverse_high, inverse_low, summed(products_b))
    second = lax.all_to_all(second, "row", split_axis=0, concat_axis=0, tiled=True)
    return join(col_index.reshape(1, 1), leading, first, second)


def solution(mesh):
    placed = (
        P("front", "row", "col"),
        P(("front", "row"), "col"),
        P(("front", "row"), None),
        P(("front", "row")),
    )
    return jax.shard_map(
        body, mesh=mesh, in_specs=placed, out_specs=P("front", "row", "col"), check_vma=False
    )
```

```python
import jax
import jax.numpy as jnp
from jax import lax
from jax.experimental import pallas as pl
from jax.experimental.pallas import tpu as pltpu
from jax.sharding import PartitionSpec as P

ELIMINATED = 1024
STAIR_BLK = 128
BLK = 128
STEPS = ELIMINATED // BLK
LINES = 8
VMEM_BYTES = 60 * 2**20
LIGHT = pl.CostEstimate(flops=1, bytes_accessed=1, transcendentals=0)


def lower_inverse(diag_block, beside):
    lane = lax.broadcasted_iota(jnp.int32, (LINES, BLK), 1)
    sublane = lax.broadcasted_iota(jnp.int32, (LINES, BLK), 0)
    count = BLK // LINES
    strips = [diag_block[LINES * i : LINES * (i + 1), :] for i in range(count)]
    for b in range(count):
        first = LINES * b
        within = (lane >= first) & (lane < first + LINES)
        strip = strips[b]
        column = [
            jnp.broadcast_to(strip[:, first + t : first + t + 1], (LINES, BLK))
            for t in range(LINES)
        ]
        entry = [
            [jnp.broadcast_to(column[t][i : i + 1, :], (LINES, BLK)) for t in range(i + 1)]
            for i in range(LINES)
        ]
        scale = []
        for t in range(LINES):
            scale.append(lax.rsqrt(entry[t][t]))
            for i in range(t + 1, LINES):
                entry[i][t] = entry[i][t] * scale[t]
            for u in range(t + 1, LINES):
                for i in range(u, LINES):
                    entry[i][u] = entry[i][u] - entry[i][t] * entry[u][t]
        solved = []
        augmented = jnp.where(within, jnp.where(lane == sublane + first, 1.0, 0.0), strip)
        for t in range(LINES):
            line = jnp.broadcast_to(augmented[t : t + 1, :], (LINES, BLK))
            for s in range(t):
                line = line - entry[t][s] * solved[s]
            solved.append(line * scale[t])
        merged = solved[0]
        for t in range(1, LINES):
            merged = jnp.where(sublane == t, solved[t], merged)
        strips[b] = merged
        beside(b, count)
        for i in range(b + 1, count):
            below = strips[i]
            rest = jnp.where(within, 0.0, below)
            factors = []
            for t in range(LINES):
                value = jnp.broadcast_to(below[:, first + t : first + t + 1], (LINES, BLK))
                for s in range(t):
                    value = value - entry[t][s] * factors[s]
                value = value * scale[t]
                factors.append(value)
                rest = rest - value * solved[t]
            strips[i] = rest
    row = lax.broadcasted_iota(jnp.int32, (BLK, BLK), 0)
    col = lax.broadcasted_iota(jnp.int32, (BLK, BLK), 1)
    return jnp.where(row >= col, jnp.concatenate(strips, axis=0), 0.0)


PAIRS = ((0, 3), (1, 2))
WIDE = 256
PACKED = ELIMINATED + WIDE


def offsets():
    found = []
    for pair, (long, short) in enumerate(PAIRS):
        found.append((long, pair, 0))
        found.append((short, pair, ELIMINATED - WIDE * long))
    return found


def halves(x):
    high = x.astype(jnp.bfloat16)
    return high, (x - high.astype(jnp.float32)).astype(jnp.bfloat16)


def place_kernel(first_ref, dest_ref, stair_ref, rows_ref, out_ref, select_ref):
    fronts, copies, capacity, width = out_ref.shape
    slots, sources = select_ref.shape
    chunk = pl.program_id(0)

    @pl.when(chunk == 0)
    def _():
        dest = dest_ref[...]
        named = lax.broadcasted_iota(jnp.int32, (fronts, sources), 0) == dest
        source = lax.broadcasted_iota(jnp.int32, (sources, sources), 0)
        later = lax.broadcasted_iota(jnp.int32, (sources, sources), 1)
        before = jnp.dot(
            named.astype(jnp.float32).astype(jnp.bfloat16),
            (source < later).astype(jnp.float32).astype(jnp.bfloat16),
            preferred_element_type=jnp.float32,
        )
        slot = jnp.sum(jnp.where(named, before, 0.0), axis=0, keepdims=True).astype(jnp.int32)
        position = dest * capacity + slot
        line = lax.broadcasted_iota(jnp.int32, (slots, sources), 0)
        select_ref[...] = (line == position).astype(jnp.float32).astype(jnp.bfloat16)

    cols = (
        first_ref[0, 0] + chunk * width + lax.broadcasted_iota(jnp.int32, (sources, width), 1)
    )
    high, low = halves(jnp.where(cols >= stair_ref[...] * STAIR_BLK, rows_ref[...], 0.0))
    select = select_ref[...]
    placed = jnp.dot(select, high, preferred_element_type=jnp.float32) + jnp.dot(
        select, low, preferred_element_type=jnp.float32
    )
    placed = placed.reshape(fronts, capacity, width)
    for copy in range(copies):
        out_ref[:, copy] = placed


def place(first_col, dest, stair, rows, start, copies, n_front, capacity):
    sources = rows.shape[0]
    skipped = start // WIDE
    return pl.pallas_call(
        place_kernel,
        grid=(ELIMINATED // WIDE,),
        out_shape=jax.ShapeDtypeStruct((n_front, copies, capacity, ELIMINATED), jnp.float32),
        in_specs=[
            pl.BlockSpec(memory_space=pltpu.SMEM),
            pl.BlockSpec((1, sources), lambda j: (0, 0)),
            pl.BlockSpec((sources, 1), lambda j: (0, 0)),
            pl.BlockSpec((sources, WIDE), lambda j: (0, skipped + j)),
        ],
        out_specs=pl.BlockSpec((n_front, copies, capacity, WIDE), lambda j: (0, 0, 0, j)),
        scratch_shapes=[pltpu.VMEM((n_front * capacity, sources), jnp.bfloat16)],
        compiler_params=pltpu.CompilerParams(vmem_limit_bytes=VMEM_BYTES),
        cost_estimate=LIGHT,
    )((first_col + start).reshape(1, 1), dest, stair, rows)


def stacked_halves(out_ref, *parts):
    count = out_ref.shape[0] // 2
    first = 0
    for x in parts:
        rows = x.shape[0]
        high, low = halves(x)
        out_ref[first : first + rows] = low
        out_ref[count + first : count + first + rows] = high
        first += rows


def turned_dot(turned, other):
    count = other.shape[0] // 2
    return jnp.dot(turned, other, preferred_element_type=jnp.float32) + jnp.dot(
        turned[:, :count], other[count:], preferred_element_type=jnp.float32
    )


def gram_kernel(turn_ref, own_ref, child_ref, *outs):
    turned_ref, both_ref, packed_ref = outs[5:]
    count = both_ref.shape[0] // 2
    stacked_halves(both_ref, own_ref[...], child_ref[:, 0].reshape(-1, ELIMINATED))
    for start in range(0, ELIMINATED, WIDE):
        cols = slice(start, start + WIDE)
        turned_ref[cols, :count] = both_ref[count:, cols].T
        turned_ref[cols, count:] = both_ref[:count, cols].T
    for block, pair, offset in offsets():
        start = WIDE * block
        total = turned_dot(turned_ref[start : start + WIDE, :], both_ref[:, start:])
        for half in range(2):
            packed_ref[2 * pair + half, :, offset : offset + ELIMINATED - start] = total[
                BLK * half : BLK * (half + 1)
            ]
    mine_ref, right_ref, left_ref, right_rest_ref, left_rest_ref, *_ = outs
    turn = turn_ref[0, 0]
    here, right, over, left = [lax.rem(turn + s, 4) for s in range(4)]
    middle = BLK // 2
    mine_ref[...] = packed_ref[here]
    right_ref[:middle], right_ref[middle:] = packed_ref[over, :middle], packed_ref[right, middle:]
    left_ref[:middle], left_ref[middle:] = packed_ref[over, middle:], packed_ref[left, :middle]
    right_rest_ref[...] = packed_ref[right, :middle]
    left_rest_ref[...] = packed_ref[left, middle:]


def packed_gram(turn, own_panel, arrived):
    fronts, _, capacity, _ = arrived.shape
    rows = own_panel.shape[0] + fronts * capacity
    vmem = pl.BlockSpec(memory_space=pltpu.VMEM)
    return pl.pallas_call(
        gram_kernel,
        grid=(1,),
        out_shape=[jax.ShapeDtypeStruct((BLK, PACKED), jnp.float32)] * 3
        + [jax.ShapeDtypeStruct((BLK // 2, PACKED), jnp.float32)] * 2
        + [jax.ShapeDtypeStruct((ELIMINATED, 2 * rows), jnp.bfloat16)],
        in_specs=[
            pl.BlockSpec(memory_space=pltpu.SMEM),
            vmem,
            pl.BlockSpec((fronts, 1, capacity, ELIMINATED), lambda j: (0, 0, 0, 0)),
        ],
        out_specs=[vmem] * 6,
        scratch_shapes=[pltpu.VMEM((2 * rows, ELIMINATED), jnp.bfloat16), pltpu.VMEM((4, BLK, PACKED), jnp.float32)],
        compiler_params=pltpu.CompilerParams(vmem_limit_bytes=VMEM_BYTES),
        cost_estimate=LIGHT,
    )(turn, own_panel, arrived)


def cross_kernel(turned_ref, own_ref, child_ref, out_ref, both_ref):
    stacked_halves(both_ref, own_ref[...], child_ref[:, 0].reshape(-1, WIDE))
    out_ref[0] = turned_dot(turned_ref[...], both_ref[...])


def cross(turned, own, start, child, part):
    fronts, _, capacity, _ = child.shape
    skipped = start // WIDE
    return pl.pallas_call(
        cross_kernel,
        grid=(ELIMINATED // WIDE,),
        out_shape=jax.ShapeDtypeStruct((ELIMINATED // WIDE, ELIMINATED, WIDE), jnp.float32),
        in_specs=[
            pl.BlockSpec(memory_space=pltpu.VMEM),
            pl.BlockSpec((own.shape[0], WIDE), lambda j: (0, skipped + j)),
            pl.BlockSpec((fronts, 1, capacity, WIDE), lambda j: (0, part, 0, j)),
        ],
        out_specs=pl.BlockSpec((1, ELIMINATED, WIDE), lambda j: (j, 0, 0)),
        scratch_shapes=[pltpu.VMEM((turned.shape[1], WIDE), jnp.bfloat16)],
        compiler_params=pltpu.CompilerParams(vmem_limit_bytes=VMEM_BYTES),
        cost_estimate=LIGHT,
    )(turned, own, child)


def shared_kernel(_, turned_ref, own_ref, child_ref, out_ref, both_ref):
    stacked_halves(both_ref, own_ref[...], child_ref[:, 0].reshape(-1, WIDE))
    total = turned_dot(turned_ref[...], both_ref[...])
    for half in range(2):
        out_ref[half] = total[:, BLK * half : BLK * (half + 1)]


def shared_cross(col, turned, own, child):
    fronts, _, capacity, _ = child.shape
    steps = own.shape[1] // WIDE
    return pl.pallas_call(
        shared_kernel,
        grid_spec=pltpu.PrefetchScalarGridSpec(
            num_scalar_prefetch=1,
            grid=(steps,),
            in_specs=[
                pl.BlockSpec(memory_space=pltpu.VMEM),
                pl.BlockSpec((own.shape[0], WIDE), lambda j, c: (0, j)),
                pl.BlockSpec((fronts, 1, capacity, WIDE), lambda j, c: (0, 1, 0, c[0] * steps + j)),
            ],
            out_specs=pl.BlockSpec((2, ELIMINATED, BLK), lambda j, c: (j, 0, 0)),
            scratch_shapes=[pltpu.VMEM((turned.shape[1], WIDE), jnp.bfloat16)],
        ),
        out_shape=jax.ShapeDtypeStruct((own.shape[1] // BLK, ELIMINATED, BLK), jnp.float32),
        compiler_params=pltpu.CompilerParams(vmem_limit_bytes=VMEM_BYTES),
        cost_estimate=LIGHT,
    )(col, turned, own, child)


def sharp_dot(a, b, dims):
    (high, low), (other_high, other_low) = a, b
    dims = (dims, ((), ()))
    total = lax.dot_general(high, other_high, dims, preferred_element_type=jnp.float32)
    total += lax.dot_general(high, other_low, dims, preferred_element_type=jnp.float32)
    return total + lax.dot_general(low, other_high, dims, preferred_element_type=jnp.float32)


PLAIN = ((1,), (0,))


def factor_kernel(
    turn_ref, piece_ref, before_ref, after_ref, across_ref, across_rest_ref, sums_ref,
    high_ref, low_ref, leading_ref, solved_ref,
    work_ref, diag_ref, packed_ref, panel_high_ref, panel_low_ref, found_ref,
):
    turn = turn_ref[0, 0]
    middle = BLK // 2
    packed_ref[turn] = piece_ref[...]
    packed_ref[lax.rem(turn + 1, 4)] = after_ref[...]
    packed_ref[lax.rem(turn + 3, 4)] = before_ref[...]
    packed_ref[lax.rem(turn + 2, 4), :middle] = across_ref[...]
    packed_ref[lax.rem(turn + 2, 4), middle:] = across_rest_ref[...]
    work_ref[...] = jnp.zeros_like(work_ref)
    panel_high_ref[...] = jnp.zeros_like(panel_high_ref)
    panel_low_ref[...] = jnp.zeros_like(panel_low_ref)
    for block, pair, offset in offsets():
        start = WIDE * block
        for half in range(2):
            work_ref[start + BLK * half : start + BLK * (half + 1), start:] = packed_ref[
                2 * pair + half, :, offset : offset + ELIMINATED - start
            ]
    row = lax.broadcasted_iota(jnp.int32, (BLK, BLK), 0)
    col = lax.broadcasted_iota(jnp.int32, (BLK, BLK), 1)
    place_of = lax.broadcasted_iota(jnp.int32, (BLK, ELIMINATED), 1) // BLK
    chunk_of = lax.broadcasted_iota(jnp.int32, (BLK, WIDE), 1) // BLK
    deferred = [(i, c) for i in range(2, STEPS) for c in range(ELIMINATED // WIDE)]

    sums = halves(sums_ref[0])

    def solve_rows(k):
        rows = pl.ds(pl.multiple_of(k * BLK, BLK), BLK)
        found_ref[rows, :] = sharp_dot((high_ref[rows, :], low_ref[rows, :]), sums, PLAIN)

    def step(k, _):
        here = pl.ds(pl.multiple_of(k * BLK, BLK), BLK)
        block = work_ref[here, here]
        turned = {}

        def update(i, c):
            below = i > k
            rows, cols = slice(BLK * i, BLK * (i + 1)), slice(WIDE * c, WIDE * (c + 1))
            if i not in turned:
                kept = jnp.where(below, 1.0, 0.0)
                turned[i] = [
                    (ref[:, rows].astype(jnp.float32) * kept).T.astype(jnp.bfloat16)
                    for ref in (panel_high_ref, panel_low_ref)
                ]
            panel = (panel_high_ref[:, cols], panel_low_ref[:, cols])
            cleared = jnp.where(below, k - 1 - c * (WIDE // BLK), -1)
            old = jnp.where(chunk_of == cleared, 0.0, work_ref[rows, cols])
            work_ref[rows, cols] = old - sharp_dot(turned[i], panel, PLAIN)

        def beside(b, count):
            for i, c in deferred[len(deferred) * b // count : len(deferred) * (b + 1) // count]:
                update(i, c)

        solve_rows(jnp.maximum(k - 1, 0))
        inverse = lower_inverse(block, beside)
        rows = sharp_dot(halves(inverse), halves(work_ref[here, :]), PLAIN)
        work_ref[here, :] = rows
        diag_ref[here, :] = jnp.where(row <= col, work_ref[here, here], 0.0)
        work_ref[here, here] = inverse
        rows = work_ref[here, :]
        panel_high_ref[...], panel_low_ref[...] = halves(rows)
        high_ref[here, :], low_ref[here, :] = halves(jnp.where(place_of <= k, rows, 0.0))

        @pl.when(k < STEPS - 1)
        def _():
            there = pl.ds(pl.multiple_of((k + 1) * BLK, BLK), BLK)
            left = [ref[:, there].astype(jnp.float32).T.astype(jnp.bfloat16) for ref in (panel_high_ref, panel_low_ref)]
            old = jnp.where(place_of == k, 0.0, work_ref[there, :])
            work_ref[there, :] = old - sharp_dot(left, (panel_high_ref[...], panel_low_ref[...]), PLAIN)

        return 0

    lax.fori_loop(0, STEPS, step, 0)
    taken = leading_ref.shape[0] // BLK
    for b in range(taken):
        block = turn * taken + b
        here = pl.ds(pl.multiple_of(block * BLK, BLK), BLK)
        diag = jnp.concatenate([diag_ref[here, :]] * STEPS, axis=1)
        leading_ref[BLK * b : BLK * (b + 1), :] = jnp.where(
            place_of > block, work_ref[here, :], jnp.where(place_of == block, diag, 0.0)
        )
    solve_rows(STEPS - 1)
    parts, copies, quarter, _ = solved_ref.shape
    for i in range(parts):
        for copy in range(copies):
            solved_ref[i, copy] = found_ref[quarter * i : quarter * (i + 1), :]


def factor(turn, piece, before, after, across, across_rest, sums):
    vmem = pl.BlockSpec(memory_space=pltpu.VMEM)
    return pl.pallas_call(
        factor_kernel,
        out_shape=(
            jax.ShapeDtypeStruct((ELIMINATED, ELIMINATED), jnp.bfloat16),
            jax.ShapeDtypeStruct((ELIMINATED, ELIMINATED), jnp.bfloat16),
            jax.ShapeDtypeStruct((ELIMINATED // 4, ELIMINATED), jnp.float32),
            jax.ShapeDtypeStruct((4, 2, ELIMINATED // 4, BLK), jnp.float32),
        ),
        in_specs=[pl.BlockSpec(memory_space=pltpu.SMEM)] + [vmem] * 6,
        out_specs=(vmem, vmem, vmem, vmem),
        scratch_shapes=[
            pltpu.VMEM((ELIMINATED, ELIMINATED), jnp.float32),
            pltpu.VMEM((ELIMINATED, BLK), jnp.float32),
            pltpu.VMEM((4, BLK, PACKED), jnp.float32),
            pltpu.VMEM((BLK, ELIMINATED), jnp.bfloat16),
            pltpu.VMEM((BLK, ELIMINATED), jnp.bfloat16),
            pltpu.VMEM((ELIMINATED, BLK), jnp.float32),
        ],
        compiler_params=pltpu.CompilerParams(vmem_limit_bytes=VMEM_BYTES),
        cost_estimate=LIGHT,
    )(turn, piece, before, after, across, across_rest, sums)


def solve_kernel(high_ref, low_ref, sums_ref, out_ref):
    parts, quarter, _ = out_ref.shape
    sums = halves(sums_ref[0])
    for i in range(parts):
        rows, depth = slice(quarter * i, quarter * (i + 1)), quarter * (i + 1)
        out_ref[i] = sharp_dot(
            (high_ref[rows, :depth], low_ref[rows, :depth]), tuple(x[:depth] for x in sums), PLAIN
        )


def solve(high, low, sums):
    vmem = pl.BlockSpec(memory_space=pltpu.VMEM)
    return pl.pallas_call(
        solve_kernel,
        out_shape=jax.ShapeDtypeStruct((4, ELIMINATED // 4, sums.shape[2]), jnp.float32),
        in_specs=[vmem] * 3,
        out_specs=vmem,
        compiler_params=pltpu.CompilerParams(vmem_limit_bytes=VMEM_BYTES),
        cost_estimate=LIGHT,
    )(high, low, sums)


def join_kernel(col_ref, leading_ref, first_ref, second_ref, out_ref):
    parts, _, width = second_ref.shape
    for j in range(parts):
        for half in range(2):
            start = ELIMINATED // 2 * half + BLK * j
            cols = slice(start, start + BLK)
            out_ref[0, :, cols] = jnp.where(
                col_ref[0, 0] == 0, leading_ref[:, cols], first_ref[j, half]
            )
    for j in range(parts):
        out_ref[0, :, ELIMINATED + width * j : ELIMINATED + width * (j + 1)] = second_ref[j]


def join(col, leading, first, second):
    vmem = pl.BlockSpec(memory_space=pltpu.VMEM)
    return pl.pallas_call(
        join_kernel,
        out_shape=jax.ShapeDtypeStruct((1, leading.shape[0], 2 * ELIMINATED), jnp.float32),
        in_specs=[pl.BlockSpec(memory_space=pltpu.SMEM)] + [vmem] * 3,
        out_specs=vmem,
        compiler_params=pltpu.CompilerParams(vmem_limit_bytes=VMEM_BYTES),
        cost_estimate=LIGHT,
    )(col, leading, first, second)


def shifted(x, shift, count):
    return lax.ppermute(x, "row", [(i, (i + shift) % count) for i in range(count)])


def body(own_rows, child_rows, child_dest, child_stair):
    n_front = lax.axis_size("front")
    row_count = lax.axis_size("row")
    source_rows, half_cols = child_rows.shape
    capacity = max(2, 2 * source_rows // n_front)
    col_index = lax.axis_index("col")
    row_index = lax.axis_index("row")
    quarter = ELIMINATED // row_count
    own = own_rows[0]
    own_a = own[:, :ELIMINATED]
    split = own_a.shape[0] // 4
    passed = lax.ppermute(own_a[:split], "col", [(0, 1), (1, 0)])
    passed_rest = lax.ppermute(own_a[split:], "col", [(0, 1), (1, 0)])

    first_col = col_index * half_cols
    dest, stair = child_dest.reshape(1, source_rows), child_stair.reshape(source_rows, 1)
    doubled = place(first_col, dest, stair, child_rows, 0, 2, n_front, capacity)
    single = place(first_col, dest, stair, child_rows, ELIMINATED, 1, n_front, capacity)
    doubled, passed = lax.optimization_barrier((doubled, passed))
    arrived = lax.all_to_all(
        doubled.reshape(2 * n_front * capacity, ELIMINATED),
        ("front", "col"),
        split_axis=0,
        concat_axis=0,
        tiled=True,
    ).reshape(n_front, 2, capacity, ELIMINATED)
    passed = jnp.concatenate([passed, passed_rest], axis=0)
    own_panel = jnp.where(col_index == 0, own_a, passed)
    own_shared = jnp.where(
        col_index == 0, passed[:, : ELIMINATED // 2], own_a[:, ELIMINATED // 2 :]
    )

    own_panel, single = lax.optimization_barrier((own_panel, single))
    child_b = lax.all_to_all(
        single.reshape(n_front * capacity, ELIMINATED), "front", split_axis=0, concat_axis=0, tiled=True
    ).reshape(n_front, 1, capacity, ELIMINATED)
    turn = row_index.reshape(1, 1)
    mine, right, left, right_rest, left_rest, turned = packed_gram(turn, own_panel, arrived)
    middle = BLK // 2
    from_left, from_right = shifted(right, 1, row_count), shifted(left, -1, row_count)
    from_left, from_right, turned_later = lax.optimization_barrier((from_left, from_right, turned))
    products_a = shared_cross(col_index.reshape(1), turned_later, own_shared, arrived)
    rest_left = shifted(right_rest + from_left[:middle], 1, row_count)
    rest_right = shifted(left_rest + from_right[:middle], -1, row_count)
    rest_left, rest_right = lax.optimization_barrier((rest_left, rest_right))
    piece = mine + jnp.concatenate(
        [rest_left + from_right[middle:], from_left[middle:] + rest_right], axis=0
    )
    piece, child_b = lax.optimization_barrier((piece, child_b))
    products_b = cross(turned, own, ELIMINATED, child_b, 0)
    before, after = shifted(piece, 1, row_count), shifted(piece, -1, row_count)
    before, after, products_b = lax.optimization_barrier((before, after, products_b))
    across, across_rest = shifted(before[:middle], 1, row_count), shifted(after[middle:], -1, row_count)
    pieces = (piece, before, after, across, across_rest)

    def summed(products):
        return lax.psum_scatter(products, "row", scatter_dimension=0, tiled=True)

    pieces, products_b = lax.optimization_barrier((pieces, products_b))
    inverse_high, inverse_low, leading, first = factor(turn, *pieces, summed(products_a))
    first = lax.all_to_all(
        first.reshape(2 * row_count, quarter, BLK), ("row", "col"), split_axis=0, concat_axis=0, tiled=True
    ).reshape(row_count, 2, quarter, BLK)
    second = solve(inverse_high, inverse_low, summed(products_b))
    second = lax.all_to_all(second, "row", split_axis=0, concat_axis=0, tiled=True)
    return join(col_index.reshape(1, 1), leading, first, second)


def solution(mesh):
    placed = (
        P("front", "row", "col"),
        P(("front", "row"), "col"),
        P(("front", "row"), None),
        P(("front", "row")),
    )
    return jax.shard_map(
        body, mesh=mesh, in_specs=placed, out_specs=P("front", "row", "col"), check_vma=False
    )
```
